32 devices in a mesh: seq: 8 (over z, x), batch: 4 (over y, core).
Axes of the slice: x: 2, y: 2, z: 4, core: 2. Of those that a mesh axis runs over, the one named last changes fastest.
Arguments:
- inputs: float32 [8, 2048, 256], P('batch', 'seq'), may hold values from -6 to 6
- guess_path: float32 [8, 2048, 128], P('batch', 'seq'), may hold values from -3 to 3
- recur_weight: float32 [128, 128], replicated, may hold values from -0.09 to 0.09
- damping: float32 [128], replicated, may hold values from 0.001953125 to 2.5
- in_weight: float32 [256, 128], replicated, may hold values from -0.375 to 0.375
- bias_term: float32 [128], replicated, may hold values from -3 to 3
- targets: float32 [8, 16, 128], P('batch', 'seq'), may hold values from -6 to 6
- target_steps: int32 [8, 16], P('batch', 'seq'), may hold values from 0 to 127
Outputs:
- trajectory: float32 [8, 2048, 128], P('batch', 'seq')
- grad_recur: float32 [128, 128], replicated
- grad_in: float32 [256, 128], replicated
The draws below stay inside these ranges and needn't reach their ends.
All inputs are finite; a program needn't handle non-finite values.
Results may differ from the reference program's by a relative error of at most 0.0003.
Values sent between devices are 32-bit elements; how exact they have to be, the bound alone decides.
No kernel may reach another device: no remote copies, remote signals or barrier semaphores. Data moves between devices by JAX's collectives and lax.ppermute only.
A program may use at most 64 MiB of HBM per device.

```python
import math
import jax
import jax.numpy as jnp
from jax import lax

H = 128
DIN = 256
TBLK = 128
SEQS = 8
SEQLEN = 2048
NTB = 16


def plant(drawn, own_key, least, high):
    spot = [jax.random.randint(jax.random.fold_in(own_key, axis), (), 0, length) for axis, length in enumerate(drawn.shape)]
    longest = drawn.shape.index(max(drawn.shape))
    next_to = spot[:longest] + [(spot[longest] + 1) % drawn.shape[longest]] + spot[longest + 1:]
    return drawn.at[tuple(spot)].set(least).at[tuple(next_to)].set(high)


def block_levels(stream_key, shape, split, smallest, high):
    loudness = 1.0
    for dim, shards_of in split:
        draws = jax.random.uniform(jax.random.fold_in(jax.random.fold_in(stream_key, 6), dim), (shards_of,), jnp.float32, smallest / len(split), high / len(split))
        loudness = loudness * jnp.repeat(jnp.exp(draws), shape[dim] // shards_of).reshape((-1,) + (1,) * (len(shape) - 1 - dim))
    return loudness


def noise(key, extent, scale, bound, shards=(), kind=jnp.bfloat16):
    factor_of = block_levels(key, extent, shards, -0.22, 0.18) if shards else 1.0
    result = jax.random.normal(key, extent, jnp.float32) * scale * factor_of
    return jnp.minimum(jnp.maximum(result, -bound), bound).astype(kind)


def setup_inputs(seed: int = 0) -> dict:
    key_of = jax.random.split(jax.random.key(seed), 9)
    inputs = noise(key_of[0], (SEQS, SEQLEN, DIN), 1.0, 6.0, ((0, 4), (1, 8)), jnp.float32)
    guess_path = noise(key_of[1], (SEQS, SEQLEN, H), 0.5, 3.0, ((0, 4), (1, 8)), jnp.float32)
    recur_weight = noise(key_of[2], (H, H), 0.015, 0.09, (), jnp.float32)
    damping = jnp.clip(jnp.exp(jax.random.uniform(key_of[3], (H,), jnp.float32, math.log(0.001953125), math.log(2.5))), 0.001953125, 2.5)
    in_weight = noise(key_of[4], (DIN, H), DIN ** -0.5, 0.375, (), jnp.float32)
    bias_term = noise(key_of[5], (H,), 0.5, 3.0, (), jnp.float32)
    targets = noise(key_of[6], (SEQS, NTB, H), 1.0, 6.0, ((0, 4), (1, 8)), jnp.float32)
    target_steps = plant(jax.random.randint(key_of[7], (SEQS, NTB), 0, TBLK), jax.random.fold_in(key_of[7], 1), 0, TBLK - 1).astype(jnp.int32)
    return {"inputs": inputs, "guess_path": guess_path, "recur_weight": recur_weight, "damping": damping, "in_weight": in_weight, "bias_term": bias_term, "targets": targets, "target_steps": target_steps}


euler_step = 0.02


def reference(inputs, guess_path, recur_weight, damping, in_weight, bias_term, targets, target_steps):
    highest = lax.Precision.HIGHEST
    skew = recur_weight - recur_weight.T
    seq_count, step_count, hidden = guess_path.shape
    prev = jnp.concatenate([jnp.zeros((seq_count, 1, hidden), jnp.float32), guess_path[:, :-1, :]], axis=1)
    drive = jnp.einsum('stc,ch->sth', inputs, in_weight, precision=highest)
    preact = jnp.einsum('stk,hk->sth', prev, skew, precision=highest) - damping * prev + drive + bias_term
    activation = jnp.tanh(preact)
    gain = euler_step * (1.0 - activation * activation)
    resid = prev + euler_step * activation - guess_path
    gain_steps = gain.transpose(1, 0, 2)

    def forward(state, inputs_now):
        gain_now, resid_now = inputs_now
        moved = jnp.dot(state, skew.T, precision=highest) - damping * state
        state = state + gain_now * moved + resid_now
        return state, state

    zero_state = jnp.zeros((seq_count, hidden), jnp.float32)
    _, deltas = lax.scan(forward, zero_state, (gain_steps, resid.transpose(1, 0, 2)))
    trajectory = guess_path + deltas.transpose(1, 0, 2)

    block_count = step_count // TBLK
    target_hit = (jnp.arange(TBLK)[None, None, :] == target_steps[:, :, None]).astype(jnp.float32)
    miss = trajectory.reshape(seq_count, block_count, TBLK, hidden) - targets[:, :, None, :]
    source = (target_hit[..., None] * miss / seq_count).reshape(seq_count, step_count, hidden)

    def backward(carry, inputs_now):
        gain_now, source_now = inputs_now
        adjoint = source_now + carry
        scaled = gain_now * adjoint
        carry = adjoint + jnp.dot(scaled, skew, precision=highest) - damping * scaled
        return carry, adjoint

    _, adjoints = lax.scan(backward, zero_state, (gain_steps, source.transpose(1, 0, 2)), reverse=True)
    grad_pre = gain * adjoints.transpose(1, 0, 2)
    recur_sum = jnp.einsum('sti,stj->ij', grad_pre, prev, precision=highest)
    grad_in = jnp.einsum('stc,sth->ch', inputs, grad_pre, precision=highest)
    return trajectory, recur_sum - recur_sum.T, grad_in
```

```python
import functools

import jax
import jax.numpy as jnp
from jax import lax
from jax.experimental import pallas as pl
from jax.experimental.pallas import tpu as pltpu
from jax.sharding import PartitionSpec as P

LANE = 16
MIB = 1 << 20
F32 = jnp.float32
BF16 = jnp.bfloat16
SMEM = pl.BlockSpec(memory_space=pltpu.SMEM)
VMEM = pl.BlockSpec(memory_space=pltpu.VMEM)

euler_step = 0.02


def split(value):
    high = value.astype(BF16)
    return high, (value - high.astype(F32)).astype(BF16)


def left(value):
    return jnp.concatenate(split(value), axis=1)


def right(weight):
    row = jnp.concatenate(split(weight), axis=1)
    return jnp.concatenate([row, row], axis=0)


def right_t(weight):
    high, low = split(weight)
    return jnp.concatenate(
        [jnp.concatenate([high, high], axis=1), jnp.concatenate([low, low], axis=1)], axis=0
    )


def halves(wide):
    hidden = wide.shape[1] // 2
    return wide[:, :hidden] + wide[:, hidden:]


def mul(x, packed):
    return halves(jnp.dot(left(x), packed, preferred_element_type=F32))


def mul_t(x, packed):
    return halves(
        lax.dot_general(left(x), packed, (((1,), (1,)), ((), ())), preferred_element_type=F32)
    )


def mm(x, weight):
    return mul(x, right(weight))


def mm_t(x, weight):
    return mul_t(x, right_t(weight))


def eight(row):
    return jnp.broadcast_to(row, (8, row.shape[1]))


def identity(hidden):
    rows = lax.broadcasted_iota(jnp.int32, (hidden, hidden), 0)
    return (rows == lax.broadcasted_iota(jnp.int32, (hidden, hidden), 1)).astype(F32)


def drift_t(recur_ref, damping_ref):
    weight = recur_ref[...]
    return weight.T - weight - identity(weight.shape[0]) * damping_ref[...]


def compose_kernel(
    seqs, blocks, total_seqs, steps_ref, x_ref, guess_ref, edge_ref, recur_ref, damping_ref,
    in_ref, bias_ref, targets_ref,
    message_ref, maps_ref, before_ref, start_ref, hit_ref, reach_ref, reach_off_ref, gain_ref,
    resid_ref, prev_ref,
    off_ref, hit_off_ref,
):
    rows, hidden = guess_ref.shape
    count = rows // seqs
    chunks = count // LANE
    lanes = seqs * chunks
    block = count // blocks
    drift = drift_t(recur_ref, damping_ref)
    drift_w = right(drift)

    guess = guess_ref[...]
    prev_ref[pl.ds(1, rows - 1), :] = guess_ref[pl.ds(0, rows - 1), :]
    for s in range(seqs):
        prev_ref[pl.ds(s * count, 1), :] = edge_ref[pl.ds(s, 1), :]
    prev = prev_ref[...]
    x_high, x_low = split(x_ref[...])
    in_w = jnp.concatenate(split(in_ref[...]), axis=1)
    drive = halves(
        jnp.dot(x_high, in_w, preferred_element_type=F32)
        + jnp.dot(x_low, in_w, preferred_element_type=F32)
    )
    activation = jnp.tanh(mul(prev, drift_w) + drive + bias_ref[...])
    gain_ref[...] = euler_step * (1.0 - activation * activation)
    resid_ref[...] = prev + euler_step * activation - guess

    unit = identity(hidden)
    for lane in range(lanes):
        maps_ref[lane] = unit + drift * gain_ref[pl.ds(lane * LANE, 1), :]
    off_ref[...] = resid_ref[pl.ds(0, lanes, stride=LANE), :]

    def place(j):
        step = (j % blocks) * block + steps_ref[j // blocks, j % blocks]
        return (j // blocks) * chunks + step // LANE, step % LANE, (j // blocks) * count + step

    def capture(now):
        for j in range(seqs * blocks):
            lane, at, _ = place(j)

            @pl.when(at == now)
            def _():
                hit_ref[j] = maps_ref[lane]
                hit_off_ref[pl.ds(j, 1), :] = off_ref[pl.ds(lane, 1), :]

    capture(0)

    def advance(now, _):
        for lane in range(0, lanes, 2):
            pair = maps_ref[lane : lane + 2].reshape(2 * hidden, hidden)
            moved = mul(pair, drift_w)
            for k in range(2):
                gain_now = gain_ref[pl.ds((lane + k) * LANE + now, 1), :]
                part = slice(k * hidden, (k + 1) * hidden)
                maps_ref[lane + k] = pair[part] + gain_now * moved[part]
        off = off_ref[...]
        off_ref[...] = (
            off
            + gain_ref[pl.ds(now, lanes, stride=LANE), :] * mul(off, drift_w)
            + resid_ref[pl.ds(now, lanes, stride=LANE), :]
        )
        capture(now)
        return 0

    lax.fori_loop(1, LANE, advance, 0)

    running = [unit] * seqs
    offset = [jnp.zeros((8, hidden), F32)] * seqs
    for chunk in range(chunks):
        for s in range(seqs):
            lane = s * chunks + chunk
            before_ref[lane] = running[s]
            start_ref[pl.ds(lane, 1), :] = offset[s][:1]
            this, this_off = maps_ref[lane], off_ref[pl.ds(lane, 1), :]
            if chunk == 0:
                running[s], offset[s] = this, eight(this_off)
            else:
                packed = right(this)
                running[s] = mul(running[s], packed)
                offset[s] = mul(offset[s], packed) + this_off

    for s in range(seqs):
        message_ref[s, pl.ds(0, hidden), :] = running[s]
        total = jnp.zeros((hidden, hidden), F32)
        total_off = jnp.zeros((8, hidden), F32)
        for k in range(blocks):
            j = s * blocks + k
            lane, _, row = place(j)
            packed = right(hit_ref[j])
            reach = mul(before_ref[lane], packed)
            reach_off = mul(eight(start_ref[pl.ds(lane, 1), :]), packed) + hit_off_ref[pl.ds(j, 1), :]
            reach_ref[j] = reach
            miss = reach_off + guess_ref[pl.ds(row, 1), :] - targets_ref[pl.ds(j, 1), :]
            reach_off_ref[pl.ds(j, 1), :] = miss[:1]
            reach_t = right_t(reach)
            total = total + mul_t(reach, reach_t)
            total_off = total_off + mul_t(miss, reach_t)
        message_ref[s, pl.ds(hidden, hidden), :] = total / total_seqs
        message_ref[s, pl.ds(2 * hidden, 8), :] = jnp.concatenate(
            [offset[s][:1], total_off[:1] / total_seqs, jnp.zeros((6, hidden), F32)], axis=0
        )


def join(first, second, hidden, with_map):
    map_1, curve_1, off_1, adj_1 = first
    map_2, curve_2, off_2, adj_2 = second
    curve_w = right(curve_2)
    map_1_t = right_t(map_1)
    curve = curve_1 + mul_t(mul(map_1, curve_w), map_1_t)
    adj = adj_1 + mul_t(mul(off_1, curve_w) + adj_2, map_1_t)
    map_w = right(map_2)
    off = mul(off_1, map_w) + off_2
    return (mul(map_1, map_w) if with_map else None), curve, off, adj


def opened(ref, s, hidden):
    return (
        ref[s, pl.ds(0, hidden), :],
        ref[s, pl.ds(hidden, hidden), :],
        eight(ref[s, pl.ds(2 * hidden, 1), :]),
        eight(ref[s, pl.ds(2 * hidden + 1, 1), :]),
    )


def pick(flag, one, other):
    return tuple(jnp.where(flag, a, b) for a, b in zip(one, other))


def vector_rows(off, adj):
    return jnp.concatenate([off[:1], adj[:1], jnp.zeros((6, off.shape[1]), F32)], axis=0)


def join_kernel(level, with_map, place_ref, mine_ref, other_ref, out_ref):
    seqs, hidden = mine_ref.shape[0], mine_ref.shape[2]
    upper = (place_ref[0] >> level) & 1 == 1
    for s in range(seqs):
        mine, other = opened(mine_ref, s, hidden), opened(other_ref, s, hidden)
        result = join(pick(upper, other, mine), pick(upper, mine, other), hidden, with_map)
        at = 0
        if with_map:
            out_ref[s, pl.ds(0, hidden), :] = result[0]
            at = hidden
        out_ref[s, pl.ds(at, hidden), :] = result[1]
        out_ref[s, pl.ds(at + hidden, 8), :] = vector_rows(result[2], result[3])


def sides_kernel(levels, place_ref, *refs):
    received, (before_ref, after_ref) = refs[:levels], refs[levels:]
    seqs, hidden = before_ref.shape[0], before_ref.shape[2]
    for s in range(seqs):
        zero = jnp.zeros((8, hidden), F32)
        unit = identity(hidden)
        blank = jnp.zeros((hidden, hidden), F32)
        before = (unit, zero)
        after = (unit, blank, zero, zero)
        for level in range(levels):
            upper = (place_ref[0] >> level) & 1 == 1
            other = opened(received[level], s, hidden)
            if level == 0:
                longer, extended = (other[0], other[2]), other
            else:
                packed = right(before[0])
                longer = (mul(other[0], packed), mul(other[2], packed) + before[1])
                extended = join(after, other, hidden, True)
            before = pick(upper, longer, before)
            after = pick(upper, after, extended)
        before_ref[s, pl.ds(0, hidden), :] = before[0]
        before_ref[s, pl.ds(hidden, 8), :] = vector_rows(before[1], zero)
        after_ref[s, pl.ds(0, hidden), :] = after[0]
        after_ref[s, pl.ds(hidden, hidden), :] = after[1]
        after_ref[s, pl.ds(2 * hidden, 8), :] = vector_rows(after[2], after[3])


def solve_kernel(
    seqs, blocks, total_seqs, level, place_ref, steps_ref, message_ref, mine_ref, other_ref,
    sides_before_ref, sides_after_ref, maps_ref, before_ref, start_ref, hit_ref, reach_ref,
    reach_off_ref, gain_ref, resid_ref, prev_ref, guess_ref, x_ref, recur_ref, damping_ref,
    path_ref, grads_ref,
    state_ref, carry_ref, source_ref, pre_ref,
):
    rows, hidden = guess_ref.shape
    count = rows // seqs
    chunks = count // LANE
    lanes = seqs * chunks
    block = count // blocks
    upper = (place_ref[0] >> level) & 1 == 1
    drift = drift_t(recur_ref, damping_ref)
    drift_w = right(drift)
    drift_wt = right_t(drift)
    source_ref[...] = jnp.zeros_like(source_ref)

    entry, tail, pulls = [], [], []
    for s in range(seqs):
        mine_off = eight(mine_ref[s, pl.ds(hidden, 1), :])
        other_off = eight(other_ref[s, pl.ds(hidden, 1), :])
        lead, lead_off = sides_before_ref[s, pl.ds(0, hidden), :], eight(sides_before_ref[s, pl.ds(hidden, 1), :])
        state = jnp.where(upper, mm(other_off, lead) + lead_off, lead_off)
        entry.append(state)
        beyond = mm(mine_off, other_ref[s, pl.ds(0, hidden), :]) + other_ref[s, pl.ds(hidden + 1, 1), :]
        beyond = jnp.where(upper, jnp.zeros_like(beyond), beyond)
        dev_map, _, dev_off, _ = opened(message_ref, s, hidden)
        leaving = mm(state, dev_map) + dev_off
        after_map, after_curve, _, after_adj = opened(sides_after_ref, s, hidden)
        tail.append(mm(leaving, after_curve) + after_adj + mm_t(beyond, after_map))

    for s in range(seqs):
        for k in range(blocks):
            j = s * blocks + k
            step = k * block + steps_ref[s, k]
            miss = (mm(entry[s], reach_ref[j]) + reach_off_ref[pl.ds(j, 1), :]) / total_seqs
            source_ref[pl.ds(s * count + step, 1), :] = miss[:1]
            pulls.append((s, step // LANE, mm_t(miss, hit_ref[j])))
        for chunk in range(chunks):
            lane = s * chunks + chunk
            if chunk == 0:
                state_ref[pl.ds(lane, 1), :] = entry[s][:1]
            else:
                state_ref[pl.ds(lane, 1), :] = (
                    mm(entry[s], before_ref[lane])[:1] + start_ref[pl.ds(lane, 1), :]
                )
    state = state_ref[...]
    for now in range(LANE):
        at = pl.ds(now, lanes, stride=LANE)
        state = state + gain_ref[at, :] * mul(state, drift_w) + resid_ref[at, :]
        path_ref[at, :] = guess_ref[at, :] + state

    for chunk in reversed(range(chunks)):
        for s in range(seqs):
            lane = s * chunks + chunk
            carry_ref[pl.ds(lane, 1), :] = tail[s][:1]
            if chunk:
                carry = mm_t(tail[s], maps_ref[lane])
                for owner, at, pull in pulls:
                    if owner == s:
                        carry = carry + jnp.where(at == chunk, pull, jnp.zeros_like(pull))
                tail[s] = carry
    carry = carry_ref[...]
    for now in reversed(range(LANE)):
        at = pl.ds(now, lanes, stride=LANE)
        adjoint = source_ref[at, :] + carry
        scaled = gain_ref[at, :] * adjoint
        pre_ref[at, :] = scaled
        if now:
            carry = adjoint + mul_t(scaled, drift_wt)

    pre_high, pre_low = split(pre_ref[...])

    def gathered(value):
        high, low = split(value)
        flat = (((0,), (0,)), ((), ()))
        return (
            lax.dot_general(high, pre_high, flat, preferred_element_type=F32)
            + lax.dot_general(high, pre_low, flat, preferred_element_type=F32)
            + lax.dot_general(low, pre_high, flat, preferred_element_type=F32)
        )

    recur = gathered(prev_ref[...])
    recur = recur.T - recur
    half = hidden // 2
    row = lax.broadcasted_iota(jnp.int32, (half, half), 0)
    col = lax.broadcasted_iota(jnp.int32, (half, half), 1)
    folded = jnp.where(col > row, recur[:half, :half], recur[half:, half:])
    grads_ref[pl.ds(0, half), :] = jnp.concatenate([folded, recur[:half, half:]], axis=1)
    grads_ref[pl.ds(half, x_ref.shape[1]), :] = gathered(x_ref[...])


def unfold_kernel(place_ref, mine_ref, other_ref, recur_ref, in_ref):
    hidden = recur_ref.shape[0]
    half = hidden // 2
    odd = place_ref[1] & 1 == 1
    mine, other = mine_ref[...], other_ref[...]
    whole = jnp.concatenate([jnp.where(odd, other, mine), jnp.where(odd, mine, other)], axis=0)
    in_ref[...] = whole[half:]
    row = lax.broadcasted_iota(jnp.int32, (half, half), 0)
    col = lax.broadcasted_iota(jnp.int32, (half, half), 1)
    folded, corner = whole[:half, :half], whole[:half, half:]
    first = jnp.where(col > row, folded, 0.0)
    last = jnp.where(col < row, folded, 0.0)
    recur_ref[pl.ds(0, half), :] = jnp.concatenate([first - first.T, corner], axis=1)
    recur_ref[pl.ds(half, half), :] = jnp.concatenate([-corner.T, last - last.T], axis=1)


def call(kernel, shapes, specs, scratch=(), flops=0, room=24):
    return pl.pallas_call(
        kernel,
        out_shape=[jax.ShapeDtypeStruct(shape, F32) for shape in shapes],
        in_specs=specs,
        out_specs=[VMEM] * len(shapes),
        scratch_shapes=[pltpu.VMEM(shape, F32) for shape in scratch],
        compiler_params=pltpu.CompilerParams(vmem_limit_bytes=room * MIB),
        cost_estimate=pl.CostEstimate(flops=flops, bytes_accessed=1 << 20, transcendentals=0),
    )


def swapped(value, axis, distance):
    return lax.ppermute(value, axis, [(i, i ^ distance) for i in range(lax.axis_size(axis))])


def levels_of(axis):
    return lax.axis_size(axis).bit_length() - 1


def on_device(
    inputs, guess_path, recur_weight, damping, in_weight, bias_term, targets, target_steps
):
    seqs, count, hidden = guess_path.shape
    blocks = targets.shape[1]
    features = inputs.shape[2]
    rows = seqs * count
    lanes = rows // LANE
    hits = seqs * blocks
    total_seqs = seqs * lax.axis_size("batch")
    place = jnp.stack([lax.axis_index("seq"), lax.axis_index("batch")]).astype(jnp.int32)
    route = [(i, i + 1) for i in range(lax.axis_size("seq") - 1)]
    edge = lax.ppermute(guess_path[:, count - 1, :], "seq", route)
    x = inputs.reshape(rows, features)
    guess = guess_path.reshape(rows, hidden)
    damping = damping.reshape(1, hidden)

    message, maps, before, start, hit, reach, reach_off, gain, resid, prev = call(
        functools.partial(compose_kernel, seqs, blocks, total_seqs),
        [
            (seqs, 2 * hidden + 8, hidden),
            (lanes, hidden, hidden),
            (lanes, hidden, hidden),
            (lanes, hidden),
            (hits, hidden, hidden),
            (hits, hidden, hidden),
            (hits, hidden),
            (rows, hidden),
            (rows, hidden),
            (rows, hidden),
        ],
        [SMEM] + [VMEM] * 8,
        [(lanes, hidden), (hits, hidden)],
    )(target_steps, x, guess, edge, recur_weight, damping, in_weight, bias_term.reshape(1, hidden),
      targets.reshape(hits, hidden))

    levels = levels_of("seq")
    group, received = message, []
    for level in range(levels - 1):
        other = swapped(group, "seq", 1 << level)
        received.append(other)
        with_map = level < levels - 2
        height = (2 if with_map else 1) * hidden + 8
        (group,) = call(
            functools.partial(join_kernel, level, with_map),
            [(seqs, height, hidden)],
            [SMEM, VMEM, VMEM],
        )(place, group, other)
    other = swapped(group, "seq", 1 << (levels - 1))
    sides_before, sides_after = call(
        functools.partial(sides_kernel, levels - 1),
        [(seqs, hidden + 8, hidden), (seqs, 2 * hidden + 8, hidden)],
        [SMEM] + [VMEM] * (levels - 1),
        flops=1 << 30,
    )(place, *received)

    path, grads = call(
        functools.partial(solve_kernel, seqs, blocks, total_seqs, levels - 1),
        [(rows, hidden), (hidden // 2 + features, hidden)],
        [SMEM, SMEM] + [VMEM] * 18,
        [(lanes, hidden), (lanes, hidden), (rows, hidden), (rows, hidden)],
    )(place, target_steps, message, group, other, sides_before, sides_after, maps, before, start,
      hit, reach, reach_off, gain, resid, prev, guess, x, recur_weight, damping)

    middle = grads.shape[0] // 2
    odd = place[1] & 1 == 1
    kept = jnp.where(odd, grads[middle:], grads[:middle])
    given = jnp.where(odd, grads[:middle], grads[middle:])
    kept = kept + swapped(given, "batch", 1)
    for level in range(1, levels_of("batch")):
        kept = kept + swapped(kept, "batch", 1 << level)
    for level in range(levels):
        kept = kept + swapped(kept, "seq", 1 << level)
    grad_recur, grad_in = call(
        unfold_kernel,
        [(hidden, hidden), (features, hidden)],
        [SMEM, VMEM, VMEM],
    )(place, kept, swapped(kept, "batch", 1))
    return (path.reshape(seqs, count, hidden), grad_recur, grad_in)


def solution(mesh):
    placed = (
        P("batch", "seq", None),
        P("batch", "seq", None),
        P(),
        P(),
        P(),
        P(),
        P("batch", "seq", None),
        P("batch", "seq"),
    )
    return jax.shard_map(
        on_device,
        mesh=mesh,
        in_specs=placed,
        out_specs=(P("batch", "seq", None), P(), P()),
        check_vma=False,
    )
```

```python
import functools

import jax
import jax.numpy as jnp
from jax import lax
from jax.experimental import pallas as pl
from jax.experimental.pallas import tpu as pltpu
from jax.sharding import PartitionSpec as P

LANE = 16
MIB = 1 << 20
UNROLL = 3
KEEP = 36 * MIB
F32 = jnp.float32
BF16 = jnp.bfloat16
SMEM = pl.BlockSpec(memory_space=pltpu.SMEM)
VMEM = pl.BlockSpec(memory_space=pltpu.VMEM)
ANY = pl.BlockSpec(memory_space=pl.ANY)

euler_step = 0.02


def split(value):
    high = value.astype(BF16)
    return high, (value - high.astype(F32)).astype(BF16)


def left(value):
    return jnp.concatenate(split(value), axis=1)


def right(weight):
    row = jnp.concatenate(split(weight), axis=1)
    return jnp.concatenate([row, row], axis=0)


def right_t(weight):
    high, low = split(weight)
    return jnp.concatenate(
        [jnp.concatenate([high, high], axis=1), jnp.concatenate([low, low], axis=1)], axis=0
    )


def halves(wide):
    hidden = wide.shape[1] // 2
    return wide[:, :hidden] + wide[:, hidden:]


def mul(x, packed):
    return halves(jnp.dot(left(x), packed, preferred_element_type=F32))


def mul_t(x, packed):
    return halves(
        lax.dot_general(left(x), packed, (((1,), (1,)), ((), ())), preferred_element_type=F32)
    )


def mm(x, weight):
    return mul(x, right(weight))


def mm_t(x, weight):
    return mul_t(x, right_t(weight))


def eight(row):
    return jnp.broadcast_to(row, (8, row.shape[1]))


def identity(hidden):
    rows = lax.broadcasted_iota(jnp.int32, (hidden, hidden), 0)
    return (rows == lax.broadcasted_iota(jnp.int32, (hidden, hidden), 1)).astype(F32)


def drift_t(recur_ref, damping_ref):
    weight = recur_ref[...]
    return weight.T - weight - identity(weight.shape[0]) * damping_ref[...]


def column(row, unit):
    return jnp.broadcast_to(jnp.sum(unit * row, axis=1, keepdims=True), unit.shape)


def along(col, weight):
    return jnp.sum(col * weight, axis=0, keepdims=True)


OFFSET, ADJOINT, DRIVE, FIRST, LAST = range(5)


def vectors(*rows):
    hidden = rows[0].shape[1]
    blank = jnp.zeros((8 - len(rows), hidden), F32)
    return jnp.concatenate([row[:1] for row in rows] + [blank], axis=0)


def compose_kernel(
    seqs, blocks, total_seqs, keep, place_ref, steps_ref, x_ref, guess_ref, recur_ref, damping_ref,
    in_ref, bias_ref, targets_ref,
    message_ref, maps_out, before_out, start_ref, hit_ref, reach_ref, reach_off_ref, gain_ref,
    resid_ref, drift_ref,
    partial_ref, before_ref, off_ref, hit_off_ref, prev_ref, maps_sem, before_sem,
):
    rows, hidden = guess_ref.shape
    count = rows // seqs
    chunks = count // LANE
    lanes = seqs * chunks
    block = count // blocks
    drift = drift_t(recur_ref, damping_ref)
    drift_ref[...] = drift
    drift_w = right(drift)

    guess = guess_ref[...]
    prev_ref[pl.ds(1, rows - 1), :] = guess_ref[pl.ds(0, rows - 1), :]
    for s in range(seqs):
        prev_ref[pl.ds(s * count, 1), :] = jnp.zeros((1, hidden), F32)
    prev = prev_ref[...]
    x_high, x_low = split(x_ref[...])
    in_w = jnp.concatenate(split(in_ref[...]), axis=1)
    drive = bias_ref[...] + halves(
        jnp.dot(x_high, in_w, preferred_element_type=F32)
        + jnp.dot(x_low, in_w, preferred_element_type=F32)
    )
    activation = jnp.tanh(mul(prev, drift_w) + drive)
    gain_ref[...] = euler_step * (1.0 - activation * activation)
    resid_ref[...] = prev + euler_step * activation - guess
    own = (place_ref[0] == 0).astype(F32)
    for s in range(seqs):
        edge = pl.ds(s * count, 1)
        gain_ref[edge, :] = gain_ref[edge, :] * own
        resid_ref[edge, :] = resid_ref[edge, :] * own

    unit = identity(hidden)
    for lane in range(lanes):
        partial_ref[0, lane] = unit + drift * gain_ref[pl.ds(lane * LANE, 1), :]
    off_ref[0] = resid_ref[pl.ds(0, lanes, stride=LANE), :]

    def place(j):
        step = (j % blocks) * block + steps_ref[j // blocks, j % blocks]
        return (j // blocks) * chunks + step // LANE, step % LANE, (j // blocks) * count + step

    def slot(now):
        return now if keep else 0

    def capture(now):
        for j in range(seqs * blocks):
            lane, at, _ = place(j)

            @pl.when(at == now)
            def _():
                hit_ref[j] = partial_ref[0, lane]
                hit_off_ref[pl.ds(j, 1), :] = off_ref[0, pl.ds(lane, 1), :]

    def advance(now, _):
        off = off_ref[slot(now - 1)]
        off_ref[slot(now)] = (
            off
            + gain_ref[pl.ds(now, lanes, stride=LANE), :] * mul(off, drift_w)
            + resid_ref[pl.ds(now, lanes, stride=LANE), :]
        )
        for lane in range(0, lanes, 2):
            pair = partial_ref[slot(now - 1), lane : lane + 2].reshape(2 * hidden, hidden)
            moved = mul(pair, drift_w)
            for k in range(2):
                gain_now = gain_ref[pl.ds((lane + k) * LANE + now, 1), :]
                part = slice(k * hidden, (k + 1) * hidden)
                partial_ref[slot(now), lane + k] = pair[part] + gain_now * moved[part]
        if not keep:
            capture(now)
        return 0

    if keep:
        lax.fori_loop(1, LANE, advance, 0, unroll=UNROLL)
        for j in range(seqs * blocks):
            lane, at, _ = place(j)
            hit_ref[j] = partial_ref[at, lane]
            hit_off_ref[pl.ds(j, 1), :] = off_ref[at, pl.ds(lane, 1), :]
    else:
        capture(0)
        lax.fori_loop(1, LANE, advance, 0)
    last = slot(LANE - 1)
    maps_copy = pltpu.make_async_copy(partial_ref.at[last], maps_out, maps_sem)
    maps_copy.start()

    running = [unit] * seqs
    offset = [jnp.zeros((8, hidden), F32)] * seqs
    for chunk in range(chunks):
        for s in range(seqs):
            lane = s * chunks + chunk
            before_ref[lane] = running[s]
            start_ref[pl.ds(lane, 1), :] = offset[s][:1]
            this, this_off = partial_ref[last, lane], off_ref[last, pl.ds(lane, 1), :]
            if chunk == 0:
                running[s], offset[s] = this, eight(this_off)
            else:
                packed = right(this)
                running[s] = mul(running[s], packed)
                offset[s] = mul(offset[s], packed) + this_off
    before_copy = pltpu.make_async_copy(before_ref, before_out, before_sem)
    before_copy.start()

    for s in range(seqs):
        message_ref[s, pl.ds(0, hidden), :] = running[s]
        total = jnp.zeros((hidden, hidden), F32)
        total_off = jnp.zeros((8, hidden), F32)
        for k in range(blocks):
            j = s * blocks + k
            lane, _, row = place(j)
            packed = right(hit_ref[j])
            reach = mul(before_ref[lane], packed)
            reach_off = mul(eight(start_ref[pl.ds(lane, 1), :]), packed) + hit_off_ref[pl.ds(j, 1), :]
            reach_ref[j] = reach
            miss = reach_off + guess_ref[pl.ds(row, 1), :] - targets_ref[pl.ds(j, 1), :]
            reach_off_ref[pl.ds(j, 1), :] = miss[:1]
            reach_t = right_t(reach)
            total = total + mul_t(reach, reach_t)
            total_off = total_off + mul_t(miss, reach_t)
        message_ref[s, pl.ds(hidden, hidden), :] = total / total_seqs
        message_ref[s, pl.ds(2 * hidden, 8), :] = vectors(
            offset[s], total_off / total_seqs, drive[s * count : s * count + 1],
            guess_ref[pl.ds(s * count, 1), :], guess_ref[pl.ds((s + 1) * count - 1, 1), :],
        )
    maps_copy.wait()
    before_copy.wait()


def opened(ref, s, with_map=True):
    hidden = ref.shape[2]
    at = hidden if with_map else 0
    rows = [eight(ref[s, pl.ds(at + hidden + k, 1), :]) for k in range(5)]
    return (ref[s, pl.ds(0, hidden), :] if with_map else None, ref[s, pl.ds(at, hidden), :], rows)


def pick(flag, one, other):
    return jax.tree.map(lambda a, b: jnp.where(flag, a, b), one, other)


def crossing(last, drive, first, drift_w):
    activation = jnp.tanh(mul(last, drift_w) + drive)
    return euler_step * (1.0 - activation * activation), last + euler_step * activation - first


def join(one, two, drift_w, with_map=True):
    map_1, curve_1, rows_1 = one
    map_2, curve_2, rows_2 = two
    gain, resid = crossing(rows_1[LAST], rows_2[DRIVE], rows_2[FIRST], drift_w)
    map_1 = map_1 + mul(map_1, drift_w) * gain[:1]
    off_1 = rows_1[OFFSET] + mul(rows_1[OFFSET], drift_w) * gain + resid
    curve_w, map_w, map_1_t = right(curve_2), right(map_2), right_t(map_1)
    curve = curve_1 + mul_t(mul(map_1, curve_w), map_1_t)
    adjoint = rows_1[ADJOINT] + mul_t(mul(off_1, curve_w) + rows_2[ADJOINT], map_1_t)
    rows = [mul(off_1, map_w) + rows_2[OFFSET], adjoint, rows_1[DRIVE], rows_1[FIRST], rows_2[LAST]]
    return (mul(map_1, map_w) if with_map else None), curve, rows


def join_kernel(level, with_map, place_ref, drift_ref, mine_ref, other_ref, out_ref):
    seqs, hidden = mine_ref.shape[0], mine_ref.shape[2]
    upper = (place_ref[0] >> level) & 1 == 1
    drift_w = right(drift_ref[...])
    for s in range(seqs):
        mine, other = opened(mine_ref, s), opened(other_ref, s)
        whole, curve, rows = join(pick(upper, other, mine), pick(upper, mine, other), drift_w, with_map)
        at = 0
        if with_map:
            out_ref[s, pl.ds(0, hidden), :] = whole
            at = hidden
        out_ref[s, pl.ds(at, hidden), :] = curve
        out_ref[s, pl.ds(at + hidden, 8), :] = vectors(*rows)


def sides_kernel(levels, place_ref, drift_ref, *refs):
    mines, others = refs[:levels], refs[levels : 2 * levels]
    entry_ref, tail_ref, back_ref, rows_ref = refs[2 * levels :]
    seqs, hidden = entry_ref.shape[0], entry_ref.shape[1]
    drift_w = right(drift_ref[...])
    unit = identity(hidden)
    for s in range(seqs):
        zero = jnp.zeros((8, hidden), F32)
        lead, lead_off = unit, zero
        after = (unit, jnp.zeros((hidden, hidden), F32), [zero] * 5)
        edge, edge_gain = zero, zero
        fresh = place_ref[0] >= 0
        for level in range(levels):
            upper = (place_ref[0] >> level) & 1 == 1
            mine, other = opened(mines[level], s), opened(others[level], s)
            gain, resid = crossing(other[2][LAST], mine[2][DRIVE], mine[2][FIRST], drift_w)
            far = other[0] + mul(other[0], drift_w) * gain[:1]
            far_off = other[2][OFFSET] + mul(other[2][OFFSET], drift_w) * gain + resid
            lead_w = right(lead)
            longer = (mul(far, lead_w), mul(far_off, lead_w) + lead_off)
            known = jnp.logical_and(upper, fresh)
            edge, edge_gain = pick(known, (other[2][LAST], gain), (edge, edge_gain))
            fresh = jnp.logical_and(fresh, jnp.logical_not(upper))
            after[2][LAST] = mine[2][LAST]
            extended = join(after, other, drift_w)
            lead, lead_off = pick(upper, longer, (lead, lead_off))
            after = pick(upper, after, extended)
        own_map, _, own_rows = opened(mines[0], s)
        own_w, curve_w = right(own_map), right(after[1])
        entry_ref[s] = lead
        tail_ref[s] = mul(mul(lead, own_w), curve_w)
        back_ref[s] = after[0].T
        leaving = mul(lead_off, own_w) + own_rows[OFFSET]
        tail_off = mul(leaving, curve_w) + after[2][ADJOINT]
        rows_ref[pl.ds(8 * s, 8), :] = vectors(lead_off, tail_off, edge, edge_gain)


def prepare_kernel(
    seqs, blocks, steps_ref, maps_ref, hit_ref, x_ref, guess_ref,
    home_ref, pull_ref, high_ref, low_ref,
    prev_ref,
):
    rows, hidden = guess_ref.shape
    count = rows // seqs
    chunks = count // LANE
    per_block = chunks // blocks
    unit = identity(hidden)
    blank = jnp.zeros((hidden, hidden), F32)
    prev_ref[pl.ds(1, rows - 1), :] = guess_ref[pl.ds(0, rows - 1), :]
    for s in range(seqs):
        prev_ref[pl.ds(s * count, 1), :] = jnp.zeros((1, hidden), F32)
    high_ref[pl.ds(0, hidden), :], low_ref[pl.ds(0, hidden), :] = split(prev_ref[...].T)
    high_ref[pl.ds(hidden, x_ref.shape[1]), :], low_ref[pl.ds(hidden, x_ref.shape[1]), :] = split(
        x_ref[...].T
    )
    home = [unit] * seqs
    pulls = [[blank] * blocks for _ in range(seqs)]
    for chunk in reversed(range(chunks)):
        for s in range(seqs):
            lane = s * chunks + chunk
            home_ref[lane] = home[s]
            active = [k for k in range(blocks) if chunk < (k + 1) * per_block]
            for k in active:
                pull_ref[s * blocks + k, chunk] = pulls[s][k]
            if chunk:
                stack = jnp.concatenate([home[s]] + [pulls[s][k] for k in active], axis=0)
                stack = mul_t(stack, right_t(maps_ref[lane]))
                home[s] = stack[:hidden]
                for i, k in enumerate(active):
                    owner = (k * (count // blocks) + steps_ref[s, k]) // LANE
                    part = stack[(i + 1) * hidden : (i + 2) * hidden]
                    pulls[s][k] = jnp.where(owner == chunk, hit_ref[s * blocks + k].T, part)


def solve_kernel(
    seqs, blocks, total_seqs, level, place_ref, steps_ref, drift_ref, mine_ref, other_ref,
    entry_ref, tail_ref, back_ref, sides_ref, before_ref, start_ref, home_ref, pull_ref, reach_ref,
    reach_off_ref, gain_ref, resid_ref, guess_ref, high_ref, low_ref,
    path_ref, grads_ref,
    state_ref, carry_ref, source_ref, pre_ref, gain_back_ref,
):
    rows, hidden = guess_ref.shape
    count = rows // seqs
    chunks = count // LANE
    lanes = seqs * chunks
    block = count // blocks
    per_block = chunks // blocks
    upper = (place_ref[0] >> level) & 1 == 1
    lowest = (place_ref[0] & ((1 << level) - 1)) == 0
    drift = drift_ref[...]
    drift_w = right(drift)
    drift_wt = right_t(drift)
    unit = identity(hidden)
    source_ref[...] = jnp.zeros_like(source_ref)
    gain_back_ref[...] = gain_ref[...]

    entries, tails, sources, edges = [], [], [], []
    for s in range(seqs):
        mine, other = opened(mine_ref, s, False), opened(other_ref, s, False)
        last, middle = pick(upper, (other[2][LAST], other[2][OFFSET]), (mine[2][LAST], mine[2][OFFSET]))
        drive, first = pick(upper, (mine[2][DRIVE], mine[2][FIRST]), (other[2][DRIVE], other[2][FIRST]))
        gain, resid = crossing(last, drive, first, drift_w)
        middle = middle + mul(middle, drift_w) * gain + resid
        middle_col = column(middle[:1], unit)
        row = along(middle_col, jnp.where(upper, entry_ref[s], other[1]))
        lead_off, tail_off, edge, edge_gain = [sides_ref[pl.ds(8 * s + k, 1), :] for k in range(4)]
        beyond = eight(row) + other[2][ADJOINT]
        beyond = beyond + mul_t(beyond * gain, drift_wt)
        entries.append(column(jnp.where(upper, row, 0.0) + lead_off, unit))
        tail = jnp.where(
            upper, along(middle_col, tail_ref[s]), along(column(beyond[:1], unit), back_ref[s])
        )
        tails.append(column(tail + tail_off, unit))
        known = jnp.logical_and(upper, lowest)
        edge = jnp.where(known, last[:1], edge)
        edges.append(edge)
        edge_gain = jnp.where(known, gain[:1], edge_gain)
        at = pl.ds(s * count, 1)
        gain_back_ref[at, :] = gain_ref[at, :] + edge_gain
        here = []
        for k in range(blocks):
            j = s * blocks + k
            miss = (along(entries[s], reach_ref[j]) + reach_off_ref[pl.ds(j, 1), :]) / total_seqs
            source_ref[pl.ds(s * count + k * block + steps_ref[s, k], 1), :] = miss
            here.append(column(miss, unit))
        sources.append(here)

    for part in range(blocks):

        def ends(chunk, _):
            for s in range(seqs):
                lane = s * chunks + chunk
                state_ref[pl.ds(lane, 1), :] = along(entries[s], before_ref[lane]) + start_ref[pl.ds(lane, 1), :]
                sums = tails[s] * home_ref[lane]
                for k in range(part, blocks):
                    sums = sums + sources[s][k] * pull_ref[s * blocks + k, chunk]
                carry_ref[pl.ds(lane, 1), :] = jnp.sum(sums, axis=0, keepdims=True)
            return 0

        lax.fori_loop(part * per_block, (part + 1) * per_block, ends, 0, unroll=2)

    def walk(now, both):
        state, carry = both
        at = pl.ds(now, lanes, stride=LANE)
        back = pl.ds(LANE - 1 - now, lanes, stride=LANE)
        state = state + gain_ref[at, :] * mul(state, drift_w) + resid_ref[at, :]
        path_ref[at, :] = guess_ref[at, :] + state
        adjoint = source_ref[back, :] + carry
        scaled = gain_back_ref[back, :] * adjoint
        pre_ref[back, :] = scaled
        return state, adjoint + mul_t(scaled, drift_wt)

    lax.fori_loop(0, LANE, walk, (state_ref[...], carry_ref[...]), unroll=2)

    pre_high, pre_low = split(pre_ref[...])
    pre_w = jnp.concatenate([pre_high, pre_low], axis=1)
    sums = halves(jnp.dot(high_ref[...], pre_w, preferred_element_type=F32)) + jnp.dot(
        low_ref[...], pre_high, preferred_element_type=F32
    )
    recur = sums[:hidden]
    for s in range(seqs):
        recur = recur + column(edges[s], unit) * pre_ref[pl.ds(s * count, 1), :]
    recur = recur.T - recur
    half = hidden // 2
    row = lax.broadcasted_iota(jnp.int32, (half, half), 0)
    col = lax.broadcasted_iota(jnp.int32, (half, half), 1)
    folded = jnp.where(col > row, recur[:half, :half], recur[half:, half:])
    grads_ref[pl.ds(0, half), :] = jnp.concatenate([folded, recur[:half, half:]], axis=1)
    grads_ref[pl.ds(half, sums.shape[0] - hidden), :] = sums[hidden:]


def unfold_kernel(place_ref, mine_ref, other_ref, recur_ref, in_ref):
    hidden = recur_ref.shape[0]
    half = hidden // 2
    odd = place_ref[1] & 1 == 1
    mine, other = mine_ref[...], other_ref[...]
    whole = jnp.concatenate([jnp.where(odd, other, mine), jnp.where(odd, mine, other)], axis=0)
    in_ref[...] = whole[half:]
    row = lax.broadcasted_iota(jnp.int32, (half, half), 0)
    col = lax.broadcasted_iota(jnp.int32, (half, half), 1)
    folded, corner = whole[:half, :half], whole[:half, half:]
    first = jnp.where(col > row, folded, 0.0)
    last = jnp.where(col < row, folded, 0.0)
    recur_ref[pl.ds(0, half), :] = jnp.concatenate([first - first.T, corner], axis=1)
    recur_ref[pl.ds(half, half), :] = jnp.concatenate([-corner.T, last - last.T], axis=1)


def call(kernel, shapes, in_specs, scratch=(), flops=0, room=24, out_specs=None):
    shapes = [shape if hasattr(shape, "dtype") else jax.ShapeDtypeStruct(shape, F32) for shape in shapes]
    return pl.pallas_call(
        kernel,
        out_shape=shapes,
        in_specs=in_specs,
        out_specs=out_specs or [VMEM] * len(shapes),
        scratch_shapes=[pltpu.VMEM(s, F32) if isinstance(s, tuple) else s for s in scratch],
        compiler_params=pltpu.CompilerParams(vmem_limit_bytes=room * MIB),
        cost_estimate=pl.CostEstimate(flops=flops, bytes_accessed=1 << 20, transcendentals=0),
    )


def swapped(value, axis, distance):
    return lax.ppermute(value, axis, [(i, i ^ distance) for i in range(lax.axis_size(axis))])


def levels_of(axis):
    return lax.axis_size(axis).bit_length() - 1


def on_device(
    inputs, guess_path, recur_weight, damping, in_weight, bias_term, targets, target_steps
):
    seqs, count, hidden = guess_path.shape
    blocks = targets.shape[1]
    features = inputs.shape[2]
    rows = seqs * count
    lanes = rows // LANE
    chunks = lanes // seqs
    hits = seqs * blocks
    total_seqs = seqs * lax.axis_size("batch")
    place = jnp.stack([lax.axis_index("seq"), lax.axis_index("batch")]).astype(jnp.int32)
    x = inputs.reshape(rows, features)
    guess = guess_path.reshape(rows, hidden)
    keep = rows * hidden * hidden * 4 <= KEEP
    depth = LANE if keep else 1

    message, maps, before, start, hit, reach, reach_off, gain, resid, drift = call(
        functools.partial(compose_kernel, seqs, blocks, total_seqs, keep),
        [
            (seqs, 2 * hidden + 8, hidden),
            (lanes, hidden, hidden),
            (lanes, hidden, hidden),
            (lanes, hidden),
            (hits, hidden, hidden),
            (hits, hidden, hidden),
            (hits, hidden),
            (rows, hidden),
            (rows, hidden),
            (hidden, hidden),
        ],
        [SMEM, SMEM] + [VMEM] * 7,
        [
            (depth, lanes, hidden, hidden),
            (lanes, hidden, hidden),
            (depth, lanes, hidden),
            (hits, hidden),
            (rows, hidden),
            pltpu.SemaphoreType.DMA(()),
            pltpu.SemaphoreType.DMA(()),
        ],
        room=56,
        out_specs=[VMEM, ANY, ANY] + [VMEM] * 7,
    )(place, target_steps, x, guess, recur_weight, damping.reshape(1, hidden), in_weight,
      bias_term.reshape(1, hidden), targets.reshape(hits, hidden))

    home, pull, high, low = call(
        functools.partial(prepare_kernel, seqs, blocks),
        [
            (lanes, hidden, hidden),
            (hits, chunks, hidden, hidden),
            jax.ShapeDtypeStruct((hidden + features, rows), BF16),
            jax.ShapeDtypeStruct((hidden + features, rows), BF16),
        ],
        [SMEM] + [VMEM] * 4,
        [(rows, hidden)],
        flops=1 << 32,
    )(target_steps, maps, hit, x, guess)

    levels = levels_of("seq")
    groups, received = [message], []
    for level in range(levels - 1):
        received.append(swapped(groups[-1], "seq", 1 << level))
        with_map = level < levels - 2
        height = (2 if with_map else 1) * hidden + 8
        groups += call(
            functools.partial(join_kernel, level, with_map),
            [(seqs, height, hidden)],
            [SMEM, VMEM, VMEM, VMEM],
        )(place, drift, groups[-1], received[-1])
    other = swapped(groups[-1], "seq", 1 << (levels - 1))
    square = (seqs, hidden, hidden)
    entry, tail, back, sides = call(
        functools.partial(sides_kernel, levels - 1),
        [square, square, square, (8 * seqs, hidden)],
        [SMEM] + [VMEM] * (2 * levels - 1),
        flops=1 << 30,
    )(place, drift, *groups[:-1], *received)

    path, grads = call(
        functools.partial(solve_kernel, seqs, blocks, total_seqs, levels - 1),
        [(rows, hidden), (hidden // 2 + features, hidden)],
        [SMEM, SMEM] + [VMEM] * 18,
        [(lanes, hidden), (lanes, hidden), (rows, hidden), (rows, hidden), (rows, hidden)],
    )(place, target_steps, drift, groups[-1], other, entry, tail, back, sides, before, start, home,
      pull, reach, reach_off, gain, resid, guess, high, low)

    middle = grads.shape[0] // 2
    odd = place[1] & 1 == 1
    kept = jnp.where(odd, grads[middle:], grads[:middle])
    given = jnp.where(odd, grads[:middle], grads[middle:])
    kept = kept + swapped(given, "batch", 1)
    for level in range(1, levels_of("batch")):
        kept = kept + swapped(kept, "batch", 1 << level)
    for level in range(levels):
        kept = kept + swapped(kept, "seq", 1 << level)
    grad_recur, grad_in = call(
        unfold_kernel,
        [(hidden, hidden), (features, hidden)],
        [SMEM, VMEM, VMEM],
    )(place, kept, swapped(kept, "batch", 1))
    return (path.reshape(seqs, count, hidden), grad_recur, grad_in)


def solution(mesh):
    placed = (
        P("batch", "seq", None),
        P("batch", "seq", None),
        P(),
        P(),
        P(),
        P(),
        P("batch", "seq", None),
        P("batch", "seq"),
    )
    return jax.shard_map(
        on_device,
        mesh=mesh,
        in_specs=placed,
        out_specs=(P("batch", "seq", None), P(), P()),
        check_vma=False,
    )
```

```python
import functools

import jax
import jax.numpy as jnp
from jax import lax
from jax.experimental import pallas as pl
from jax.experimental.pallas import tpu as pltpu
from jax.sharding import PartitionSpec as P

LANE = 16
MIB = 1 << 20
UNROLL = 5
ROOM = 41
KEEP = 36 * MIB
F32 = jnp.float32
BF16 = jnp.bfloat16
VMEM = pl.BlockSpec(memory_space=pltpu.VMEM)
HBM = pl.BlockSpec(memory_space=pltpu.HBM)


def far(shape):
    return pltpu.HBM(shape, F32)


def near(shape):
    return pltpu.VMEM(shape, F32)


euler_step = 0.02


def split(value):
    high = value.astype(BF16)
    return high, (value - high.astype(F32)).astype(BF16)


def left(value):
    return jnp.concatenate(split(value), axis=1)


def right(weight):
    row = jnp.concatenate(split(weight), axis=1)
    return jnp.concatenate([row, row], axis=0)


def right_t(weight):
    high, low = split(weight)
    return jnp.concatenate(
        [jnp.concatenate([high, high], axis=1), jnp.concatenate([low, low], axis=1)], axis=0
    )


def halves(wide):
    hidden = wide.shape[1] // 2
    return wide[:, :hidden] + wide[:, hidden:]


def mul(x, packed):
    return halves(jnp.dot(left(x), packed, preferred_element_type=F32))


def mul_t(x, packed):
    return halves(
        lax.dot_general(left(x), packed, (((1,), (1,)), ((), ())), preferred_element_type=F32)
    )


def mm(x, weight):
    return mul(x, right(weight))


def mm_t(x, weight):
    return mul_t(x, right_t(weight))


def eight(row):
    return jnp.broadcast_to(row, (8, row.shape[1]))


def identity(hidden):
    rows = lax.broadcasted_iota(jnp.int32, (hidden, hidden), 0)
    return (rows == lax.broadcasted_iota(jnp.int32, (hidden, hidden), 1)).astype(F32)


def drift_t(recur_ref, damping_ref):
    weight = recur_ref[...]
    return weight.T - weight - identity(weight.shape[0]) * damping_ref[...]


def column(row, unit):
    return jnp.broadcast_to(jnp.sum(unit * row, axis=1, keepdims=True), unit.shape)


def along(col, weight):
    return jnp.sum(col * weight, axis=0, keepdims=True)


OFFSET, ADJOINT, DRIVE, FIRST, LAST = range(5)


def vectors(*rows):
    hidden = rows[0].shape[1]
    blank = jnp.zeros((8 - len(rows), hidden), F32)
    return jnp.concatenate([row[:1] for row in rows] + [blank], axis=0)


def compose_kernel(
    seqs, blocks, total_seqs, keep, steps_in, x_in, guess_in, recur_in, damping_in, in_in, bias_in,
    targets_in,
    message_ref, maps_out, before_out, start_ref, hit_ref, reach_ref, reach_off_ref, gain_ref,
    resid_ref, drift_ref,
    record_ref, record_off_ref, maps_ref, before_ref, off_ref, hit_off_ref, prev_ref,
    steps_ref, x_ref, guess_ref, recur_ref, damping_ref, in_ref, bias_ref, targets_ref, sems,
):
    fetches = [
        pltpu.make_async_copy(source, to, sems.at[i])
        for i, (source, to) in enumerate([
            (recur_in, recur_ref), (damping_in, damping_ref), (guess_in, guess_ref), (x_in, x_ref),
            (in_in, in_ref), (bias_in, bias_ref), (targets_in, targets_ref), (steps_in, steps_ref),
        ])
    ]
    for fetch in fetches:
        fetch.start()
    for fetch in fetches[:3]:
        fetch.wait()
    rows, hidden = guess_ref.shape
    count = rows // seqs
    chunks = count // LANE
    lanes = seqs * chunks
    block = count // blocks
    drift = drift_t(recur_ref, damping_ref)
    drift_ref[...] = drift
    drift_w = right(drift)

    guess = guess_ref[...]
    prev_ref[pl.ds(1, rows - 1), :] = guess_ref[pl.ds(0, rows - 1), :]
    for s in range(seqs):
        prev_ref[pl.ds(s * count, 1), :] = jnp.zeros((1, hidden), F32)
    prev = prev_ref[...]
    for fetch in fetches[3:]:
        fetch.wait()
    x_high, x_low = split(x_ref[...])
    in_w = jnp.concatenate(split(in_ref[...]), axis=1)
    drive = bias_ref[...] + halves(
        jnp.dot(x_high, in_w, preferred_element_type=F32)
        + jnp.dot(x_low, in_w, preferred_element_type=F32)
    )
    activation = jnp.tanh(mul(prev, drift_w) + drive)
    gain_ref[...] = euler_step * (1.0 - activation * activation)
    resid_ref[...] = prev + euler_step * activation - guess
    own = (lax.axis_index("seq") == 0).astype(F32)
    for s in range(seqs):
        edge = pl.ds(s * count, 1)
        gain_ref[edge, :] = gain_ref[edge, :] * own
        resid_ref[edge, :] = resid_ref[edge, :] * own

    unit = identity(hidden)
    for lane in range(lanes):
        first = unit + drift * gain_ref[pl.ds(lane * LANE, 1), :]
        maps_ref[lane] = first
        if keep:
            record_ref[0, lane] = first
    off_ref[...] = resid_ref[pl.ds(0, lanes, stride=LANE), :]
    if keep:
        record_off_ref[0] = off_ref[...]

    def place(j):
        step = (j % blocks) * block + steps_ref[j // blocks, j % blocks]
        return (j // blocks) * chunks + step // LANE, step % LANE, (j // blocks) * count + step

    def capture(now):
        for j in range(seqs * blocks):
            lane, at, _ = place(j)

            @pl.when(at == now)
            def _():
                hit_ref[j] = maps_ref[lane]
                hit_off_ref[pl.ds(j, 1), :] = off_ref[pl.ds(lane, 1), :]

    def advance(now, _):
        off = off_ref[...]
        off = (
            off
            + gain_ref[pl.ds(now, lanes, stride=LANE), :] * mul(off, drift_w)
            + resid_ref[pl.ds(now, lanes, stride=LANE), :]
        )
        off_ref[...] = off
        if keep:
            record_off_ref[now] = off
        for lane in range(0, lanes, 2):
            pair = maps_ref[lane : lane + 2].reshape(2 * hidden, hidden)
            moved = mul(pair, drift_w)
            for k in range(2):
                gain_now = gain_ref[pl.ds((lane + k) * LANE + now, 1), :]
                part = slice(k * hidden, (k + 1) * hidden)
                longer = pair[part] + gain_now * moved[part]
                maps_ref[lane + k] = longer
                if keep:
                    record_ref[now, lane + k] = longer
        if not keep:
            capture(now)
        return 0

    if keep:
        lax.fori_loop(1, LANE, advance, 0, unroll=UNROLL)
        for j in range(seqs * blocks):
            lane, at, _ = place(j)
            hit_ref[j] = record_ref[at, lane]
            hit_off_ref[pl.ds(j, 1), :] = record_off_ref[at, pl.ds(lane, 1), :]
    else:
        capture(0)
        lax.fori_loop(1, LANE, advance, 0)
    maps_copy = pltpu.make_async_copy(maps_ref, maps_out, sems.at[8])
    maps_copy.start()

    running = [unit] * seqs
    offset = [jnp.zeros((8, hidden), F32)] * seqs
    for chunk in range(chunks):
        for s in range(seqs):
            lane = s * chunks + chunk
            before_ref[lane] = running[s]
            start_ref[pl.ds(lane, 1), :] = offset[s][:1]
            this, this_off = maps_ref[lane], off_ref[pl.ds(lane, 1), :]
            if chunk == 0:
                running[s], offset[s] = this, eight(this_off)
            else:
                packed = right(this)
                running[s] = mul(running[s], packed)
                offset[s] = mul(offset[s], packed) + this_off
    before_copy = pltpu.make_async_copy(before_ref, before_out, sems.at[9])
    before_copy.start()

    for s in range(seqs):
        message_ref[s, pl.ds(0, hidden), :] = running[s]
        total = jnp.zeros((hidden, hidden), F32)
        total_off = jnp.zeros((8, hidden), F32)
        for k in range(blocks):
            j = s * blocks + k
            lane, _, row = place(j)
            packed = right(hit_ref[j])
            reach = mul(before_ref[lane], packed)
            reach_off = mul(eight(start_ref[pl.ds(lane, 1), :]), packed) + hit_off_ref[pl.ds(j, 1), :]
            reach_ref[j] = reach
            miss = reach_off + guess_ref[pl.ds(row, 1), :] - targets_ref[pl.ds(j, 1), :]
            reach_off_ref[pl.ds(j, 1), :] = miss[:1]
            reach_t = right_t(reach)
            total = total + mul_t(reach, reach_t)
            total_off = total_off + mul_t(miss, reach_t)
        message_ref[s, pl.ds(hidden, hidden), :] = total / total_seqs
        message_ref[s, pl.ds(2 * hidden, 8), :] = vectors(
            offset[s], total_off / total_seqs, drive[s * count : s * count + 1],
            guess_ref[pl.ds(s * count, 1), :], guess_ref[pl.ds((s + 1) * count - 1, 1), :],
        )
    maps_copy.wait()
    before_copy.wait()


def opened(ref, s, with_map=True):
    hidden = ref.shape[2]
    at = hidden if with_map else 0
    rows = [eight(ref[s, pl.ds(at + hidden + k, 1), :]) for k in range(5)]
    return (ref[s, pl.ds(0, hidden), :] if with_map else None, ref[s, pl.ds(at, hidden), :], rows)


def pick(flag, one, other):
    return jax.tree.map(lambda a, b: jnp.where(flag, a, b), one, other)


def crossing(last, drive, first, drift_w):
    activation = jnp.tanh(mul(last, drift_w) + drive)
    return euler_step * (1.0 - activation * activation), last + euler_step * activation - first


def join(one, two, drift_w, with_map=True):
    map_1, curve_1, rows_1 = one
    map_2, curve_2, rows_2 = two
    gain, resid = crossing(rows_1[LAST], rows_2[DRIVE], rows_2[FIRST], drift_w)
    map_1 = map_1 + mul(map_1, drift_w) * gain[:1]
    off_1 = rows_1[OFFSET] + mul(rows_1[OFFSET], drift_w) * gain + resid
    curve_w, map_w, map_1_t = right(curve_2), right(map_2), right_t(map_1)
    curve = curve_1 + mul_t(mul(map_1, curve_w), map_1_t)
    adjoint = rows_1[ADJOINT] + mul_t(mul(off_1, curve_w) + rows_2[ADJOINT], map_1_t)
    rows = [mul(off_1, map_w) + rows_2[OFFSET], adjoint, rows_1[DRIVE], rows_1[FIRST], rows_2[LAST]]
    return (mul(map_1, map_w) if with_map else None), curve, rows


def join_kernel(level, with_map, drift_ref, mine_ref, other_ref, _, out_ref):
    seqs, hidden = mine_ref.shape[0], mine_ref.shape[2]
    upper = (lax.axis_index("seq") >> level) & 1 == 1
    drift_w = right(drift_ref[...])
    for s in range(seqs):
        mine, other = opened(mine_ref, s), opened(other_ref, s)
        whole, curve, rows = join(pick(upper, other, mine), pick(upper, mine, other), drift_w, with_map)
        at = 0
        if with_map:
            out_ref[s, pl.ds(0, hidden), :] = whole
            at = hidden
        out_ref[s, pl.ds(at, hidden), :] = curve
        out_ref[s, pl.ds(at + hidden, 8), :] = vectors(*rows)


def sides_kernel(levels, drift_ref, *refs):
    mines, others = refs[:levels], refs[levels : 2 * levels]
    entry_ref, tail_ref, back_ref, rows_ref = refs[2 * levels :]
    seqs, hidden = entry_ref.shape[0], entry_ref.shape[1]
    drift_w = right(drift_ref[...])
    unit = identity(hidden)
    for s in range(seqs):
        zero = jnp.zeros((8, hidden), F32)
        lead, lead_off = unit, zero
        after = (unit, jnp.zeros((hidden, hidden), F32), [zero] * 5)
        edge, edge_gain = zero, zero
        place = lax.axis_index("seq")
        fresh = place >= 0
        for level in range(levels):
            upper = (place >> level) & 1 == 1
            mine, other = opened(mines[level], s), opened(others[level], s)
            gain, resid = crossing(other[2][LAST], mine[2][DRIVE], mine[2][FIRST], drift_w)
            far = other[0] + mul(other[0], drift_w) * gain[:1]
            far_off = other[2][OFFSET] + mul(other[2][OFFSET], drift_w) * gain + resid
            lead_w = right(lead)
            longer = (mul(far, lead_w), mul(far_off, lead_w) + lead_off)
            known = jnp.logical_and(upper, fresh)
            edge, edge_gain = pick(known, (other[2][LAST], gain), (edge, edge_gain))
            fresh = jnp.logical_and(fresh, jnp.logical_not(upper))
            after[2][LAST] = mine[2][LAST]
            extended = join(after, other, drift_w)
            lead, lead_off = pick(upper, longer, (lead, lead_off))
            after = pick(upper, after, extended)
        own_map, _, own_rows = opened(mines[0], s)
        own_w, curve_w = right(own_map), right(after[1])
        entry_ref[s] = lead
        tail_ref[s] = mul(mul(lead, own_w), curve_w)
        back_ref[s] = after[0].T
        leaving = mul(lead_off, own_w) + own_rows[OFFSET]
        tail_off = mul(leaving, curve_w) + after[2][ADJOINT]
        rows_ref[pl.ds(8 * s, 8), :] = vectors(lead_off, tail_off, edge, edge_gain)


def prepare_kernel(
    seqs, blocks, steps_in, maps_in, x_in, guess_in, hit_ref,
    home_out, pull_out, high_ref, low_ref, ready_ref,
    home_ref, pull_ref, prev_ref, steps_ref, maps_ref, x_ref, guess_ref, in_sems, out_sems,
):
    fetches = [
        pltpu.make_async_copy(source, to, in_sems.at[i])
        for i, (source, to) in enumerate(
            [(maps_in, maps_ref), (steps_in, steps_ref), (guess_in, guess_ref), (x_in, x_ref)]
        )
    ]
    for fetch in fetches:
        fetch.start()
    ready_ref[...] = jnp.zeros_like(ready_ref)
    rows, hidden = guess_ref.shape
    count = rows // seqs
    chunks = count // LANE
    per_block = chunks // blocks
    unit = identity(hidden)
    blank = jnp.zeros((hidden, hidden), F32)
    home = [unit] * seqs
    pulls = [[blank] * blocks for _ in range(seqs)]
    sends = []

    def send(source, to):
        copy = pltpu.make_async_copy(source, to, out_sems.at[len(sends)])
        copy.start()
        sends.append(copy)

    fetches[0].wait()
    fetches[1].wait()
    for chunk in reversed(range(chunks)):
        for s in range(seqs):
            lane = s * chunks + chunk
            home_ref[lane] = home[s]
            active = [k for k in range(blocks) if chunk < (k + 1) * per_block]
            for k in active:
                pull_ref[s * blocks + k, chunk] = pulls[s][k]
            if chunk % per_block == 0:
                for k in active:
                    part = (s * blocks + k, pl.ds(chunk, per_block))
                    send(pull_ref.at[part], pull_out.at[part])
                part = pl.ds(lane, per_block)
                send(home_ref.at[part], home_out.at[part])
            if chunk:
                stack = jnp.concatenate([home[s]] + [pulls[s][k] for k in active], axis=0)
                stack = mul_t(stack, right_t(maps_ref[lane]))
                home[s] = stack[:hidden]
                for i, k in enumerate(active):
                    owner = (k * (count // blocks) + steps_ref[s, k]) // LANE
                    part = stack[(i + 1) * hidden : (i + 2) * hidden]
                    pulls[s][k] = jnp.where(owner == chunk, hit_ref[s * blocks + k].T, part)
    fetches[2].wait()
    fetches[3].wait()
    prev_ref[pl.ds(1, rows - 1), :] = guess_ref[pl.ds(0, rows - 1), :]
    for s in range(seqs):
        prev_ref[pl.ds(s * count, 1), :] = jnp.zeros((1, hidden), F32)
    high_ref[pl.ds(0, hidden), :], low_ref[pl.ds(0, hidden), :] = split(prev_ref[...].T)
    high_ref[pl.ds(hidden, x_ref.shape[1]), :], low_ref[pl.ds(hidden, x_ref.shape[1]), :] = split(
        x_ref[...].T
    )
    for copy in sends:
        copy.wait()


def solve_kernel(
    seqs, blocks, total_seqs, level, steps_in, drift_ref, mine_ref, other_ref,
    home_in, pull_in, entry_ref, tail_ref, back_ref, sides_ref, before_ref, start_ref, reach_ref,
    reach_off_ref, gain_ref, resid_ref, guess_ref, high_ref, low_ref,
    path_out, grads_ref,
    state_ref, carry_ref, source_ref, pre_ref, gain_back_ref, path_ref, home_ref, pull_ref, steps_ref, sems,
):
    rows, hidden = guess_ref.shape
    count = rows // seqs
    chunks = count // LANE
    lanes = seqs * chunks
    block = count // blocks
    per_block = chunks // blocks
    fetch_steps = pltpu.make_async_copy(steps_in, steps_ref, sems.at[0])
    fetch_steps.start()
    per_block = guess_ref.shape[0] // seqs // LANE // blocks
    fetches = [[] for _ in range(blocks)]

    def fetch(part, source, to):
        copy = pltpu.make_async_copy(source, to, sems.at[2 + sum(map(len, fetches))])
        copy.start()
        fetches[part].append(copy)

    for part in range(blocks):
        for s in range(seqs):
            at = pl.ds((s * blocks + part) * per_block, per_block)
            fetch(part, home_in.at[at], home_ref.at[at])
            for k in range(part, blocks):
                at = (s * blocks + k, pl.ds(part * per_block, per_block))
                fetch(part, pull_in.at[at], pull_ref.at[at])
    place = lax.axis_index("seq")
    upper = (place >> level) & 1 == 1
    lowest = (place & ((1 << level) - 1)) == 0
    drift = drift_ref[...]
    drift_w = right(drift)
    drift_wt = right_t(drift)
    unit = identity(hidden)
    source_ref[...] = jnp.zeros_like(source_ref)
    gain_back_ref[...] = gain_ref[...]

    entries, tails, sources, edges = [], [], [], []
    for s in range(seqs):
        mine, other = opened(mine_ref, s, False), opened(other_ref, s, False)
        last, middle = pick(upper, (other[2][LAST], other[2][OFFSET]), (mine[2][LAST], mine[2][OFFSET]))
        drive, first = pick(upper, (mine[2][DRIVE], mine[2][FIRST]), (other[2][DRIVE], other[2][FIRST]))
        gain, resid = crossing(last, drive, first, drift_w)
        middle = middle + mul(middle, drift_w) * gain + resid
        middle_col = column(middle[:1], unit)
        row = along(middle_col, jnp.where(upper, entry_ref[s], other[1]))
        lead_off, tail_off, edge, edge_gain = [sides_ref[pl.ds(8 * s + k, 1), :] for k in range(4)]
        beyond = eight(row) + other[2][ADJOINT]
        beyond = beyond + mul_t(beyond * gain, drift_wt)
        entries.append(column(jnp.where(upper, row, 0.0) + lead_off, unit))
        tail = jnp.where(
            upper, along(middle_col, tail_ref[s]), along(column(beyond[:1], unit), back_ref[s])
        )
        tails.append(column(tail + tail_off, unit))
        known = jnp.logical_and(upper, lowest)
        edge = jnp.where(known, last[:1], edge)
        edges.append(edge)
        edge_gain = jnp.where(known, gain[:1], edge_gain)
        at = pl.ds(s * count, 1)
        gain_back_ref[at, :] = gain_ref[at, :] + edge_gain
        here = []
        if s == 0:
            fetch_steps.wait()
        for k in range(blocks):
            j = s * blocks + k
            miss = (along(entries[s], reach_ref[j]) + reach_off_ref[pl.ds(j, 1), :]) / total_seqs
            source_ref[pl.ds(s * count + k * block + steps_ref[s, k], 1), :] = miss
            here.append(column(miss, unit))
        sources.append(here)

    for part in range(blocks):
        for copy in fetches[part]:
            copy.wait()

        def ends(chunk, _):
            for s in range(seqs):
                lane = s * chunks + chunk
                state_ref[pl.ds(lane, 1), :] = along(entries[s], before_ref[lane]) + start_ref[pl.ds(lane, 1), :]
                sums = tails[s] * home_ref[lane]
                for k in range(part, blocks):
                    sums = sums + sources[s][k] * pull_ref[s * blocks + k, chunk]
                carry_ref[pl.ds(lane, 1), :] = jnp.sum(sums, axis=0, keepdims=True)
            return 0

        lax.fori_loop(part * per_block, (part + 1) * per_block, ends, 0, unroll=2)

    def walk(now, both):
        state, carry = both
        at = pl.ds(now, lanes, stride=LANE)
        back = pl.ds(LANE - 1 - now, lanes, stride=LANE)
        state = state + gain_ref[at, :] * mul(state, drift_w) + resid_ref[at, :]
        path_ref[at, :] = guess_ref[at, :] + state
        adjoint = source_ref[back, :] + carry
        scaled = gain_back_ref[back, :] * adjoint
        pre_ref[back, :] = scaled
        return state, adjoint + mul_t(scaled, drift_wt)

    lax.fori_loop(0, LANE, walk, (state_ref[...], carry_ref[...]), unroll=2)
    path_copy = pltpu.make_async_copy(path_ref, path_out, sems.at[1])
    path_copy.start()

    pre_high, pre_low = split(pre_ref[...])
    pre_w = jnp.concatenate([pre_high, pre_low], axis=1)
    sums = halves(jnp.dot(high_ref[...], pre_w, preferred_element_type=F32)) + jnp.dot(
        low_ref[...], pre_high, preferred_element_type=F32
    )
    recur = sums[:hidden]
    for s in range(seqs):
        recur = recur + column(edges[s], unit) * pre_ref[pl.ds(s * count, 1), :]
    recur = recur.T - recur
    half = hidden // 2
    row = lax.broadcasted_iota(jnp.int32, (half, half), 0)
    col = lax.broadcasted_iota(jnp.int32, (half, half), 1)
    folded = jnp.where(col > row, recur[:half, :half], recur[half:, half:])
    grads_ref[pl.ds(0, half), :] = jnp.concatenate([folded, recur[:half, half:]], axis=1)
    grads_ref[pl.ds(half, sums.shape[0] - hidden), :] = sums[hidden:]
    path_copy.wait()


def unfold_kernel(mine_ref, other_ref, recur_ref, in_ref):
    hidden = recur_ref.shape[0]
    half = hidden // 2
    odd = lax.axis_index("batch") & 1 == 1
    mine, other = mine_ref[...], other_ref[...]
    whole = jnp.concatenate([jnp.where(odd, other, mine), jnp.where(odd, mine, other)], axis=0)
    in_ref[...] = whole[half:]
    row = lax.broadcasted_iota(jnp.int32, (half, half), 0)
    col = lax.broadcasted_iota(jnp.int32, (half, half), 1)
    folded, corner = whole[:half, :half], whole[:half, half:]
    first = jnp.where(col > row, folded, 0.0)
    last = jnp.where(col < row, folded, 0.0)
    recur_ref[pl.ds(0, half), :] = jnp.concatenate([first - first.T, corner], axis=1)
    recur_ref[pl.ds(half, half), :] = jnp.concatenate([-corner.T, last - last.T], axis=1)


def call(kernel, shapes, in_specs, scratch=(), flops=0, room=14):
    out_shapes = [jax.ShapeDtypeStruct(s, F32) if isinstance(s, tuple) else s for s in shapes]
    run = pl.pallas_call(
        kernel,
        out_shape=out_shapes,
        in_specs=in_specs,
        out_specs=[
            HBM if getattr(s, "memory_space", None) == pltpu.HBM else VMEM for s in out_shapes
        ],
        scratch_shapes=[pltpu.VMEM(s, F32) if isinstance(s, tuple) else s for s in scratch],
        compiler_params=pltpu.CompilerParams(vmem_limit_bytes=room * MIB),
        cost_estimate=pl.CostEstimate(flops=flops, bytes_accessed=1 << 20, transcendentals=0),
    )

    def pinned(*operands):
        return run(*[
            pltpu.with_memory_space_constraint(x, pltpu.HBM) if spec is HBM else x
            for x, spec in zip(operands, in_specs, strict=True)
        ])

    return pinned


def swapped(value, axis, distance):
    return lax.ppermute(value, axis, [(i, i ^ distance) for i in range(lax.axis_size(axis))])


def levels_of(axis):
    return lax.axis_size(axis).bit_length() - 1


def on_device(
    inputs, guess_path, recur_weight, damping, in_weight, bias_term, targets, target_steps
):
    seqs, count, hidden = guess_path.shape
    blocks = targets.shape[1]
    features = inputs.shape[2]
    rows = seqs * count
    lanes = rows // LANE
    chunks = lanes // seqs
    hits = seqs * blocks
    total_seqs = seqs * lax.axis_size("batch")
    x = inputs.reshape(rows, features)
    guess = guess_path.reshape(rows, hidden)
    keep = rows * hidden * hidden * 4 <= KEEP
    depth = LANE if keep else 1

    message, maps, before, start, hit, reach, reach_off, gain, resid, drift = call(
        functools.partial(compose_kernel, seqs, blocks, total_seqs, keep),
        [
            near((seqs, 2 * hidden + 8, hidden)),
            far((lanes, hidden, hidden)),
            far((lanes, hidden, hidden)),
            (lanes, hidden),
            (hits, hidden, hidden),
            (hits, hidden, hidden),
            (hits, hidden),
            (rows, hidden),
            (rows, hidden),
            (hidden, hidden),
        ],
        [HBM] * 8,
        [
            (depth, lanes if keep else 1, hidden, hidden),
            (depth, lanes if keep else 1, hidden),
            (lanes, hidden, hidden),
            (lanes, hidden, hidden),
            (lanes, hidden),
            (hits, hidden),
            (rows, hidden),
            pltpu.SMEM((seqs, blocks), jnp.int32),
            (rows, features),
            (rows, hidden),
            (hidden, hidden),
            (1, hidden),
            (features, hidden),
            (1, hidden),
            (hits, hidden),
            pltpu.SemaphoreType.DMA((10,)),
        ],
        room=ROOM,
    )(target_steps, x, guess, recur_weight, damping.reshape(1, hidden), in_weight,
      bias_term.reshape(1, hidden), targets.reshape(hits, hidden))

    home, pull, high, low, ready = call(
        functools.partial(prepare_kernel, seqs, blocks),
        [
            far((lanes, hidden, hidden)),
            far((hits, chunks, hidden, hidden)),
            jax.ShapeDtypeStruct((hidden + features, rows), BF16),
            jax.ShapeDtypeStruct((hidden + features, rows), BF16),
            (8, hidden),
        ],
        [HBM, HBM, HBM, HBM, VMEM],
        [
            (lanes, hidden, hidden),
            (hits, chunks, hidden, hidden),
            (rows, hidden),
            pltpu.SMEM((seqs, blocks), jnp.int32),
            (lanes, hidden, hidden),
            (rows, features),
            (rows, hidden),
            pltpu.SemaphoreType.DMA((4,)),
            pltpu.SemaphoreType.DMA((seqs * blocks * (blocks + 3) // 2,)),
        ],
        flops=1 << 32,
        room=20,
    )(target_steps, maps, x, guess, hit)

    levels = levels_of("seq")
    groups, received = [message], []
    for level in range(levels - 1):
        received.append(swapped(groups[-1], "seq", 1 << level))
        with_map = level < levels - 2
        height = (2 if with_map else 1) * hidden + 8
        groups += call(
            functools.partial(join_kernel, level, with_map),
            [(seqs, height, hidden)],
            [VMEM, VMEM, VMEM, VMEM],
        )(drift, groups[-1], received[-1], ready)
    other = swapped(groups[-1], "seq", 1 << (levels - 1))
    square = (seqs, hidden, hidden)
    entry, tail, back, sides = call(
        functools.partial(sides_kernel, levels - 1),
        [square, square, square, (8 * seqs, hidden)],
        [VMEM] * (2 * levels - 1),
        flops=1 << 30,
    )(drift, *groups[:-1], *received)

    path, grads = call(
        functools.partial(solve_kernel, seqs, blocks, total_seqs, levels - 1),
        [far((rows, hidden)), near((hidden // 2 + features, hidden))],
        [HBM] + [VMEM] * 3 + [HBM] * 2 + [VMEM] * 13,
        [(lanes, hidden)] * 2 + [(rows, hidden)] * 4 + [
            (lanes, hidden, hidden),
            (hits, chunks, hidden, hidden),
            pltpu.SMEM((seqs, blocks), jnp.int32),
            pltpu.SemaphoreType.DMA((2 + seqs * blocks * (blocks + 3) // 2,)),
        ],
    )(target_steps, drift, groups[-1], other, home, pull, entry, tail, back, sides, before, start,
      reach, reach_off, gain, resid, guess, high, low)

    middle = grads.shape[0] // 2
    odd = lax.axis_index("batch") & 1 == 1
    kept = jnp.where(odd, grads[middle:], grads[:middle])
    given = jnp.where(odd, grads[:middle], grads[middle:])
    kept = kept + swapped(given, "batch", 1)
    for level in range(1, levels_of("batch")):
        kept = kept + swapped(kept, "batch", 1 << level)
    for level in range(levels):
        kept = kept + swapped(kept, "seq", 1 << level)
    grad_recur, grad_in = call(
        unfold_kernel,
        [(hidden, hidden), (features, hidden)],
        [VMEM, VMEM],
    )(kept, swapped(kept, "batch", 1))
    return (path.reshape(seqs, count, hidden), grad_recur, grad_in)


def solution(mesh):
    placed = (
        P("batch", "seq", None),
        P("batch", "seq", None),
        P(),
        P(),
        P(),
        P(),
        P("batch", "seq", None),
        P("batch", "seq"),
    )
    return jax.shard_map(
        on_device,
        mesh=mesh,
        in_specs=placed,
        out_specs=(P("batch", "seq", None), P(), P()),
        check_vma=False,
    )
```

```python
import functools

import jax
import jax.numpy as jnp
from jax import lax
from jax.experimental import pallas as pl
from jax.experimental.pallas import tpu as pltpu
from jax.sharding import PartitionSpec as P

LANE = 16
MIB = 1 << 20
UNROLL = 5
ROOM = 41
KEEP = 36 * MIB
F32 = jnp.float32
BF16 = jnp.bfloat16
VMEM = pl.BlockSpec(memory_space=pltpu.VMEM)
HBM = pl.BlockSpec(memory_space=pltpu.HBM)


def far(shape):
    return pltpu.HBM(shape, F32)


def near(shape):
    return pltpu.VMEM(shape, F32)


euler_step = 0.02


def split(value):
    high = value.astype(BF16)
    return high, (value - high.astype(F32)).astype(BF16)


def left(value):
    return jnp.concatenate(split(value), axis=1)


def right(weight):
    row = jnp.concatenate(split(weight), axis=1)
    return jnp.concatenate([row, row], axis=0)


def right_t(weight):
    high, low = split(weight)
    return jnp.concatenate(
        [jnp.concatenate([high, high], axis=1), jnp.concatenate([low, low], axis=1)], axis=0
    )


def halves(wide):
    hidden = wide.shape[1] // 2
    return wide[:, :hidden] + wide[:, hidden:]


def mul(x, packed):
    return halves(jnp.dot(left(x), packed, preferred_element_type=F32))


def mul_t(x, packed):
    return halves(
        lax.dot_general(left(x), packed, (((1,), (1,)), ((), ())), preferred_element_type=F32)
    )


def mm(x, weight):
    return mul(x, right(weight))


def mm_t(x, weight):
    return mul_t(x, right_t(weight))


def eight(row):
    return jnp.broadcast_to(row, (8, row.shape[1]))


def identity(hidden):
    rows = lax.broadcasted_iota(jnp.int32, (hidden, hidden), 0)
    return (rows == lax.broadcasted_iota(jnp.int32, (hidden, hidden), 1)).astype(F32)


def drift_t(recur_ref, damping_ref):
    weight = recur_ref[...]
    return weight.T - weight - identity(weight.shape[0]) * damping_ref[...]


def column(row, unit):
    return jnp.broadcast_to(jnp.sum(unit * row, axis=1, keepdims=True), unit.shape)


def along(col, weight):
    return jnp.sum(col * weight, axis=0, keepdims=True)


OFFSET, ADJOINT, DRIVE, FIRST, LAST, DIAGONAL = range(6)


def triangles(half):
    row = lax.broadcasted_iota(jnp.int32, (half, half), 0)
    col = lax.broadcasted_iota(jnp.int32, (half, half), 1)
    return col > row, col < row


def fold(whole):
    half = whole.shape[0] // 2
    above, _ = triangles(half)
    return jnp.concatenate(
        [jnp.where(above, whole[:half, :half], whole[half:, half:]), whole[:half, half:]], axis=1
    )


def unfold(folded):
    half = folded.shape[0]
    above, below = triangles(half)
    both = folded[:, :half]
    upper = jnp.concatenate([jnp.where(above, both, 0.0), folded[:, half:]], axis=1)
    lower = jnp.concatenate([jnp.zeros((half, half), F32), jnp.where(below, both, 0.0)], axis=1)
    return jnp.concatenate([upper, lower], axis=0)


def vectors(*rows):
    hidden = rows[0].shape[1]
    blank = jnp.zeros((8 - len(rows), hidden), F32)
    return jnp.concatenate([row[:1] for row in rows] + [blank], axis=0)


def compose_kernel(
    seqs, blocks, total_seqs, keep, steps_in, x_in, guess_in, recur_in, damping_in, in_in, bias_in,
    targets_in,
    message_ref, maps_out, before_out, start_ref, hit_ref, reach_ref, reach_off_ref, gain_ref,
    resid_ref, drift_ref,
    record_ref, record_off_ref, maps_ref, before_ref, off_ref, hit_off_ref, prev_ref,
    steps_ref, x_ref, guess_ref, recur_ref, damping_ref, in_ref, bias_ref, targets_ref, sems,
):
    fetches = [
        pltpu.make_async_copy(source, to, sems.at[i])
        for i, (source, to) in enumerate([
            (recur_in, recur_ref), (damping_in, damping_ref), (guess_in, guess_ref), (x_in, x_ref),
            (in_in, in_ref), (bias_in, bias_ref), (targets_in, targets_ref), (steps_in, steps_ref),
        ])
    ]
    for fetch in fetches:
        fetch.start()
    for fetch in fetches[:3]:
        fetch.wait()
    rows, hidden = guess_ref.shape
    count = rows // seqs
    chunks = count // LANE
    lanes = seqs * chunks
    block = count // blocks
    drift = drift_t(recur_ref, damping_ref)
    drift_ref[...] = drift
    drift_w = right(drift)

    guess = guess_ref[...]
    prev_ref[pl.ds(1, rows - 1), :] = guess_ref[pl.ds(0, rows - 1), :]
    for s in range(seqs):
        prev_ref[pl.ds(s * count, 1), :] = jnp.zeros((1, hidden), F32)
    prev = prev_ref[...]
    for fetch in fetches[3:]:
        fetch.wait()
    x_high, x_low = split(x_ref[...])
    in_w = jnp.concatenate(split(in_ref[...]), axis=1)
    drive = bias_ref[...] + halves(
        jnp.dot(x_high, in_w, preferred_element_type=F32)
        + jnp.dot(x_low, in_w, preferred_element_type=F32)
    )
    activation = jnp.tanh(mul(prev, drift_w) + drive)
    gain_ref[...] = euler_step * (1.0 - activation * activation)
    resid_ref[...] = prev + euler_step * activation - guess
    own = (lax.axis_index("seq") == 0).astype(F32)
    for s in range(seqs):
        edge = pl.ds(s * count, 1)
        gain_ref[edge, :] = gain_ref[edge, :] * own
        resid_ref[edge, :] = resid_ref[edge, :] * own

    unit = identity(hidden)
    for lane in range(lanes):
        first = unit + drift * gain_ref[pl.ds(lane * LANE, 1), :]
        maps_ref[lane] = first
        if keep:
            record_ref[0, lane] = first
    off_ref[...] = resid_ref[pl.ds(0, lanes, stride=LANE), :]
    if keep:
        record_off_ref[0] = off_ref[...]

    def place(j):
        step = (j % blocks) * block + steps_ref[j // blocks, j % blocks]
        return (j // blocks) * chunks + step // LANE, step % LANE, (j // blocks) * count + step

    def capture(now):
        for j in range(seqs * blocks):
            lane, at, _ = place(j)

            @pl.when(at == now)
            def _():
                hit_ref[j] = maps_ref[lane]
                hit_off_ref[pl.ds(j, 1), :] = off_ref[pl.ds(lane, 1), :]

    def advance(now, _):
        off = off_ref[...]
        off = (
            off
            + gain_ref[pl.ds(now, lanes, stride=LANE), :] * mul(off, drift_w)
            + resid_ref[pl.ds(now, lanes, stride=LANE), :]
        )
        off_ref[...] = off
        if keep:
            record_off_ref[now] = off
        for lane in range(0, lanes, 2):
            pair = maps_ref[lane : lane + 2].reshape(2 * hidden, hidden)
            moved = mul(pair, drift_w)
            for k in range(2):
                gain_now = gain_ref[pl.ds((lane + k) * LANE + now, 1), :]
                part = slice(k * hidden, (k + 1) * hidden)
                longer = pair[part] + gain_now * moved[part]
                maps_ref[lane + k] = longer
                if keep:
                    record_ref[now, lane + k] = longer
        if not keep:
            capture(now)
        return 0

    if keep:
        lax.fori_loop(1, LANE, advance, 0, unroll=UNROLL)
        for j in range(seqs * blocks):
            lane, at, _ = place(j)
            hit_ref[j] = record_ref[at, lane]
            hit_off_ref[pl.ds(j, 1), :] = record_off_ref[at, pl.ds(lane, 1), :]
    else:
        capture(0)
        lax.fori_loop(1, LANE, advance, 0)
    maps_copy = pltpu.make_async_copy(maps_ref, maps_out, sems.at[8])
    maps_copy.start()

    running = [unit] * seqs
    offset = [jnp.zeros((8, hidden), F32)] * seqs
    for chunk in range(chunks):
        for s in range(seqs):
            lane = s * chunks + chunk
            before_ref[lane] = running[s]
            start_ref[pl.ds(lane, 1), :] = offset[s][:1]
            this, this_off = maps_ref[lane], off_ref[pl.ds(lane, 1), :]
            if chunk == 0:
                running[s], offset[s] = this, eight(this_off)
            else:
                packed = right(this)
                running[s] = mul(running[s], packed)
                offset[s] = mul(offset[s], packed) + this_off
    before_copy = pltpu.make_async_copy(before_ref, before_out, sems.at[9])
    before_copy.start()

    for s in range(seqs):
        message_ref[s, pl.ds(0, hidden), :] = running[s]
        total = jnp.zeros((hidden, hidden), F32)
        total_off = jnp.zeros((8, hidden), F32)
        for k in range(blocks):
            j = s * blocks + k
            lane, _, row = place(j)
            packed = right(hit_ref[j])
            reach = mul(before_ref[lane], packed)
            reach_off = mul(eight(start_ref[pl.ds(lane, 1), :]), packed) + hit_off_ref[pl.ds(j, 1), :]
            reach_ref[j] = reach
            miss = reach_off + guess_ref[pl.ds(row, 1), :] - targets_ref[pl.ds(j, 1), :]
            reach_off_ref[pl.ds(j, 1), :] = miss[:1]
            reach_t = right_t(reach)
            total = total + mul_t(reach, reach_t)
            total_off = total_off + mul_t(miss, reach_t)
        total = total / total_seqs
        message_ref[s, pl.ds(hidden, hidden // 2), :] = fold(total)
        message_ref[s, pl.ds(hidden + hidden // 2, 8), :] = vectors(
            offset[s], total_off / total_seqs, drive[s * count : s * count + 1],
            guess_ref[pl.ds(s * count, 1), :], guess_ref[pl.ds((s + 1) * count - 1, 1), :],
            jnp.sum(unit * total, axis=0, keepdims=True),
        )
    maps_copy.wait()
    before_copy.wait()


def opened(ref, s, with_map=True):
    hidden = ref.shape[2]
    at = hidden if with_map else 0
    rows = [eight(ref[s, pl.ds(at + hidden // 2 + k, 1), :]) for k in range(5)]
    diagonal = ref[s, pl.ds(at + hidden // 2 + DIAGONAL, 1), :]
    half = unfold(ref[s, pl.ds(at, hidden // 2), :])
    curve = half + half.T + identity(hidden) * diagonal
    return (ref[s, pl.ds(0, hidden), :] if with_map else None, curve, rows)


def pick(flag, one, other):
    return jax.tree.map(lambda a, b: jnp.where(flag, a, b), one, other)


def crossing(last, drive, first, drift_w):
    activation = jnp.tanh(mul(last, drift_w) + drive)
    return euler_step * (1.0 - activation * activation), last + euler_step * activation - first


def join(one, two, drift_w, with_map=True):
    map_1, curve_1, rows_1 = one
    map_2, curve_2, rows_2 = two
    gain, resid = crossing(rows_1[LAST], rows_2[DRIVE], rows_2[FIRST], drift_w)
    map_1 = map_1 + mul(map_1, drift_w) * gain[:1]
    off_1 = rows_1[OFFSET] + mul(rows_1[OFFSET], drift_w) * gain + resid
    curve_w, map_w, map_1_t = right(curve_2), right(map_2), right_t(map_1)
    curve = curve_1 + mul_t(mul(map_1, curve_w), map_1_t)
    adjoint = rows_1[ADJOINT] + mul_t(mul(off_1, curve_w) + rows_2[ADJOINT], map_1_t)
    rows = [mul(off_1, map_w) + rows_2[OFFSET], adjoint, rows_1[DRIVE], rows_1[FIRST], rows_2[LAST]]
    return (mul(map_1, map_w) if with_map else None), curve, rows


def join_kernel(level, with_map, drift_ref, mine_ref, other_ref, _, out_ref):
    seqs, hidden = mine_ref.shape[0], mine_ref.shape[2]
    upper = (lax.axis_index("seq") >> level) & 1 == 1
    drift_w = right(drift_ref[...])
    for s in range(seqs):
        mine, other = opened(mine_ref, s), opened(other_ref, s)
        whole, curve, rows = join(pick(upper, other, mine), pick(upper, mine, other), drift_w, with_map)
        at = 0
        if with_map:
            out_ref[s, pl.ds(0, hidden), :] = whole
            at = hidden
        out_ref[s, pl.ds(at, hidden // 2), :] = fold(curve)
        diagonal = jnp.sum(identity(hidden) * curve, axis=0, keepdims=True)
        out_ref[s, pl.ds(at + hidden // 2, 8), :] = vectors(*rows, diagonal)


def sides_kernel(levels, drift_ref, *refs):
    mines, others = refs[:levels], refs[levels : 2 * levels]
    entry_ref, tail_ref, back_ref, rows_ref = refs[2 * levels :]
    seqs, hidden = entry_ref.shape[0], entry_ref.shape[1]
    drift_w = right(drift_ref[...])
    unit = identity(hidden)
    for s in range(seqs):
        zero = jnp.zeros((8, hidden), F32)
        lead, lead_off = unit, zero
        after = (unit, jnp.zeros((hidden, hidden), F32), [zero] * 5)
        edge, edge_gain = zero, zero
        place = lax.axis_index("seq")
        fresh = place >= 0
        for level in range(levels):
            upper = (place >> level) & 1 == 1
            mine, other = opened(mines[level], s), opened(others[level], s)
            gain, resid = crossing(other[2][LAST], mine[2][DRIVE], mine[2][FIRST], drift_w)
            far = other[0] + mul(other[0], drift_w) * gain[:1]
            far_off = other[2][OFFSET] + mul(other[2][OFFSET], drift_w) * gain + resid
            lead_w = right(lead)
            longer = (mul(far, lead_w), mul(far_off, lead_w) + lead_off)
            known = jnp.logical_and(upper, fresh)
            edge, edge_gain = pick(known, (other[2][LAST], gain), (edge, edge_gain))
            fresh = jnp.logical_and(fresh, jnp.logical_not(upper))
            after[2][LAST] = mine[2][LAST]
            extended = join(after, other, drift_w)
            lead, lead_off = pick(upper, longer, (lead, lead_off))
            after = pick(upper, after, extended)
        own_map, _, own_rows = opened(mines[0], s)
        own_w, curve_w = right(own_map), right(after[1])
        entry_ref[s] = lead
        tail_ref[s] = mul(mul(lead, own_w), curve_w)
        back_ref[s] = after[0].T
        leaving = mul(lead_off, own_w) + own_rows[OFFSET]
        tail_off = mul(leaving, curve_w) + after[2][ADJOINT]
        rows_ref[pl.ds(8 * s, 8), :] = vectors(lead_off, tail_off, edge, edge_gain)


def prepare_kernel(
    seqs, blocks, steps_in, maps_in, hit_ref, home_out, pull_out, ready_ref,
    home_ref, pull_ref, steps_ref, maps_ref, in_sems, out_sems,
):
    fetches = [
        pltpu.make_async_copy(source, to, in_sems.at[i])
        for i, (source, to) in enumerate([(maps_in, maps_ref), (steps_in, steps_ref)])
    ]
    for fetch in fetches:
        fetch.start()
    ready_ref[...] = jnp.zeros_like(ready_ref)
    lanes, hidden, _ = maps_ref.shape
    chunks = lanes // seqs
    count = chunks * LANE
    per_block = chunks // blocks
    unit = identity(hidden)
    blank = jnp.zeros((hidden, hidden), F32)
    home = [unit] * seqs
    pulls = [[blank] * blocks for _ in range(seqs)]
    sends = []

    def send(source, to):
        copy = pltpu.make_async_copy(source, to, out_sems.at[len(sends)])
        copy.start()
        sends.append(copy)

    fetches[0].wait()
    fetches[1].wait()
    for chunk in reversed(range(chunks)):
        for s in range(seqs):
            lane = s * chunks + chunk
            home_ref[lane] = home[s]
            active = [k for k in range(blocks) if chunk < (k + 1) * per_block]
            for k in active:
                pull_ref[s * blocks + k, chunk] = pulls[s][k]
            if chunk % per_block == 0:
                for k in active:
                    part = (s * blocks + k, pl.ds(chunk, per_block))
                    send(pull_ref.at[part], pull_out.at[part])
                part = pl.ds(lane, per_block)
                send(home_ref.at[part], home_out.at[part])
            if chunk:
                stack = jnp.concatenate([home[s]] + [pulls[s][k] for k in active], axis=0)
                stack = mul_t(stack, right_t(maps_ref[lane]))
                home[s] = stack[:hidden]
                for i, k in enumerate(active):
                    owner = (k * (count // blocks) + steps_ref[s, k]) // LANE
                    part = stack[(i + 1) * hidden : (i + 2) * hidden]
                    pulls[s][k] = jnp.where(owner == chunk, hit_ref[s * blocks + k].T, part)
    for copy in sends:
        copy.wait()


def factors_kernel(seqs, x_in, guess_in, _, high_ref, low_ref, ready_ref, prev_ref, x_ref, guess_ref, sems):
    fetch_guess = pltpu.make_async_copy(guess_in, guess_ref, sems.at[0])
    fetch_x = pltpu.make_async_copy(x_in, x_ref, sems.at[1])
    fetch_guess.start()
    fetch_x.start()
    ready_ref[...] = jnp.zeros_like(ready_ref)
    rows, hidden = guess_ref.shape
    fetch_guess.wait()
    prev_ref[pl.ds(1, rows - 1), :] = guess_ref[pl.ds(0, rows - 1), :]
    for s in range(seqs):
        prev_ref[pl.ds(s * (rows // seqs), 1), :] = jnp.zeros((1, hidden), F32)
    high_ref[pl.ds(0, hidden), :], low_ref[pl.ds(0, hidden), :] = split(prev_ref[...].T)
    fetch_x.wait()
    rest = pl.ds(hidden, x_ref.shape[1])
    high_ref[rest, :], low_ref[rest, :] = split(x_ref[...].T)


def solve_kernel(
    seqs, blocks, total_seqs, level, steps_in, drift_ref, mine_ref, other_ref,
    home_in, pull_in, entry_ref, tail_ref, back_ref, sides_ref, before_ref, start_ref, reach_ref,
    reach_off_ref, gain_ref, resid_ref, guess_ref, high_ref, low_ref,
    path_out, grads_ref,
    state_ref, carry_ref, source_ref, pre_ref, gain_back_ref, path_ref, home_ref, pull_ref, steps_ref, sems,
):
    rows, hidden = guess_ref.shape
    count = rows // seqs
    chunks = count // LANE
    lanes = seqs * chunks
    block = count // blocks
    per_block = chunks // blocks
    fetch_steps = pltpu.make_async_copy(steps_in, steps_ref, sems.at[0])
    fetch_steps.start()
    per_block = guess_ref.shape[0] // seqs // LANE // blocks
    fetches = [[] for _ in range(blocks)]

    def fetch(part, source, to):
        copy = pltpu.make_async_copy(source, to, sems.at[2 + sum(map(len, fetches))])
        copy.start()
        fetches[part].append(copy)

    for part in range(blocks):
        for s in range(seqs):
            at = pl.ds((s * blocks + part) * per_block, per_block)
            fetch(part, home_in.at[at], home_ref.at[at])
            for k in range(part, blocks):
                at = (s * blocks + k, pl.ds(part * per_block, per_block))
                fetch(part, pull_in.at[at], pull_ref.at[at])
    place = lax.axis_index("seq")
    upper = (place >> level) & 1 == 1
    lowest = (place & ((1 << level) - 1)) == 0
    drift = drift_ref[...]
    drift_w = right(drift)
    drift_wt = right_t(drift)
    unit = identity(hidden)
    source_ref[...] = jnp.zeros_like(source_ref)
    gain_back_ref[...] = gain_ref[...]

    entries, tails, sources, edges = [], [], [], []
    for s in range(seqs):
        mine, other = opened(mine_ref, s, False), opened(other_ref, s, False)
        last, middle = pick(upper, (other[2][LAST], other[2][OFFSET]), (mine[2][LAST], mine[2][OFFSET]))
        drive, first = pick(upper, (mine[2][DRIVE], mine[2][FIRST]), (other[2][DRIVE], other[2][FIRST]))
        gain, resid = crossing(last, drive, first, drift_w)
        middle = middle + mul(middle, drift_w) * gain + resid
        middle_col = column(middle[:1], unit)
        row = along(middle_col, jnp.where(upper, entry_ref[s], other[1]))
        lead_off, tail_off, edge, edge_gain = [sides_ref[pl.ds(8 * s + k, 1), :] for k in range(4)]
        beyond = eight(row) + other[2][ADJOINT]
        beyond = beyond + mul_t(beyond * gain, drift_wt)
        entries.append(column(jnp.where(upper, row, 0.0) + lead_off, unit))
        tail = jnp.where(
            upper, along(middle_col, tail_ref[s]), along(column(beyond[:1], unit), back_ref[s])
        )
        tails.append(column(tail + tail_off, unit))
        known = jnp.logical_and(upper, lowest)
        edge = jnp.where(known, last[:1], edge)
        edges.append(edge)
        edge_gain = jnp.where(known, gain[:1], edge_gain)
        at = pl.ds(s * count, 1)
        gain_back_ref[at, :] = gain_ref[at, :] + edge_gain
        here = []
        if s == 0:
            fetch_steps.wait()
        for k in range(blocks):
            j = s * blocks + k
            miss = (along(entries[s], reach_ref[j]) + reach_off_ref[pl.ds(j, 1), :]) / total_seqs
            source_ref[pl.ds(s * count + k * block + steps_ref[s, k], 1), :] = miss
            here.append(column(miss, unit))
        sources.append(here)

    for part in range(blocks):
        for copy in fetches[part]:
            copy.wait()

        def ends(chunk, _):
            for s in range(seqs):
                lane = s * chunks + chunk
                state_ref[pl.ds(lane, 1), :] = along(entries[s], before_ref[lane]) + start_ref[pl.ds(lane, 1), :]
                sums = tails[s] * home_ref[lane]
                for k in range(part, blocks):
                    sums = sums + sources[s][k] * pull_ref[s * blocks + k, chunk]
                carry_ref[pl.ds(lane, 1), :] = jnp.sum(sums, axis=0, keepdims=True)
            return 0

        lax.fori_loop(part * per_block, (part + 1) * per_block, ends, 0, unroll=2)

    def walk(now, both):
        state, carry = both
        at = pl.ds(now, lanes, stride=LANE)
        back = pl.ds(LANE - 1 - now, lanes, stride=LANE)
        state = state + gain_ref[at, :] * mul(state, drift_w) + resid_ref[at, :]
        path_ref[at, :] = guess_ref[at, :] + state
        adjoint = source_ref[back, :] + carry
        scaled = gain_back_ref[back, :] * adjoint
        pre_ref[back, :] = scaled
        return state, adjoint + mul_t(scaled, drift_wt)

    lax.fori_loop(0, LANE, walk, (state_ref[...], carry_ref[...]), unroll=2)
    path_copy = pltpu.make_async_copy(path_ref, path_out, sems.at[1])
    path_copy.start()

    pre_high, pre_low = split(pre_ref[...])
    pre_w = jnp.concatenate([pre_high, pre_low], axis=1)
    sums = halves(jnp.dot(high_ref[...], pre_w, preferred_element_type=F32)) + jnp.dot(
        low_ref[...], pre_high, preferred_element_type=F32
    )
    recur = sums[:hidden]
    for s in range(seqs):
        recur = recur + column(edges[s], unit) * pre_ref[pl.ds(s * count, 1), :]
    recur = recur.T - recur
    half = hidden // 2
    grads_ref[pl.ds(0, half), :] = fold(recur)
    grads_ref[pl.ds(half, sums.shape[0] - hidden), :] = sums[hidden:]
    path_copy.wait()


def finish_kernel(mine_ref, other_ref, recur_ref, in_ref):
    hidden = recur_ref.shape[0]
    half = hidden // 2
    odd = lax.axis_index("batch") & 1 == 1
    mine, other = mine_ref[...], other_ref[...]
    whole = jnp.concatenate([jnp.where(odd, other, mine), jnp.where(odd, mine, other)], axis=0)
    in_ref[...] = whole[half:]
    upper = unfold(whole[:half])
    recur_ref[...] = upper - upper.T


def call(kernel, shapes, in_specs, scratch=(), flops=0, room=14):
    out_shapes = [jax.ShapeDtypeStruct(s, F32) if isinstance(s, tuple) else s for s in shapes]
    run = pl.pallas_call(
        kernel,
        out_shape=out_shapes,
        in_specs=in_specs,
        out_specs=[
            HBM if getattr(s, "memory_space", None) == pltpu.HBM else VMEM for s in out_shapes
        ],
        scratch_shapes=[pltpu.VMEM(s, F32) if isinstance(s, tuple) else s for s in scratch],
        compiler_params=pltpu.CompilerParams(vmem_limit_bytes=room * MIB),
        cost_estimate=pl.CostEstimate(flops=flops, bytes_accessed=1 << 20, transcendentals=0),
    )

    def pinned(*operands):
        return run(*[
            pltpu.with_memory_space_constraint(x, pltpu.HBM) if spec is HBM else x
            for x, spec in zip(operands, in_specs, strict=True)
        ])

    return pinned


def swapped(value, axis, distance):
    return lax.ppermute(value, axis, [(i, i ^ distance) for i in range(lax.axis_size(axis))])


def levels_of(axis):
    return lax.axis_size(axis).bit_length() - 1


def on_device(
    inputs, guess_path, recur_weight, damping, in_weight, bias_term, targets, target_steps
):
    seqs, count, hidden = guess_path.shape
    blocks = targets.shape[1]
    features = inputs.shape[2]
    rows = seqs * count
    lanes = rows // LANE
    chunks = lanes // seqs
    hits = seqs * blocks
    total_seqs = seqs * lax.axis_size("batch")
    x = inputs.reshape(rows, features)
    guess = guess_path.reshape(rows, hidden)
    keep = rows * hidden * hidden * 4 <= KEEP
    depth = LANE if keep else 1

    message, maps, before, start, hit, reach, reach_off, gain, resid, drift = call(
        functools.partial(compose_kernel, seqs, blocks, total_seqs, keep),
        [
            near((seqs, hidden + hidden // 2 + 8, hidden)),
            far((lanes, hidden, hidden)),
            far((lanes, hidden, hidden)),
            (lanes, hidden),
            (hits, hidden, hidden),
            (hits, hidden, hidden),
            (hits, hidden),
            (rows, hidden),
            (rows, hidden),
            (hidden, hidden),
        ],
        [HBM] * 8,
        [
            (depth, lanes if keep else 1, hidden, hidden),
            (depth, lanes if keep else 1, hidden),
            (lanes, hidden, hidden),
            (lanes, hidden, hidden),
            (lanes, hidden),
            (hits, hidden),
            (rows, hidden),
            pltpu.SMEM((seqs, blocks), jnp.int32),
            (rows, features),
            (rows, hidden),
            (hidden, hidden),
            (1, hidden),
            (features, hidden),
            (1, hidden),
            (hits, hidden),
            pltpu.SemaphoreType.DMA((10,)),
        ],
        room=ROOM,
    )(target_steps, x, guess, recur_weight, damping.reshape(1, hidden), in_weight,
      bias_term.reshape(1, hidden), targets.reshape(hits, hidden))

    home, pull, ready = call(
        functools.partial(prepare_kernel, seqs, blocks),
        [far((lanes, hidden, hidden)), far((hits, chunks, hidden, hidden)), (8, hidden)],
        [HBM, HBM, VMEM],
        [
            (lanes, hidden, hidden),
            (hits, chunks, hidden, hidden),
            pltpu.SMEM((seqs, blocks), jnp.int32),
            (lanes, hidden, hidden),
            pltpu.SemaphoreType.DMA((2,)),
            pltpu.SemaphoreType.DMA((seqs * blocks * (blocks + 3) // 2,)),
        ],
        flops=1 << 32,
        room=20,
    )(target_steps, maps, hit)

    levels = levels_of("seq")
    groups, received = [message], []
    for level in range(levels - 1):
        received.append(swapped(groups[-1], "seq", 1 << level))
        if level == 1:
            high, low, ready = call(
                functools.partial(factors_kernel, seqs),
                [
                    jax.ShapeDtypeStruct((hidden + features, rows), BF16),
                    jax.ShapeDtypeStruct((hidden + features, rows), BF16),
                    (8, hidden),
                ],
                [HBM, HBM, VMEM],
                [(rows, hidden), (rows, features), (rows, hidden), pltpu.SemaphoreType.DMA((2,))],
                flops=1 << 31,
            )(x, guess, groups[1])
        with_map = level < levels - 2
        height = (hidden if with_map else 0) + hidden // 2 + 8
        groups += call(
            functools.partial(join_kernel, level, with_map),
            [(seqs, height, hidden)],
            [VMEM, VMEM, VMEM, VMEM],
        )(drift, groups[-1], received[-1], ready)
    other = swapped(groups[-1], "seq", 1 << (levels - 1))
    square = (seqs, hidden, hidden)
    entry, tail, back, sides = call(
        functools.partial(sides_kernel, levels - 1),
        [square, square, square, (8 * seqs, hidden)],
        [VMEM] * (2 * levels - 1),
        flops=1 << 30,
    )(drift, *groups[:-1], *received)

    path, grads = call(
        functools.partial(solve_kernel, seqs, blocks, total_seqs, levels - 1),
        [far((rows, hidden)), near((hidden // 2 + features, hidden))],
        [HBM] + [VMEM] * 3 + [HBM] * 2 + [VMEM] * 13,
        [(lanes, hidden)] * 2 + [(rows, hidden)] * 4 + [
            (lanes, hidden, hidden),
            (hits, chunks, hidden, hidden),
            pltpu.SMEM((seqs, blocks), jnp.int32),
            pltpu.SemaphoreType.DMA((2 + seqs * blocks * (blocks + 3) // 2,)),
        ],
    )(target_steps, drift, groups[-1], other, home, pull, entry, tail, back, sides, before, start,
      reach, reach_off, gain, resid, guess, high, low)

    middle = grads.shape[0] // 2
    odd = lax.axis_index("batch") & 1 == 1
    kept = jnp.where(odd, grads[middle:], grads[:middle])
    given = jnp.where(odd, grads[:middle], grads[middle:])
    kept = kept + swapped(given, "batch", 1)
    width = lax.axis_size("batch")
    hops = [(0, 1 << k) for k in range(1, levels_of("batch"))] + [(1 << k, 0) for k in range(levels)]
    for stage in range(len(hops)):
        route = []
        for i in range(lax.axis_size("seq")):
            for j in range(width):
                along_seq, along_batch = hops[(stage + (j & 1) * (len(hops) // 2)) % len(hops)]
                route.append((i * width + j, (i ^ along_seq) * width + (j ^ along_batch)))
        kept = kept + lax.ppermute(kept, ("seq", "batch"), route)
    grad_recur, grad_in = call(
        finish_kernel,
        [(hidden, hidden), (features, hidden)],
        [VMEM, VMEM],
    )(kept, swapped(kept, "batch", 1))
    return (path.reshape(seqs, count, hidden), grad_recur, grad_in)


def solution(mesh):
    placed = (
        P("batch", "seq", None),
        P("batch", "seq", None),
        P(),
        P(),
        P(),
        P(),
        P("batch", "seq", None),
        P("batch", "seq"),
    )
    return jax.shard_map(
        on_device,
        mesh=mesh,
        in_specs=placed,
        out_specs=(P("batch", "seq", None), P(), P()),
        check_vma=False,
    )
```

```python
import functools

import jax
import jax.numpy as jnp
from jax import lax
from jax.experimental import pallas as pl
from jax.experimental.pallas import tpu as pltpu
from jax.sharding import PartitionSpec as P

LANE = 16
MIB = 1 << 20
UNROLL = 5
ROOM = 41
KEEP = 36 * MIB
F32 = jnp.float32
BF16 = jnp.bfloat16
VMEM = pl.BlockSpec(memory_space=pltpu.VMEM)
HBM = pl.BlockSpec(memory_space=pltpu.HBM)


def far(shape):
    return pltpu.HBM(shape, F32)


def near(shape):
    return pltpu.VMEM(shape, F32)


euler_step = 0.02


def split(value):
    high = value.astype(BF16)
    return high, (value - high.astype(F32)).astype(BF16)


def left(value):
    return jnp.concatenate(split(value), axis=1)


def right(weight):
    row = jnp.concatenate(split(weight), axis=1)
    return jnp.concatenate([row, row], axis=0)


def right_t(weight):
    high, low = split(weight)
    return jnp.concatenate(
        [jnp.concatenate([high, high], axis=1), jnp.concatenate([low, low], axis=1)], axis=0
    )


def halves(wide):
    hidden = wide.shape[1] // 2
    return wide[:, :hidden] + wide[:, hidden:]


def mul(x, packed):
    return halves(jnp.dot(left(x), packed, preferred_element_type=F32))


def mul_t(x, packed):
    return halves(
        lax.dot_general(left(x), packed, (((1,), (1,)), ((), ())), preferred_element_type=F32)
    )


def mm(x, weight):
    return mul(x, right(weight))


def mm_t(x, weight):
    return mul_t(x, right_t(weight))


def eight(row):
    return jnp.broadcast_to(row, (8, row.shape[1]))


def identity(hidden):
    rows = lax.broadcasted_iota(jnp.int32, (hidden, hidden), 0)
    return (rows == lax.broadcasted_iota(jnp.int32, (hidden, hidden), 1)).astype(F32)


def drift_t(recur_ref, damping_ref):
    weight = recur_ref[...]
    return weight.T - weight - identity(weight.shape[0]) * damping_ref[...]


def column(row, unit):
    return jnp.broadcast_to(jnp.sum(unit * row, axis=1, keepdims=True), unit.shape)


def along(col, weight):
    return jnp.sum(col * weight, axis=0, keepdims=True)


OFFSET, ADJOINT, DRIVE, FIRST, LAST, DIAGONAL = range(6)


def triangles(half):
    row = lax.broadcasted_iota(jnp.int32, (half, half), 0)
    col = lax.broadcasted_iota(jnp.int32, (half, half), 1)
    return col > row, col < row


def fold(whole):
    half = whole.shape[0] // 2
    above, _ = triangles(half)
    return jnp.concatenate(
        [jnp.where(above, whole[:half, :half], whole[half:, half:]), whole[:half, half:]], axis=1
    )


def unfold(folded):
    half = folded.shape[0]
    above, below = triangles(half)
    both = folded[:, :half]
    upper = jnp.concatenate([jnp.where(above, both, 0.0), folded[:, half:]], axis=1)
    lower = jnp.concatenate([jnp.zeros((half, half), F32), jnp.where(below, both, 0.0)], axis=1)
    return jnp.concatenate([upper, lower], axis=0)


def vectors(*rows):
    hidden = rows[0].shape[1]
    blank = jnp.zeros((8 - len(rows), hidden), F32)
    return jnp.concatenate([row[:1] for row in rows] + [blank], axis=0)


def compose_kernel(
    seqs, blocks, total_seqs, keep, steps_in, x_in, guess_in, recur_in, damping_in, in_in, bias_in,
    targets_in,
    message_ref, maps_ref, before_out, start_ref, hit_out, reach_ref, reach_off_ref, gain_ref,
    resid_ref, drift_ref,
    record_ref, record_off_ref, before_ref, off_ref, hit_ref, hit_off_ref, prev_ref,
    steps_ref, x_ref, guess_ref, recur_ref, damping_ref, in_ref, bias_ref, targets_ref, sems,
):
    fetches = [
        pltpu.make_async_copy(source, to, sems.at[i])
        for i, (source, to) in enumerate([
            (recur_in, recur_ref), (damping_in, damping_ref), (guess_in, guess_ref), (x_in, x_ref),
            (in_in, in_ref), (bias_in, bias_ref), (targets_in, targets_ref), (steps_in, steps_ref),
        ])
    ]
    for fetch in fetches:
        fetch.start()
    for fetch in fetches[:3]:
        fetch.wait()
    rows, hidden = guess_ref.shape
    count = rows // seqs
    chunks = count // LANE
    lanes = seqs * chunks
    block = count // blocks
    drift = drift_t(recur_ref, damping_ref)
    drift_ref[...] = drift
    drift_w = right(drift)

    guess = guess_ref[...]
    prev_ref[pl.ds(1, rows - 1), :] = guess_ref[pl.ds(0, rows - 1), :]
    for s in range(seqs):
        prev_ref[pl.ds(s * count, 1), :] = jnp.zeros((1, hidden), F32)
    prev = prev_ref[...]
    for fetch in fetches[3:]:
        fetch.wait()
    x_high, x_low = split(x_ref[...])
    in_w = jnp.concatenate(split(in_ref[...]), axis=1)
    drive = bias_ref[...] + halves(
        jnp.dot(x_high, in_w, preferred_element_type=F32)
        + jnp.dot(x_low, in_w, preferred_element_type=F32)
    )
    activation = jnp.tanh(mul(prev, drift_w) + drive)
    gain_ref[...] = euler_step * (1.0 - activation * activation)
    resid_ref[...] = prev + euler_step * activation - guess
    own = (lax.axis_index("seq") == 0).astype(F32)
    for s in range(seqs):
        edge = pl.ds(s * count, 1)
        gain_ref[edge, :] = gain_ref[edge, :] * own
        resid_ref[edge, :] = resid_ref[edge, :] * own

    unit = identity(hidden)
    for lane in range(lanes):
        first = unit + drift * gain_ref[pl.ds(lane * LANE, 1), :]
        maps_ref[lane] = first
        if keep:
            record_ref[0, lane] = first
    off_ref[...] = resid_ref[pl.ds(0, lanes, stride=LANE), :]
    if keep:
        record_off_ref[0] = off_ref[...]

    def place(j):
        step = (j % blocks) * block + steps_ref[j // blocks, j % blocks]
        return (j // blocks) * chunks + step // LANE, step % LANE, (j // blocks) * count + step

    def capture(now):
        for j in range(seqs * blocks):
            lane, at, _ = place(j)

            @pl.when(at == now)
            def _():
                hit_ref[j] = maps_ref[lane]
                hit_off_ref[pl.ds(j, 1), :] = off_ref[pl.ds(lane, 1), :]

    def advance(now, _):
        off = off_ref[...]
        off = (
            off
            + gain_ref[pl.ds(now, lanes, stride=LANE), :] * mul(off, drift_w)
            + resid_ref[pl.ds(now, lanes, stride=LANE), :]
        )
        off_ref[...] = off
        if keep:
            record_off_ref[now] = off
        for lane in range(0, lanes, 2):
            pair = maps_ref[lane : lane + 2].reshape(2 * hidden, hidden)
            moved = mul(pair, drift_w)
            for k in range(2):
                gain_now = gain_ref[pl.ds((lane + k) * LANE + now, 1), :]
                part = slice(k * hidden, (k + 1) * hidden)
                longer = pair[part] + gain_now * moved[part]
                maps_ref[lane + k] = longer
                if keep:
                    record_ref[now, lane + k] = longer
        if not keep:
            capture(now)
        return 0

    if keep:
        lax.fori_loop(1, LANE, advance, 0, unroll=UNROLL)
        for j in range(seqs * blocks):
            lane, at, _ = place(j)
            hit_ref[j] = record_ref[at, lane]
            hit_off_ref[pl.ds(j, 1), :] = record_off_ref[at, pl.ds(lane, 1), :]
    else:
        capture(0)
        lax.fori_loop(1, LANE, advance, 0)
    hit_copy = pltpu.make_async_copy(hit_ref, hit_out, sems.at[9])
    hit_copy.start()

    running = [unit] * seqs
    offset = [jnp.zeros((8, hidden), F32)] * seqs
    for chunk in range(chunks):
        for s in range(seqs):
            lane = s * chunks + chunk
            before_ref[lane] = running[s]
            start_ref[pl.ds(lane, 1), :] = offset[s][:1]
            this, this_off = maps_ref[lane], off_ref[pl.ds(lane, 1), :]
            if chunk == 0:
                running[s], offset[s] = this, eight(this_off)
            else:
                packed = right(this)
                running[s] = mul(running[s], packed)
                offset[s] = mul(offset[s], packed) + this_off
    before_copy = pltpu.make_async_copy(before_ref, before_out, sems.at[8])
    before_copy.start()

    for s in range(seqs):
        message_ref[s, pl.ds(0, hidden), :] = running[s]
        total = jnp.zeros((hidden, hidden), F32)
        total_off = jnp.zeros((8, hidden), F32)
        for k in range(blocks):
            j = s * blocks + k
            lane, _, row = place(j)
            packed = right(hit_ref[j])
            reach = mul(before_ref[lane], packed)
            reach_off = mul(eight(start_ref[pl.ds(lane, 1), :]), packed) + hit_off_ref[pl.ds(j, 1), :]
            reach_ref[j] = reach
            miss = reach_off + guess_ref[pl.ds(row, 1), :] - targets_ref[pl.ds(j, 1), :]
            reach_off_ref[pl.ds(j, 1), :] = miss[:1]
            reach_t = right_t(reach)
            total = total + mul_t(reach, reach_t)
            total_off = total_off + mul_t(miss, reach_t)
        total = total / total_seqs
        message_ref[s, pl.ds(hidden, hidden // 2), :] = fold(total)
        message_ref[s, pl.ds(hidden + hidden // 2, 8), :] = vectors(
            offset[s], total_off / total_seqs, drive[s * count : s * count + 1],
            guess_ref[pl.ds(s * count, 1), :], guess_ref[pl.ds((s + 1) * count - 1, 1), :],
            jnp.sum(unit * total, axis=0, keepdims=True),
        )
    before_copy.wait()
    hit_copy.wait()


def opened(ref, s, with_map=True):
    hidden = ref.shape[2]
    at = hidden if with_map else 0
    rows = [eight(ref[s, pl.ds(at + hidden // 2 + k, 1), :]) for k in range(5)]
    diagonal = ref[s, pl.ds(at + hidden // 2 + DIAGONAL, 1), :]
    half = unfold(ref[s, pl.ds(at, hidden // 2), :])
    curve = half + half.T + identity(hidden) * diagonal
    return (ref[s, pl.ds(0, hidden), :] if with_map else None, curve, rows)


def pick(flag, one, other):
    return jax.tree.map(lambda a, b: jnp.where(flag, a, b), one, other)


def crossing(last, drive, first, drift_w):
    activation = jnp.tanh(mul(last, drift_w) + drive)
    return euler_step * (1.0 - activation * activation), last + euler_step * activation - first


def join(one, two, drift_w, with_map=True):
    map_1, curve_1, rows_1 = one
    map_2, curve_2, rows_2 = two
    gain, resid = crossing(rows_1[LAST], rows_2[DRIVE], rows_2[FIRST], drift_w)
    map_1 = map_1 + mul(map_1, drift_w) * gain[:1]
    off_1 = rows_1[OFFSET] + mul(rows_1[OFFSET], drift_w) * gain + resid
    curve_w, map_w, map_1_t = right(curve_2), right(map_2), right_t(map_1)
    curve = curve_1 + mul_t(mul(map_1, curve_w), map_1_t)
    adjoint = rows_1[ADJOINT] + mul_t(mul(off_1, curve_w) + rows_2[ADJOINT], map_1_t)
    rows = [mul(off_1, map_w) + rows_2[OFFSET], adjoint, rows_1[DRIVE], rows_1[FIRST], rows_2[LAST]]
    return (mul(map_1, map_w) if with_map else None), curve, rows


def join_kernel(level, with_map, drift_ref, mine_ref, other_ref, _, out_ref):
    seqs, hidden = mine_ref.shape[0], mine_ref.shape[2]
    upper = (lax.axis_index("seq") >> level) & 1 == 1
    drift_w = right(drift_ref[...])
    for s in range(seqs):
        mine, other = opened(mine_ref, s), opened(other_ref, s)
        whole, curve, rows = join(pick(upper, other, mine), pick(upper, mine, other), drift_w, with_map)
        at = 0
        if with_map:
            out_ref[s, pl.ds(0, hidden), :] = whole
            at = hidden
        out_ref[s, pl.ds(at, hidden // 2), :] = fold(curve)
        diagonal = jnp.sum(identity(hidden) * curve, axis=0, keepdims=True)
        out_ref[s, pl.ds(at + hidden // 2, 8), :] = vectors(*rows, diagonal)


def sides_kernel(levels, drift_ref, *refs):
    mines, others = refs[:levels], refs[levels : 2 * levels]
    entry_ref, tail_ref, back_ref, rows_ref = refs[2 * levels :]
    seqs, hidden = entry_ref.shape[0], entry_ref.shape[1]
    drift_w = right(drift_ref[...])
    unit = identity(hidden)
    for s in range(seqs):
        zero = jnp.zeros((8, hidden), F32)
        lead, lead_off = unit, zero
        after = (unit, jnp.zeros((hidden, hidden), F32), [zero] * 5)
        edge, edge_gain = zero, zero
        place = lax.axis_index("seq")
        fresh = place >= 0
        for level in range(levels):
            upper = (place >> level) & 1 == 1
            mine, other = opened(mines[level], s), opened(others[level], s)
            gain, resid = crossing(other[2][LAST], mine[2][DRIVE], mine[2][FIRST], drift_w)
            far = other[0] + mul(other[0], drift_w) * gain[:1]
            far_off = other[2][OFFSET] + mul(other[2][OFFSET], drift_w) * gain + resid
            lead_w = right(lead)
            longer = (mul(far, lead_w), mul(far_off, lead_w) + lead_off)
            known = jnp.logical_and(upper, fresh)
            edge, edge_gain = pick(known, (other[2][LAST], gain), (edge, edge_gain))
            fresh = jnp.logical_and(fresh, jnp.logical_not(upper))
            after[2][LAST] = mine[2][LAST]
            extended = join(after, other, drift_w)
            lead, lead_off = pick(upper, longer, (lead, lead_off))
            after = pick(upper, after, extended)
        own_map, _, own_rows = opened(mines[0], s)
        own_w, curve_w = right(own_map), right(after[1])
        entry_ref[s] = lead
        tail_ref[s] = mul(mul(lead, own_w), curve_w)
        back_ref[s] = after[0].T
        leaving = mul(lead_off, own_w) + own_rows[OFFSET]
        tail_off = mul(leaving, curve_w) + after[2][ADJOINT]
        rows_ref[pl.ds(8 * s, 8), :] = vectors(lead_off, tail_off, edge, edge_gain)


def prepare_kernel(
    seq, blocks, steps_in, hit_in, maps_ref, _, home_ref, pull_ref, ready_ref, steps_ref, hit_ref, sems
):
    fetch_steps = pltpu.make_async_copy(steps_in, steps_ref, sems.at[0])
    fetch_hit = pltpu.make_async_copy(hit_in.at[pl.ds(seq * blocks, blocks)], hit_ref, sems.at[1])
    fetch_steps.start()
    fetch_hit.start()
    ready_ref[...] = jnp.zeros_like(ready_ref)
    chunks, hidden = home_ref.shape[:2]
    per_block = chunks // blocks
    unit = identity(hidden)
    home = unit
    pulls = [jnp.zeros((hidden, hidden), F32)] * blocks
    fetch_steps.wait()
    fetch_hit.wait()
    for chunk in reversed(range(chunks)):
        home_ref[chunk] = home
        active = [k for k in range(blocks) if chunk < (k + 1) * per_block]
        for k in active:
            pull_ref[k, chunk] = pulls[k]
        if chunk:
            stack = jnp.concatenate([home] + [pulls[k] for k in active], axis=0)
            stack = mul_t(stack, right_t(maps_ref[seq * chunks + chunk]))
            home = stack[:hidden]
            for i, k in enumerate(active):
                owner = (k * per_block * LANE + steps_ref[seq, k]) // LANE
                part = stack[(i + 1) * hidden : (i + 2) * hidden]
                pulls[k] = jnp.where(owner == chunk, hit_ref[k].T, part)


def factors_kernel(
    seqs, blocks, steps_in, x_in, guess_in, _, high_ref, low_ref, mark_ref, ready_ref,
    prev_ref, x_ref, guess_ref, steps_ref, sems,
):
    fetch_steps = pltpu.make_async_copy(steps_in, steps_ref, sems.at[2])
    fetch_steps.start()
    fetch_guess = pltpu.make_async_copy(guess_in, guess_ref, sems.at[0])
    fetch_x = pltpu.make_async_copy(x_in, x_ref, sems.at[1])
    fetch_guess.start()
    fetch_x.start()
    ready_ref[...] = jnp.zeros_like(ready_ref)
    rows, hidden = guess_ref.shape
    fetch_guess.wait()
    prev_ref[pl.ds(1, rows - 1), :] = guess_ref[pl.ds(0, rows - 1), :]
    for s in range(seqs):
        prev_ref[pl.ds(s * (rows // seqs), 1), :] = jnp.zeros((1, hidden), F32)
    high_ref[pl.ds(0, hidden), :], low_ref[pl.ds(0, hidden), :] = split(prev_ref[...].T)
    fetch_x.wait()
    rest = pl.ds(hidden, x_ref.shape[1])
    high_ref[rest, :], low_ref[rest, :] = split(x_ref[...].T)
    fetch_steps.wait()
    block = rows // (seqs * blocks)
    row = lax.broadcasted_iota(jnp.int32, (block, hidden), 0)
    for s in range(seqs):
        for k in range(blocks):
            mark_ref[pl.ds((s * blocks + k) * block, block), :] = (row == steps_ref[s, k]).astype(F32)


def ends_kernel(
    seqs, blocks, total_seqs, level, drift_ref, mine_ref, other_ref, *refs
):
    home_refs, pull_refs, refs = refs[:seqs], refs[seqs : 2 * seqs], refs[2 * seqs :]
    (
        entry_ref, tail_ref, back_ref, sides_ref, before_ref, start_ref, reach_ref, reach_off_ref,
        gain_ref, mark_ref,
        state_ref, carry_ref, source_ref, gain_back_ref, edge_ref,
    ) = refs
    rows, hidden = gain_ref.shape
    count = rows // seqs
    chunks = count // LANE
    block = count // blocks
    per_block = chunks // blocks
    place = lax.axis_index("seq")
    upper = (place >> level) & 1 == 1
    lowest = (place & ((1 << level) - 1)) == 0
    drift = drift_ref[...]
    drift_w = right(drift)
    drift_wt = right_t(drift)
    unit = identity(hidden)
    gain_back_ref[...] = gain_ref[...]

    entries, tails, sources = [], [], []
    for s in range(seqs):
        mine, other = opened(mine_ref, s, False), opened(other_ref, s, False)
        last, middle = pick(upper, (other[2][LAST], other[2][OFFSET]), (mine[2][LAST], mine[2][OFFSET]))
        drive, first = pick(upper, (mine[2][DRIVE], mine[2][FIRST]), (other[2][DRIVE], other[2][FIRST]))
        gain, resid = crossing(last, drive, first, drift_w)
        middle = middle + mul(middle, drift_w) * gain + resid
        middle_col = column(middle[:1], unit)
        row = along(middle_col, jnp.where(upper, entry_ref[s], other[1]))
        lead_off, tail_off, edge, edge_gain = [sides_ref[pl.ds(8 * s + k, 1), :] for k in range(4)]
        beyond = eight(row) + other[2][ADJOINT]
        beyond = beyond + mul_t(beyond * gain, drift_wt)
        entries.append(column(jnp.where(upper, row, 0.0) + lead_off, unit))
        tail = jnp.where(
            upper, along(middle_col, tail_ref[s]), along(column(beyond[:1], unit), back_ref[s])
        )
        tails.append(column(tail + tail_off, unit))
        known = jnp.logical_and(upper, lowest)
        edge = jnp.where(known, last[:1], edge)
        edge_ref[pl.ds(s, 1), :] = edge
        edge_gain = jnp.where(known, gain[:1], edge_gain)
        at = pl.ds(s * count, 1)
        gain_back_ref[at, :] = gain_ref[at, :] + edge_gain
        here = []
        for k in range(blocks):
            j = s * blocks + k
            miss = (along(entries[s], reach_ref[j]) + reach_off_ref[pl.ds(j, 1), :]) / total_seqs
            here_rows = pl.ds(j * block, block)
            source_ref[here_rows, :] = mark_ref[here_rows, :] * miss
            here.append(column(miss, unit))
        sources.append(here)

    for part in range(blocks):

        def ends(chunk, _):
            for s in range(seqs):
                lane = s * chunks + chunk
                state_ref[pl.ds(lane, 1), :] = along(entries[s], before_ref[lane]) + start_ref[pl.ds(lane, 1), :]
                sums = tails[s] * home_refs[s][chunk]
                for k in range(part, blocks):
                    sums = sums + sources[s][k] * pull_refs[s][k, chunk]
                carry_ref[pl.ds(lane, 1), :] = jnp.sum(sums, axis=0, keepdims=True)
            return 0

        lax.fori_loop(part * per_block, (part + 1) * per_block, ends, 0, unroll=2)


def walk_kernel(
    drift_ref, state_ref, carry_ref, source_ref, gain_ref, gain_back_ref, resid_ref, guess_ref,
    path_ref, pre_ref,
):
    lanes, hidden = state_ref.shape
    drift = drift_ref[...]

    def walks(ahead_ref, behind_ref):
        pltpu.matmul_push_rhs(right(drift), 0, 0)
        pltpu.matmul_push_rhs(right_t(drift), 0, 1, transpose=True)

        def walk(now, both, staged=None):
            state, carry = both
            at = pl.ds(now, lanes, stride=LANE)
            back = pl.ds(LANE - 1 - now, lanes, stride=LANE)
            adjoint = source_ref[back, :] + carry
            scaled = gain_back_ref[back, :] * adjoint
            pltpu.matmul_acc_lhs(ahead_ref, left(state), staged)
            pltpu.matmul_acc_lhs(behind_ref, left(scaled), staged)
            pre_ref[back, :] = scaled
            rest = state + resid_ref[at, :]
            state = rest + gain_ref[at, :] * halves(pltpu.matmul_pop(ahead_ref))
            path_ref[at, :] = guess_ref[at, :] + state
            return state, adjoint + halves(pltpu.matmul_pop(behind_ref))

        both = walk(0, (state_ref[...], carry_ref[...]), 0)
        lax.fori_loop(1, LANE, walk, both, unroll=3)

    wide = (lanes, 2 * hidden)
    pl.run_scoped(walks, pltpu.ACC(0)(wide, F32), pltpu.ACC(1)(wide, F32))


def gradients_kernel(edge_ref, pre_ref, high_ref, low_ref, grads_ref):
    rows, hidden = pre_ref.shape
    seqs = edge_ref.shape[0]
    count = rows // seqs
    unit = identity(hidden)
    pre_high, pre_low = split(pre_ref[...])
    pre_w = jnp.concatenate([pre_high, pre_low], axis=1)
    sums = halves(jnp.dot(high_ref[...], pre_w, preferred_element_type=F32)) + jnp.dot(
        low_ref[...], pre_high, preferred_element_type=F32
    )
    recur = sums[:hidden]
    for s in range(seqs):
        recur = recur + column(edge_ref[pl.ds(s, 1), :], unit) * pre_ref[pl.ds(s * count, 1), :]
    recur = recur.T - recur
    half = hidden // 2
    grads_ref[pl.ds(0, half), :] = fold(recur)
    grads_ref[pl.ds(half, sums.shape[0] - hidden), :] = sums[hidden:]


def finish_kernel(mine_ref, other_ref, recur_ref, in_ref):
    hidden = recur_ref.shape[0]
    half = hidden // 2
    odd = lax.axis_index("batch") & 1 == 1
    mine, other = mine_ref[...], other_ref[...]
    whole = jnp.concatenate([jnp.where(odd, other, mine), jnp.where(odd, mine, other)], axis=0)
    in_ref[...] = whole[half:]
    upper = unfold(whole[:half])
    recur_ref[...] = upper - upper.T


def call(kernel, shapes, in_specs, scratch=(), flops=0, room=14):
    out_shapes = [jax.ShapeDtypeStruct(s, F32) if isinstance(s, tuple) else s for s in shapes]
    run = pl.pallas_call(
        kernel,
        out_shape=out_shapes,
        in_specs=in_specs,
        out_specs=[
            HBM if getattr(s, "memory_space", None) == pltpu.HBM else VMEM for s in out_shapes
        ],
        scratch_shapes=[pltpu.VMEM(s, F32) if isinstance(s, tuple) else s for s in scratch],
        compiler_params=pltpu.CompilerParams(vmem_limit_bytes=room * MIB),
        cost_estimate=pl.CostEstimate(flops=flops, bytes_accessed=1 << 20, transcendentals=0),
    )

    def pinned(*operands):
        return run(*[
            pltpu.with_memory_space_constraint(x, pltpu.HBM) if spec is HBM else x
            for x, spec in zip(operands, in_specs, strict=True)
        ])

    return pinned


def swapped(value, axis, distance):
    return lax.ppermute(value, axis, [(i, i ^ distance) for i in range(lax.axis_size(axis))])


def levels_of(axis):
    return lax.axis_size(axis).bit_length() - 1


def on_device(
    inputs, guess_path, recur_weight, damping, in_weight, bias_term, targets, target_steps
):
    seqs, count, hidden = guess_path.shape
    blocks = targets.shape[1]
    features = inputs.shape[2]
    rows = seqs * count
    lanes = rows // LANE
    chunks = lanes // seqs
    hits = seqs * blocks
    total_seqs = seqs * lax.axis_size("batch")
    x = inputs.reshape(rows, features)
    guess = guess_path.reshape(rows, hidden)
    keep = rows * hidden * hidden * 4 <= KEEP
    depth = LANE if keep else 1

    message, maps, before, start, hit, reach, reach_off, gain, resid, drift = call(
        functools.partial(compose_kernel, seqs, blocks, total_seqs, keep),
        [
            near((seqs, hidden + hidden // 2 + 8, hidden)),
            near((lanes, hidden, hidden)),
            far((lanes, hidden, hidden)),
            (lanes, hidden),
            far((hits, hidden, hidden)),
            near((hits, hidden, hidden)),
            (hits, hidden),
            (rows, hidden),
            (rows, hidden),
            (hidden, hidden),
        ],
        [HBM] * 8,
        [
            (depth, lanes if keep else 1, hidden, hidden),
            (depth, lanes if keep else 1, hidden),
            (lanes, hidden, hidden),
            (lanes, hidden),
            (hits, hidden, hidden),
            (hits, hidden),
            (rows, hidden),
            pltpu.SMEM((seqs, blocks), jnp.int32),
            (rows, features),
            (rows, hidden),
            (hidden, hidden),
            (1, hidden),
            (features, hidden),
            (1, hidden),
            (hits, hidden),
            pltpu.SemaphoreType.DMA((10,)),
        ],
        room=ROOM,
    )(target_steps, x, guess, recur_weight, damping.reshape(1, hidden), in_weight,
      bias_term.reshape(1, hidden), targets.reshape(hits, hidden))

    def prepare(seq, gate):
        return call(
            functools.partial(prepare_kernel, seq, blocks),
            [
                near((chunks, hidden, hidden)),
                near((blocks, chunks, hidden, hidden)),
                (8, hidden),
            ],
            [HBM, HBM, VMEM, VMEM],
            [
                pltpu.SMEM((seqs, blocks), jnp.int32),
                (blocks, hidden, hidden),
                pltpu.SemaphoreType.DMA((2,)),
            ],
            flops=1 << 32,
        )(target_steps, hit, maps, gate)

    prepared = [prepare(0, drift)]
    ready = prepared[0][2]
    levels = levels_of("seq")
    groups, received = [message], []
    for level in range(levels - 1):
        received.append(swapped(groups[-1], "seq", 1 << level))
        if level == 1:
            prepared += [prepare(s, groups[1]) for s in range(1, seqs)]
            high, low, mark, ready = call(
                functools.partial(factors_kernel, seqs, blocks),
                [
                    jax.ShapeDtypeStruct((hidden + features, rows), BF16),
                    jax.ShapeDtypeStruct((hidden + features, rows), BF16),
                    near((rows, hidden)),
                    (8, hidden),
                ],
                [HBM, HBM, HBM, VMEM],
                [
                    (rows, hidden),
                    (rows, features),
                    (rows, hidden),
                    pltpu.SMEM((seqs, blocks), jnp.int32),
                    pltpu.SemaphoreType.DMA((3,)),
                ],
                flops=1 << 31,
            )(target_steps, x, guess, prepared[-1][2])
        with_map = level < levels - 2
        height = (hidden if with_map else 0) + hidden // 2 + 8
        groups += call(
            functools.partial(join_kernel, level, with_map),
            [(seqs, height, hidden)],
            [VMEM, VMEM, VMEM, VMEM],
        )(drift, groups[-1], received[-1], ready)
    other = swapped(groups[-1], "seq", 1 << (levels - 1))
    square = (seqs, hidden, hidden)
    entry, tail, back, sides = call(
        functools.partial(sides_kernel, levels - 1),
        [square, square, square, (8 * seqs, hidden)],
        [VMEM] * (2 * levels - 1),
        flops=1 << 30,
    )(drift, *groups[:-1], *received)

    state, carry, source, gain_back, edge = call(
        functools.partial(ends_kernel, seqs, blocks, total_seqs, levels - 1),
        [
            near((lanes, hidden)),
            near((lanes, hidden)),
            near((rows, hidden)),
            near((rows, hidden)),
            near((seqs, hidden)),
        ],
        [VMEM] * (13 + 2 * seqs),
    )(drift, groups[-1], other, *[p[0] for p in prepared],
      *[p[1] for p in prepared], entry, tail, back, sides, before, start, reach, reach_off, gain, mark)
    path, pre = call(
        walk_kernel,
        [near((rows, hidden)), near((rows, hidden))],
        [VMEM] * 8,
    )(drift, state, carry, source, gain, gain_back, resid, guess)
    (grads,) = call(
        gradients_kernel, [near((hidden // 2 + features, hidden))], [VMEM] * 4
    )(edge, pre, high, low)

    middle = grads.shape[0] // 2
    odd = lax.axis_index("batch") & 1 == 1
    kept = jnp.where(odd, grads[middle:], grads[:middle])
    given = jnp.where(odd, grads[:middle], grads[middle:])
    kept = kept + swapped(given, "batch", 1)
    width = lax.axis_size("batch")
    hops = [(0, 1 << k) for k in range(1, levels_of("batch"))] + [(1 << k, 0) for k in range(levels)]
    for stage in range(len(hops)):
        route = []
        for i in range(lax.axis_size("seq")):
            for j in range(width):
                along_seq, along_batch = hops[(stage + (j & 1) * (len(hops) // 2)) % len(hops)]
                route.append((i * width + j, (i ^ along_seq) * width + (j ^ along_batch)))
        kept = kept + lax.ppermute(kept, ("seq", "batch"), route)
    grad_recur, grad_in = call(
        finish_kernel,
        [(hidden, hidden), (features, hidden)],
        [VMEM, VMEM],
    )(kept, swapped(kept, "batch", 1))
    return (path.reshape(seqs, count, hidden), grad_recur, grad_in)


def solution(mesh):
    placed = (
        P("batch", "seq", None),
        P("batch", "seq", None),
        P(),
        P(),
        P(),
        P(),
        P("batch", "seq", None),
        P("batch", "seq"),
    )
    return jax.shard_map(
        on_device,
        mesh=mesh,
        in_specs=placed,
        out_specs=(P("batch", "seq", None), P(), P()),
        check_vma=False,
    )
```

```python
import functools

import jax
import jax.numpy as jnp
from jax import lax
from jax.experimental import pallas as pl
from jax.experimental.pallas import tpu as pltpu
from jax.sharding import PartitionSpec as P

LANE = 16
MIB = 1 << 20
UNROLL = 7
RUN = 4
ROOM = 40
KEEP = 36 * MIB
F32 = jnp.float32
BF16 = jnp.bfloat16
VMEM = pl.BlockSpec(memory_space=pltpu.VMEM)
HBM = pl.BlockSpec(memory_space=pltpu.HBM)


def far(shape):
    return pltpu.HBM(shape, F32)


def near(shape):
    return pltpu.VMEM(shape, F32)


euler_step = 0.02


def split(value):
    high = value.astype(BF16)
    return high, (value - high.astype(F32)).astype(BF16)


def left(value):
    return jnp.concatenate(split(value), axis=1)


def right(weight):
    row = jnp.concatenate(split(weight), axis=1)
    return jnp.concatenate([row, row], axis=0)


def right_t(weight):
    high, low = split(weight)
    return jnp.concatenate(
        [jnp.concatenate([high, high], axis=1), jnp.concatenate([low, low], axis=1)], axis=0
    )


def halves(wide):
    hidden = wide.shape[1] // 2
    return wide[:, :hidden] + wide[:, hidden:]


def mul(x, packed):
    return halves(jnp.dot(left(x), packed, preferred_element_type=F32))


def mul_t(x, packed):
    return halves(
        lax.dot_general(left(x), packed, (((1,), (1,)), ((), ())), preferred_element_type=F32)
    )


def mm(x, weight):
    return mul(x, right(weight))


def mm_t(x, weight):
    return mul_t(x, right_t(weight))


def eight(row):
    return jnp.broadcast_to(row, (8, row.shape[1]))


def identity(hidden):
    rows = lax.broadcasted_iota(jnp.int32, (hidden, hidden), 0)
    return (rows == lax.broadcasted_iota(jnp.int32, (hidden, hidden), 1)).astype(F32)


def drift_t(recur_ref, damping_ref):
    weight = recur_ref[...]
    return weight.T - weight - identity(weight.shape[0]) * damping_ref[...]


def column(row, unit):
    return jnp.broadcast_to(jnp.sum(unit * row, axis=1, keepdims=True), unit.shape)


def along(col, weight):
    return jnp.sum(col * weight, axis=0, keepdims=True)


OFFSET, ADJOINT, DRIVE, FIRST, LAST, MOVED, DIAGONAL = range(7)


def triangles(half):
    row = lax.broadcasted_iota(jnp.int32, (half, half), 0)
    col = lax.broadcasted_iota(jnp.int32, (half, half), 1)
    return col > row, col < row


def fold(whole):
    half = whole.shape[0] // 2
    above, _ = triangles(half)
    return jnp.concatenate(
        [jnp.where(above, whole[:half, :half], whole[half:, half:]), whole[:half, half:]], axis=1
    )


def unfold(folded):
    half = folded.shape[0]
    above, below = triangles(half)
    both = folded[:, :half]
    upper = jnp.concatenate([jnp.where(above, both, 0.0), folded[:, half:]], axis=1)
    lower = jnp.concatenate([jnp.zeros((half, half), F32), jnp.where(below, both, 0.0)], axis=1)
    return jnp.concatenate([upper, lower], axis=0)


def vectors(*rows):
    hidden = rows[0].shape[1]
    blank = jnp.zeros((8 - len(rows), hidden), F32)
    return jnp.concatenate([row[:1] for row in rows] + [blank], axis=0)


def compose_kernel(
    seqs, blocks, total_seqs, keep, steps_in, x_in, guess_in, recur_in, damping_in, in_in, bias_in,
    targets_in,
    message_ref, maps_ref, before_out, start_ref, lead_ref, lead_off_ref, hit_out, reach_ref,
    reach_off_ref, gain_out, resid_out, drift_ref,
    gain_ref, resid_ref, record_ref, record_off_ref, before_ref, off_ref, hit_ref, hit_off_ref, prev_ref,
    steps_ref, x_ref, guess_ref, recur_ref, damping_ref, in_ref, bias_ref, targets_ref, sems,
):
    fetches = [
        pltpu.make_async_copy(source, to, sems.at[i])
        for i, (source, to) in enumerate([
            (recur_in, recur_ref), (damping_in, damping_ref), (guess_in, guess_ref), (x_in, x_ref),
            (in_in, in_ref), (bias_in, bias_ref), (targets_in, targets_ref), (steps_in, steps_ref),
        ])
    ]
    for fetch in fetches:
        fetch.start()
    for fetch in fetches[:3]:
        fetch.wait()
    rows, hidden = guess_ref.shape
    count = rows // seqs
    chunks = count // LANE
    lanes = seqs * chunks
    block = count // blocks
    per_block = chunks // blocks
    drift = drift_t(recur_ref, damping_ref)
    drift_ref[...] = drift
    drift_w = right(drift)
    for s in range(seqs):
        last = guess_ref[pl.ds((s + 1) * count - 1, 1), :]
        message_ref[s, pl.ds(hidden + hidden // 2 + LAST, 1), :] = last
        message_ref[s, pl.ds(hidden + hidden // 2 + MOVED, 1), :] = mul(eight(last), drift_w)[:1]
    prev_ref[pl.ds(1, rows - 1), :] = guess_ref[pl.ds(0, rows - 1), :]
    for s in range(seqs):
        prev_ref[pl.ds(s * count, 1), :] = jnp.zeros((1, hidden), F32)
    for fetch in fetches[3:]:
        fetch.wait()
    in_w = jnp.concatenate(split(in_ref[...]), axis=1)

    for top in range(0, rows, block):
        part = pl.ds(top, block)
        x_high, x_low = split(x_ref[part, :])
        drive = bias_ref[...] + halves(
            jnp.dot(x_high, in_w, preferred_element_type=F32)
            + jnp.dot(x_low, in_w, preferred_element_type=F32)
        )
        prev = prev_ref[part, :]
        activation = jnp.tanh(mul(prev, drift_w) + drive)
        gain_ref[part, :] = euler_step * (1.0 - activation * activation)
        resid_ref[part, :] = prev + euler_step * activation - guess_ref[part, :]
        if top % count == 0:
            own = (lax.axis_index("seq") == 0).astype(F32)
            edge = pl.ds(top, 1)
            gain_ref[edge, :] = gain_ref[edge, :] * own
            resid_ref[edge, :] = resid_ref[edge, :] * own
            message_ref[top // count, pl.ds(hidden + hidden // 2 + DRIVE, 1), :] = drive[:1]

    sends = [
        pltpu.make_async_copy(gain_ref, gain_out, sems.at[9]),
        pltpu.make_async_copy(resid_ref, resid_out, sems.at[10]),
    ]
    for send in sends:
        send.start()
    unit = identity(hidden)

    def place(j):
        step = (j % blocks) * block + steps_ref[j // blocks, j % blocks]
        return (j // blocks) * chunks + step // LANE, step % LANE, (j // blocks) * count + step

    def opening(lane):
        return unit + drift * gain_ref[pl.ds(lane * LANE, 1), :]

    def capture(now):
        for j in range(seqs * blocks):
            lane, at, _ = place(j)

            @pl.when(at == now)
            def _():
                hit_ref[j] = maps_ref[lane]
                hit_off_ref[pl.ds(j, 1), :] = off_ref[pl.ds(lane, 1), :]

    def advance(now, _, opened_here=False):
        off = off_ref[...]
        off = (
            off
            + gain_ref[pl.ds(now, lanes, stride=LANE), :] * mul(off, drift_w)
            + resid_ref[pl.ds(now, lanes, stride=LANE), :]
        )
        off_ref[...] = off
        if keep:
            record_off_ref[now] = off
        for lane in range(0, lanes, 2):
            if opened_here:
                pair = jnp.concatenate([opening(lane), opening(lane + 1)], axis=0)
            else:
                pair = maps_ref[lane : lane + 2].reshape(2 * hidden, hidden)
            moved = mul(pair, drift_w)
            for k in range(2):
                gain_now = gain_ref[pl.ds((lane + k) * LANE + now, 1), :]
                part = slice(k * hidden, (k + 1) * hidden)
                longer = pair[part] + gain_now * moved[part]
                maps_ref[lane + k] = longer
                if keep:
                    record_ref[now, lane + k] = longer
        if not keep:
            capture(now)
        return 0

    off_ref[...] = resid_ref[pl.ds(0, lanes, stride=LANE), :]
    if keep:
        record_off_ref[0] = off_ref[...]
        advance(1, 0, True)
        lax.fori_loop(2, LANE, advance, 0, unroll=UNROLL)
        for j in range(seqs * blocks):
            lane, at, _ = place(j)
            hit_ref[j] = jnp.where(at == 0, opening(lane), record_ref[jnp.maximum(at, 1), lane])
            hit_off_ref[pl.ds(j, 1), :] = record_off_ref[at, pl.ds(lane, 1), :]
    else:
        for lane in range(lanes):
            maps_ref[lane] = opening(lane)
        capture(0)
        lax.fori_loop(1, LANE, advance, 0)
    hit_copy = pltpu.make_async_copy(hit_ref, hit_out, sems.at[8])
    hit_copy.start()

    hits = seqs * blocks
    running = [None] * hits
    offset = [None] * hits
    for chunk in range(per_block):
        for j in range(hits):
            lane = j * per_block + chunk
            this, this_off = maps_ref[lane], off_ref[pl.ds(lane, 1), :]
            if chunk == 0:
                before_ref[lane] = unit
                start_ref[pl.ds(lane, 1), :] = jnp.zeros((1, hidden), F32)
                running[j], offset[j] = this, eight(this_off)
            else:
                before_ref[lane] = running[j]
                start_ref[pl.ds(lane, 1), :] = offset[j][:1]
                packed = right(this)
                running[j] = mul(running[j], packed)
                offset[j] = mul(offset[j], packed) + this_off
            if (chunk + 1) % RUN == 0:
                run = pl.ds(lane + 1 - RUN, RUN)
                sends.append(
                    pltpu.make_async_copy(before_ref.at[run], before_out.at[run], sems.at[9 + len(sends)])
                )
                sends[-1].start()

    for s in range(seqs):
        lead, lead_off = None, None
        total = jnp.zeros((hidden, hidden), F32)
        total_off = jnp.zeros((8, hidden), F32)
        for k in range(blocks):
            j = s * blocks + k
            lane, _, row = place(j)
            packed = right(hit_ref[j])
            reach = mul(before_ref[lane], packed)
            reach_off = mul(eight(start_ref[pl.ds(lane, 1), :]), packed) + hit_off_ref[pl.ds(j, 1), :]
            if k:
                lead_ref[j] = lead
                lead_off_ref[pl.ds(j, 1), :] = lead_off[:1]
                reach_w, whole_w = right(reach), right(running[j])
                reach, reach_off = mul(lead, reach_w), mul(lead_off, reach_w) + reach_off
                lead, lead_off = mul(lead, whole_w), mul(lead_off, whole_w) + offset[j]
            else:
                lead_ref[j] = unit
                lead_off_ref[pl.ds(j, 1), :] = jnp.zeros((1, hidden), F32)
                lead, lead_off = running[j], offset[j]
            reach_ref[j] = reach
            miss = reach_off + guess_ref[pl.ds(row, 1), :] - targets_ref[pl.ds(j, 1), :]
            reach_off_ref[pl.ds(j, 1), :] = miss[:1]
            reach_t = right_t(reach)
            total = total + mul_t(reach, reach_t)
            total_off = total_off + mul_t(miss, reach_t)
        total = total / total_seqs
        message_ref[s, pl.ds(0, hidden), :] = lead
        message_ref[s, pl.ds(hidden, hidden // 2), :] = fold(total)
        tail = hidden + hidden // 2
        for at, row in (
            (OFFSET, lead_off[:1]),
            (ADJOINT, total_off[:1] / total_seqs),
            (FIRST, guess_ref[pl.ds(s * count, 1), :]),
            (DIAGONAL, jnp.sum(unit * total, axis=0, keepdims=True)),
        ):
            message_ref[s, pl.ds(tail + at, 1), :] = row
        message_ref[s, pl.ds(tail + DIAGONAL + 1, 7 - DIAGONAL), :] = jnp.zeros((7 - DIAGONAL, hidden), F32)
    for send in [*sends, hit_copy]:
        send.wait()


def opened(ref, s, with_map=True):
    hidden = ref.shape[2]
    at = hidden if with_map else 0
    rows = [eight(ref[s, pl.ds(at + hidden // 2 + k, 1), :]) for k in range(6)]
    diagonal = ref[s, pl.ds(at + hidden // 2 + DIAGONAL, 1), :]
    half = unfold(ref[s, pl.ds(at, hidden // 2), :])
    curve = half + half.T + identity(hidden) * diagonal
    return (ref[s, pl.ds(0, hidden), :] if with_map else None, curve, rows)


def pick(flag, one, other):
    return jax.tree.map(lambda a, b: jnp.where(flag, a, b), one, other)


def crossing(last, moved, drive, first):
    activation = jnp.tanh(moved + drive)
    return euler_step * (1.0 - activation * activation), last + euler_step * activation - first


def join(one, two, drift_w, with_map=True):
    map_1, curve_1, rows_1 = one
    map_2, curve_2, rows_2 = two
    gain, resid = crossing(rows_1[LAST], rows_1[MOVED], rows_2[DRIVE], rows_2[FIRST])
    map_1 = map_1 + mul(map_1, drift_w) * gain[:1]
    off_1 = rows_1[OFFSET] + mul(rows_1[OFFSET], drift_w) * gain + resid
    curve_w, map_w, map_1_t = right(curve_2), right(map_2), right_t(map_1)
    curve = curve_1 + mul_t(mul(map_1, curve_w), map_1_t)
    adjoint = rows_1[ADJOINT] + mul_t(mul(off_1, curve_w) + rows_2[ADJOINT], map_1_t)
    rows = [mul(off_1, map_w) + rows_2[OFFSET], adjoint, rows_1[DRIVE], rows_1[FIRST], rows_2[LAST], rows_2[MOVED]]
    return (mul(map_1, map_w) if with_map else None), curve, rows


def join_kernel(level, with_map, drift_ref, mine_ref, other_ref, _, out_ref):
    seqs, hidden = mine_ref.shape[0], mine_ref.shape[2]
    upper = (lax.axis_index("seq") >> level) & 1 == 1
    drift_w = right(drift_ref[...])
    for s in range(seqs):
        mine, other = opened(mine_ref, s), opened(other_ref, s)
        whole, curve, rows = join(pick(upper, other, mine), pick(upper, mine, other), drift_w, with_map)
        at = 0
        if with_map:
            out_ref[s, pl.ds(0, hidden), :] = whole
            at = hidden
        out_ref[s, pl.ds(at, hidden // 2), :] = fold(curve)
        diagonal = jnp.sum(identity(hidden) * curve, axis=0, keepdims=True)
        out_ref[s, pl.ds(at + hidden // 2, 8), :] = vectors(*rows, diagonal)


def sides_kernel(levels, drift_ref, *refs):
    mines, others = refs[:levels], refs[levels : 2 * levels]
    entry_ref, tail_ref, back_ref, rows_ref = refs[2 * levels :]
    seqs, hidden = entry_ref.shape[0], entry_ref.shape[1]
    drift_w = right(drift_ref[...])
    unit = identity(hidden)
    for s in range(seqs):
        zero = jnp.zeros((8, hidden), F32)
        lead, lead_off = unit, zero
        after = (unit, jnp.zeros((hidden, hidden), F32), [zero] * 6)
        edge, edge_gain = zero, zero
        place = lax.axis_index("seq")
        fresh = place >= 0
        for level in range(levels):
            upper = (place >> level) & 1 == 1
            mine, other = opened(mines[level], s), opened(others[level], s)
            gain, resid = crossing(other[2][LAST], other[2][MOVED], mine[2][DRIVE], mine[2][FIRST])
            far = other[0] + mul(other[0], drift_w) * gain[:1]
            far_off = other[2][OFFSET] + mul(other[2][OFFSET], drift_w) * gain + resid
            lead_w = right(lead)
            longer = (mul(far, lead_w), mul(far_off, lead_w) + lead_off)
            known = jnp.logical_and(upper, fresh)
            edge, edge_gain = pick(known, (other[2][LAST], gain), (edge, edge_gain))
            fresh = jnp.logical_and(fresh, jnp.logical_not(upper))
            after[2][LAST], after[2][MOVED] = mine[2][LAST], mine[2][MOVED]
            extended = join(after, other, drift_w)
            lead, lead_off = pick(upper, longer, (lead, lead_off))
            after = pick(upper, after, extended)
        own_map, _, own_rows = opened(mines[0], s)
        own_w, curve_w = right(own_map), right(after[1])
        entry_ref[s] = lead
        tail_ref[s] = mul(mul(lead, own_w), curve_w)
        back_ref[s] = after[0].T
        leaving = mul(lead_off, own_w) + own_rows[OFFSET]
        tail_off = mul(leaving, curve_w) + after[2][ADJOINT]
        rows_ref[pl.ds(8 * s, 8), :] = vectors(lead_off, tail_off, edge, edge_gain)


def prepare_kernel(
    seq, blocks, steps_in, hit_in, maps_ref, _, home_ref, pull_ref, ready_ref, steps_ref, hit_ref, sems
):
    fetch_steps = pltpu.make_async_copy(steps_in, steps_ref, sems.at[0])
    fetch_hit = pltpu.make_async_copy(hit_in.at[pl.ds(seq * blocks, blocks)], hit_ref, sems.at[1])
    fetch_steps.start()
    fetch_hit.start()
    ready_ref[...] = jnp.zeros_like(ready_ref)
    chunks, hidden = home_ref.shape[:2]
    per_block = chunks // blocks
    unit = identity(hidden)
    home = unit
    pulls = [jnp.zeros((hidden, hidden), F32)] * blocks
    fetch_steps.wait()
    fetch_hit.wait()
    for chunk in reversed(range(chunks)):
        home_ref[chunk] = home
        active = [k for k in range(blocks) if chunk < (k + 1) * per_block]
        for k in active:
            pull_ref[k, chunk] = pulls[k]
        if chunk:
            stack = jnp.concatenate([home] + [pulls[k] for k in active], axis=0)
            stack = mul_t(stack, right_t(maps_ref[seq * chunks + chunk]))
            home = stack[:hidden]
            for i, k in enumerate(active):
                owner = (k * per_block * LANE + steps_ref[seq, k]) // LANE
                part = stack[(i + 1) * hidden : (i + 2) * hidden]
                pulls[k] = jnp.where(owner == chunk, hit_ref[k].T, part)


def factors_kernel(
    seqs, blocks, steps_in, x_in, guess_in, _, high_ref, low_ref, mark_ref, ready_ref,
    prev_ref, x_ref, guess_ref, steps_ref, sems,
):
    fetch_steps = pltpu.make_async_copy(steps_in, steps_ref, sems.at[2])
    fetch_steps.start()
    fetch_guess = pltpu.make_async_copy(guess_in, guess_ref, sems.at[0])
    fetch_x = pltpu.make_async_copy(x_in, x_ref, sems.at[1])
    fetch_guess.start()
    fetch_x.start()
    ready_ref[...] = jnp.zeros_like(ready_ref)
    rows, hidden = guess_ref.shape
    fetch_guess.wait()
    prev_ref[pl.ds(1, rows - 1), :] = guess_ref[pl.ds(0, rows - 1), :]
    for s in range(seqs):
        prev_ref[pl.ds(s * (rows // seqs), 1), :] = jnp.zeros((1, hidden), F32)
    high_ref[pl.ds(0, hidden), :], low_ref[pl.ds(0, hidden), :] = split(prev_ref[...].T)
    fetch_x.wait()
    rest = pl.ds(hidden, x_ref.shape[1])
    high_ref[rest, :], low_ref[rest, :] = split(x_ref[...].T)
    fetch_steps.wait()
    block = rows // (seqs * blocks)
    row = lax.broadcasted_iota(jnp.int32, (block, hidden), 0)
    for s in range(seqs):
        for k in range(blocks):
            mark_ref[pl.ds((s * blocks + k) * block, block), :] = (row == steps_ref[s, k]).astype(F32)


def ends_kernel(
    seqs, blocks, total_seqs, level, drift_ref, mine_ref, other_ref, *refs
):
    home_refs, pull_refs, refs = refs[:seqs], refs[seqs : 2 * seqs], refs[2 * seqs :]
    (
        before_ref, start_ref, lead_ref, lead_off_ref, entry_ref, tail_ref, back_ref, sides_ref,
        reach_ref, reach_off_ref, gain_ref, mark_ref,
        state_ref, carry_ref, source_ref, gain_back_ref, edge_ref,
    ) = refs
    rows, hidden = gain_ref.shape
    count = rows // seqs
    chunks = count // LANE
    block = count // blocks
    per_block = chunks // blocks
    place = lax.axis_index("seq")
    upper = (place >> level) & 1 == 1
    lowest = (place & ((1 << level) - 1)) == 0
    drift = drift_ref[...]
    drift_w = right(drift)
    drift_wt = right_t(drift)
    unit = identity(hidden)
    gain_back_ref[...] = gain_ref[...]

    entries, tails, sources = [], [], []
    for s in range(seqs):
        mine, other = opened(mine_ref, s, False), opened(other_ref, s, False)
        last, moved, middle = pick(
            upper,
            (other[2][LAST], other[2][MOVED], other[2][OFFSET]),
            (mine[2][LAST], mine[2][MOVED], mine[2][OFFSET]),
        )
        drive, first = pick(upper, (mine[2][DRIVE], mine[2][FIRST]), (other[2][DRIVE], other[2][FIRST]))
        gain, resid = crossing(last, moved, drive, first)
        middle = middle + mul(middle, drift_w) * gain + resid
        middle_col = column(middle[:1], unit)
        row = along(middle_col, jnp.where(upper, entry_ref[s], other[1]))
        lead_off, tail_off, edge, edge_gain = [sides_ref[pl.ds(8 * s + k, 1), :] for k in range(4)]
        beyond = eight(row) + other[2][ADJOINT]
        beyond = beyond + mul_t(beyond * gain, drift_wt)
        entry = column(jnp.where(upper, row, 0.0) + lead_off, unit)
        entries.append([entry])
        for k in range(1, blocks):
            j = s * blocks + k
            entries[s].append(column(along(entry, lead_ref[j]) + lead_off_ref[pl.ds(j, 1), :], unit))
        tail = jnp.where(
            upper, along(middle_col, tail_ref[s]), along(column(beyond[:1], unit), back_ref[s])
        )
        tails.append(column(tail + tail_off, unit))
        known = jnp.logical_and(upper, lowest)
        edge = jnp.where(known, last[:1], edge)
        edge_ref[pl.ds(s, 1), :] = edge
        edge_gain = jnp.where(known, gain[:1], edge_gain)
        at = pl.ds(s * count, 1)
        gain_back_ref[at, :] = gain_ref[at, :] + edge_gain
        here = []
        for k in range(blocks):
            j = s * blocks + k
            miss = (along(entries[s][0], reach_ref[j]) + reach_off_ref[pl.ds(j, 1), :]) / total_seqs
            here_rows = pl.ds(j * block, block)
            source_ref[here_rows, :] = mark_ref[here_rows, :] * miss
            here.append(column(miss, unit))
        sources.append(here)

    def starts(part, chunk, _):
        for s in range(seqs):
            lane = s * chunks + chunk
            row = along(entries[s][part], before_ref[lane])
            state_ref[pl.ds(lane, 1), :] = row + start_ref[pl.ds(lane, 1), :]
        return 0

    def homes(chunk, _):
        for s in range(seqs):
            lane = s * chunks + chunk
            carry_ref[pl.ds(lane, 1), :] = along(tails[s], home_refs[s][chunk])
        return 0

    def pulls(s, part, chunk, _):
        at = pl.ds(s * chunks + chunk, 1)
        row = sum(sources[s][k] * pull_refs[s][k, chunk] for k in range(part, blocks))
        carry_ref[at, :] = carry_ref[at, :] + jnp.sum(row, axis=0, keepdims=True)
        return 0

    for part in range(blocks):
        starting = functools.partial(starts, part)
        lax.fori_loop(part * per_block, (part + 1) * per_block, starting, 0, unroll=4)
    lax.fori_loop(0, chunks, homes, 0, unroll=4)
    for s in range(seqs):
        for part in range(blocks):
            pulling = functools.partial(pulls, s, part)
            lax.fori_loop(part * per_block, (part + 1) * per_block, pulling, 0, unroll=4)


def walk_kernel(
    drift_ref, state_ref, carry_ref, source_ref, gain_ref, gain_back_ref, resid_ref, guess_ref,
    path_ref, pre_ref,
):
    lanes, hidden = state_ref.shape
    drift = drift_ref[...]

    def walks(ahead_ref, behind_ref):
        pltpu.matmul_push_rhs(right(drift), 0, 0)
        pltpu.matmul_push_rhs(right_t(drift), 0, 1, transpose=True)

        def walk(now, both, staged=None):
            state, carry = both
            at = pl.ds(now, lanes, stride=LANE)
            back = pl.ds(LANE - 1 - now, lanes, stride=LANE)
            adjoint = source_ref[back, :] + carry
            scaled = gain_back_ref[back, :] * adjoint
            pltpu.matmul_acc_lhs(ahead_ref, left(state), staged)
            pltpu.matmul_acc_lhs(behind_ref, left(scaled), staged)
            pre_ref[back, :] = scaled
            rest = state + resid_ref[at, :]
            state = rest + gain_ref[at, :] * halves(pltpu.matmul_pop(ahead_ref))
            path_ref[at, :] = guess_ref[at, :] + state
            return state, adjoint + halves(pltpu.matmul_pop(behind_ref))

        both = walk(0, (state_ref[...], carry_ref[...]), 0)
        lax.fori_loop(1, LANE, walk, both, unroll=3)

    wide = (lanes, 2 * hidden)
    pl.run_scoped(walks, pltpu.ACC(0)(wide, F32), pltpu.ACC(1)(wide, F32))


def gradients_kernel(edge_ref, pre_ref, high_ref, low_ref, grads_ref):
    rows, hidden = pre_ref.shape
    seqs = edge_ref.shape[0]
    count = rows // seqs
    unit = identity(hidden)
    pre_high, pre_low = split(pre_ref[...])
    pre_w = jnp.concatenate([pre_high, pre_low], axis=1)
    sums = halves(jnp.dot(high_ref[...], pre_w, preferred_element_type=F32)) + jnp.dot(
        low_ref[...], pre_high, preferred_element_type=F32
    )
    recur = sums[:hidden]
    for s in range(seqs):
        recur = recur + column(edge_ref[pl.ds(s, 1), :], unit) * pre_ref[pl.ds(s * count, 1), :]
    recur = recur.T - recur
    half = hidden // 2
    grads_ref[pl.ds(0, half), :] = fold(recur)
    grads_ref[pl.ds(half, sums.shape[0] - hidden), :] = sums[hidden:]


def finish_kernel(mine_ref, other_ref, recur_ref, in_ref):
    hidden = recur_ref.shape[0]
    half = hidden // 2
    odd = lax.axis_index("batch") & 1 == 1
    mine, other = mine_ref[...], other_ref[...]
    whole = jnp.concatenate([jnp.where(odd, other, mine), jnp.where(odd, mine, other)], axis=0)
    in_ref[...] = whole[half:]
    upper = unfold(whole[:half])
    recur_ref[...] = upper - upper.T


def call(kernel, shapes, in_specs, scratch=(), flops=0, room=14):
    out_shapes = [jax.ShapeDtypeStruct(s, F32) if isinstance(s, tuple) else s for s in shapes]
    run = pl.pallas_call(
        kernel,
        out_shape=out_shapes,
        in_specs=in_specs,
        out_specs=[
            HBM if getattr(s, "memory_space", None) == pltpu.HBM else VMEM for s in out_shapes
        ],
        scratch_shapes=[pltpu.VMEM(s, F32) if isinstance(s, tuple) else s for s in scratch],
        compiler_params=pltpu.CompilerParams(vmem_limit_bytes=room * MIB),
        cost_estimate=pl.CostEstimate(flops=flops, bytes_accessed=1 << 20, transcendentals=0),
    )

    def pinned(*operands):
        placed = [
            pltpu.with_memory_space_constraint(x, pltpu.HBM) if spec is HBM else x
            for x, spec in zip(operands, in_specs, strict=True)
        ]
        return run(*placed)

    return pinned


def swapped(value, axis, distance):
    return lax.ppermute(value, axis, [(i, i ^ distance) for i in range(lax.axis_size(axis))])


def levels_of(axis):
    return lax.axis_size(axis).bit_length() - 1


def on_device(
    inputs, guess_path, recur_weight, damping, in_weight, bias_term, targets, target_steps
):
    seqs, count, hidden = guess_path.shape
    blocks = targets.shape[1]
    features = inputs.shape[2]
    rows = seqs * count
    lanes = rows // LANE
    chunks = lanes // seqs
    hits = seqs * blocks
    total_seqs = seqs * lax.axis_size("batch")
    x = inputs.reshape(rows, features)
    guess = guess_path.reshape(rows, hidden)
    keep = rows * hidden * hidden * 4 <= KEEP
    depth = LANE if keep else 1

    message, maps, before, start, lead, lead_off, hit, reach, reach_off, gain, resid, drift = call(
        functools.partial(compose_kernel, seqs, blocks, total_seqs, keep),
        [
            near((seqs, hidden + hidden // 2 + 8, hidden)),
            near((lanes, hidden, hidden)),
            far((lanes, hidden, hidden)),
            near((lanes, hidden)),
            near((hits, hidden, hidden)),
            near((hits, hidden)),
            far((hits, hidden, hidden)),
            near((hits, hidden, hidden)),
            (hits, hidden),
            far((rows, hidden)),
            far((rows, hidden)),
            (hidden, hidden),
        ],
        [HBM] * 8,
        [
            (rows, hidden),
            (rows, hidden),
            (depth, lanes if keep else 1, hidden, hidden),
            (depth, lanes if keep else 1, hidden),
            (lanes, hidden, hidden),
            (lanes, hidden),
            (hits, hidden, hidden),
            (hits, hidden),
            (rows, hidden),
            pltpu.SMEM((seqs, blocks), jnp.int32),
            (rows, features),
            (rows, hidden),
            (hidden, hidden),
            (1, hidden),
            (features, hidden),
            (1, hidden),
            (hits, hidden),
            pltpu.SemaphoreType.DMA((11 + lanes // RUN,)),
        ],
        room=ROOM,
    )(target_steps, x, guess, recur_weight, damping.reshape(1, hidden), in_weight,
      bias_term.reshape(1, hidden), targets.reshape(hits, hidden))

    def prepare(seq, gate):
        return call(
            functools.partial(prepare_kernel, seq, blocks),
            [
                near((chunks, hidden, hidden)),
                near((blocks, chunks, hidden, hidden)),
                (8, hidden),
            ],
            [HBM, HBM, VMEM, VMEM],
            [
                pltpu.SMEM((seqs, blocks), jnp.int32),
                (blocks, hidden, hidden),
                pltpu.SemaphoreType.DMA((2,)),
            ],
            flops=1 << 32,
        )(target_steps, hit, maps, gate)

    prepared = [prepare(0, drift)]
    ready = prepared[0][2]
    levels = levels_of("seq")
    groups, received = [message], []
    for level in range(levels - 1):
        received.append(swapped(groups[-1], "seq", 1 << level))
        if level == 1:
            prepared += [prepare(s, groups[1]) for s in range(1, seqs)]
            high, low, mark, ready = call(
                functools.partial(factors_kernel, seqs, blocks),
                [
                    jax.ShapeDtypeStruct((hidden + features, rows), BF16),
                    jax.ShapeDtypeStruct((hidden + features, rows), BF16),
                    near((rows, hidden)),
                    (8, hidden),
                ],
                [HBM, HBM, HBM, VMEM],
                [
                    (rows, hidden),
                    (rows, features),
                    (rows, hidden),
                    pltpu.SMEM((seqs, blocks), jnp.int32),
                    pltpu.SemaphoreType.DMA((3,)),
                ],
                flops=1 << 31,
            )(target_steps, x, guess, prepared[-1][2])
        with_map = level < levels - 2
        height = (hidden if with_map else 0) + hidden // 2 + 8
        groups += call(
            functools.partial(join_kernel, level, with_map),
            [(seqs, height, hidden)],
            [VMEM, VMEM, VMEM, VMEM],
        )(drift, groups[-1], received[-1], ready)
    other = swapped(groups[-1], "seq", 1 << (levels - 1))
    square = (seqs, hidden, hidden)
    entry, tail, back, sides = call(
        functools.partial(sides_kernel, levels - 1),
        [square, square, square, (8 * seqs, hidden)],
        [VMEM] * (2 * levels - 1),
        flops=1 << 30,
    )(drift, *groups[:-1], *received)

    state, carry, source, gain_back, edge = call(
        functools.partial(ends_kernel, seqs, blocks, total_seqs, levels - 1),
        [
            near((lanes, hidden)),
            near((lanes, hidden)),
            near((rows, hidden)),
            near((rows, hidden)),
            near((seqs, hidden)),
        ],
        [VMEM] * (15 + 2 * seqs),
    )(drift, groups[-1], other, *[p[0] for p in prepared], *[p[1] for p in prepared], before, start, lead, lead_off, entry, tail, back, sides, reach, reach_off, gain, mark)
    path, pre = call(
        walk_kernel,
        [near((rows, hidden)), near((rows, hidden))],
        [VMEM] * 8,
    )(drift, state, carry, source, gain, gain_back, resid, guess)
    (grads,) = call(
        gradients_kernel, [near((hidden // 2 + features, hidden))], [VMEM] * 4
    )(edge, pre, high, low)

    middle = grads.shape[0] // 2
    odd = lax.axis_index("batch") & 1 == 1
    kept = jnp.where(odd, grads[middle:], grads[:middle])
    given = jnp.where(odd, grads[:middle], grads[middle:])
    kept = kept + swapped(given, "batch", 1)
    width = lax.axis_size("batch")
    hops = [(0, 1 << k) for k in range(1, levels_of("batch"))] + [(1 << k, 0) for k in range(levels)]
    for stage in range(len(hops)):
        route = []
        for i in range(lax.axis_size("seq")):
            for j in range(width):
                along_seq, along_batch = hops[(stage + (j & 1) * (len(hops) // 2)) % len(hops)]
                route.append((i * width + j, (i ^ along_seq) * width + (j ^ along_batch)))
        kept = kept + lax.ppermute(kept, ("seq", "batch"), route)
    grad_recur, grad_in = call(
        finish_kernel,
        [(hidden, hidden), (features, hidden)],
        [VMEM, VMEM],
    )(kept, swapped(kept, "batch", 1))
    return (path.reshape(seqs, count, hidden), grad_recur, grad_in)


def solution(mesh):
    placed = (
        P("batch", "seq", None),
        P("batch", "seq", None),
        P(),
        P(),
        P(),
        P(),
        P("batch", "seq", None),
        P("batch", "seq"),
    )
    return jax.shard_map(
        on_device,
        mesh=mesh,
        in_specs=placed,
        out_specs=(P("batch", "seq", None), P(), P()),
        check_vma=False,
    )
```

```python
import functools

import jax
import jax.numpy as jnp
from jax import lax
from jax.experimental import pallas as pl
from jax.experimental.pallas import tpu as pltpu
from jax.sharding import PartitionSpec as P

LANE = 16
MIB = 1 << 20
UNROLL = 14
RUN = 4
ROOM = 40
KEEP = 36 * MIB
F32 = jnp.float32
BF16 = jnp.bfloat16
VMEM = pl.BlockSpec(memory_space=pltpu.VMEM)
HBM = pl.BlockSpec(memory_space=pltpu.HBM)


def far(shape):
    return pltpu.HBM(shape, F32)


def near(shape):
    return pltpu.VMEM(shape, F32)


euler_step = 0.02


def split(value):
    high = value.astype(BF16)
    return high, (value - high.astype(F32)).astype(BF16)


def left(value):
    return jnp.concatenate(split(value), axis=1)


def right(weight):
    row = jnp.concatenate(split(weight), axis=1)
    return jnp.concatenate([row, row], axis=0)


def right_t(weight):
    high, low = split(weight)
    return jnp.concatenate(
        [jnp.concatenate([high, high], axis=1), jnp.concatenate([low, low], axis=1)], axis=0
    )


def halves(wide):
    hidden = wide.shape[1] // 2
    return wide[:, :hidden] + wide[:, hidden:]


def mul(x, packed):
    return halves(jnp.dot(left(x), packed, preferred_element_type=F32))


def mul_t(x, packed):
    return halves(
        lax.dot_general(left(x), packed, (((1,), (1,)), ((), ())), preferred_element_type=F32)
    )


def mm(x, weight):
    return mul(x, right(weight))


def mm_t(x, weight):
    return mul_t(x, right_t(weight))


def eight(row):
    return jnp.broadcast_to(row, (8, row.shape[1]))


def identity(hidden):
    rows = lax.broadcasted_iota(jnp.int32, (hidden, hidden), 0)
    return (rows == lax.broadcasted_iota(jnp.int32, (hidden, hidden), 1)).astype(F32)


def drift_t(recur_ref, damping_ref):
    weight = recur_ref[...]
    return weight.T - weight - identity(weight.shape[0]) * damping_ref[...]


def column(row, unit):
    return jnp.broadcast_to(jnp.sum(unit * row, axis=1, keepdims=True), unit.shape)


def along(col, weight):
    return jnp.sum(col * weight, axis=0, keepdims=True)


OFFSET, ADJOINT, DRIVE, FIRST, LAST, MOVED, DIAGONAL = range(7)


def triangles(half):
    row = lax.broadcasted_iota(jnp.int32, (half, half), 0)
    col = lax.broadcasted_iota(jnp.int32, (half, half), 1)
    return col > row, col < row


def fold(whole):
    half = whole.shape[0] // 2
    above, _ = triangles(half)
    return jnp.concatenate(
        [jnp.where(above, whole[:half, :half], whole[half:, half:]), whole[:half, half:]], axis=1
    )


def unfold(folded):
    half = folded.shape[0]
    above, below = triangles(half)
    both = folded[:, :half]
    upper = jnp.concatenate([jnp.where(above, both, 0.0), folded[:, half:]], axis=1)
    lower = jnp.concatenate([jnp.zeros((half, half), F32), jnp.where(below, both, 0.0)], axis=1)
    return jnp.concatenate([upper, lower], axis=0)


def vectors(*rows):
    hidden = rows[0].shape[1]
    blank = jnp.zeros((8 - len(rows), hidden), F32)
    return jnp.concatenate([row[:1] for row in rows] + [blank], axis=0)


def compose_kernel(
    seqs, blocks, total_seqs, keep, steps_in, x_in, guess_in, recur_in, damping_in, in_in, bias_in,
    targets_in,
    message_ref, maps_ref, before_out, start_ref, lead_ref, lead_off_ref, hit_out, reach_ref,
    reach_off_ref, gain_out, resid_out, drift_ref,
    gain_ref, resid_ref, record_ref, record_off_ref, before_ref, off_ref, hit_ref, hit_off_ref, prev_ref,
    steps_ref, x_ref, guess_ref, recur_ref, damping_ref, in_ref, bias_ref, targets_ref, sems,
):
    fetches = [
        pltpu.make_async_copy(source, to, sems.at[i])
        for i, (source, to) in enumerate([
            (recur_in, recur_ref), (damping_in, damping_ref), (guess_in, guess_ref), (x_in, x_ref),
            (in_in, in_ref), (bias_in, bias_ref), (targets_in, targets_ref), (steps_in, steps_ref),
        ])
    ]
    for fetch in fetches:
        fetch.start()
    for fetch in fetches[:3]:
        fetch.wait()
    rows, hidden = guess_ref.shape
    count = rows // seqs
    chunks = count // LANE
    lanes = seqs * chunks
    block = count // blocks
    per_block = chunks // blocks
    drift = drift_t(recur_ref, damping_ref)
    drift_ref[...] = drift
    drift_w = right(drift)
    for s in range(seqs):
        last = guess_ref[pl.ds((s + 1) * count - 1, 1), :]
        message_ref[s, pl.ds(hidden + hidden // 2 + LAST, 1), :] = last
        message_ref[s, pl.ds(hidden + hidden // 2 + MOVED, 1), :] = mul(eight(last), drift_w)[:1]
    prev_ref[pl.ds(1, rows - 1), :] = guess_ref[pl.ds(0, rows - 1), :]
    for s in range(seqs):
        prev_ref[pl.ds(s * count, 1), :] = jnp.zeros((1, hidden), F32)
    for fetch in fetches[3:]:
        fetch.wait()
    in_w = jnp.concatenate(split(in_ref[...]), axis=1)

    for top in range(0, rows, block):
        part = pl.ds(top, block)
        x_high, x_low = split(x_ref[part, :])
        drive = bias_ref[...] + halves(
            jnp.dot(x_high, in_w, preferred_element_type=F32)
            + jnp.dot(x_low, in_w, preferred_element_type=F32)
        )
        prev = prev_ref[part, :]
        activation = jnp.tanh(mul(prev, drift_w) + drive)
        gain_ref[part, :] = euler_step * (1.0 - activation * activation)
        resid_ref[part, :] = prev + euler_step * activation - guess_ref[part, :]
        if top % count == 0:
            own = (lax.axis_index("seq") == 0).astype(F32)
            edge = pl.ds(top, 1)
            gain_ref[edge, :] = gain_ref[edge, :] * own
            resid_ref[edge, :] = resid_ref[edge, :] * own
            message_ref[top // count, pl.ds(hidden + hidden // 2 + DRIVE, 1), :] = drive[:1]

    sends = [
        pltpu.make_async_copy(gain_ref, gain_out, sems.at[9]),
        pltpu.make_async_copy(resid_ref, resid_out, sems.at[10]),
    ]
    for send in sends:
        send.start()
    unit = identity(hidden)

    def place(j):
        step = (j % blocks) * block + steps_ref[j // blocks, j % blocks]
        return (j // blocks) * chunks + step // LANE, step % LANE, (j // blocks) * count + step

    def opening(lane):
        return unit + drift * gain_ref[pl.ds(lane * LANE, 1), :]

    def capture(now):
        for j in range(seqs * blocks):
            lane, at, _ = place(j)

            @pl.when(at == now)
            def _():
                hit_ref[j] = maps_ref[lane]
                hit_off_ref[pl.ds(j, 1), :] = off_ref[pl.ds(lane, 1), :]

    def advance(now, _, opened_here=False):
        off = off_ref[...]
        off = (
            off
            + gain_ref[pl.ds(now, lanes, stride=LANE), :] * mul(off, drift_w)
            + resid_ref[pl.ds(now, lanes, stride=LANE), :]
        )
        off_ref[...] = off
        if keep:
            record_off_ref[now] = off
        for lane in range(0, lanes, 2):
            if opened_here:
                pair = jnp.concatenate([opening(lane), opening(lane + 1)], axis=0)
            else:
                pair = maps_ref[lane : lane + 2].reshape(2 * hidden, hidden)
            moved = mul(pair, drift_w)
            for k in range(2):
                gain_now = gain_ref[pl.ds((lane + k) * LANE + now, 1), :]
                part = slice(k * hidden, (k + 1) * hidden)
                longer = pair[part] + gain_now * moved[part]
                maps_ref[lane + k] = longer
                if keep:
                    record_ref[now, lane + k] = longer
        if not keep:
            capture(now)
        return 0

    off_ref[...] = resid_ref[pl.ds(0, lanes, stride=LANE), :]
    if keep:
        record_off_ref[0] = off_ref[...]
        advance(1, 0, True)
        lax.fori_loop(2, LANE, advance, 0, unroll=UNROLL)
        for j in range(seqs * blocks):
            lane, at, _ = place(j)
            hit_ref[j] = jnp.where(at == 0, opening(lane), record_ref[jnp.maximum(at, 1), lane])
            hit_off_ref[pl.ds(j, 1), :] = record_off_ref[at, pl.ds(lane, 1), :]
    else:
        for lane in range(lanes):
            maps_ref[lane] = opening(lane)
        capture(0)
        lax.fori_loop(1, LANE, advance, 0)
    hit_copy = pltpu.make_async_copy(hit_ref, hit_out, sems.at[8])
    hit_copy.start()

    hits = seqs * blocks
    running = [None] * hits
    offset = [None] * hits
    for chunk in range(per_block):
        for j in range(hits):
            lane = j * per_block + chunk
            this, this_off = maps_ref[lane], off_ref[pl.ds(lane, 1), :]
            if chunk == 0:
                before_ref[lane] = unit
                start_ref[pl.ds(lane, 1), :] = jnp.zeros((1, hidden), F32)
                running[j], offset[j] = this, eight(this_off)
            else:
                before_ref[lane] = running[j]
                start_ref[pl.ds(lane, 1), :] = offset[j][:1]
                packed = right(this)
                running[j] = mul(running[j], packed)
                offset[j] = mul(offset[j], packed) + this_off
            if (chunk + 1) % RUN == 0:
                run = pl.ds(lane + 1 - RUN, RUN)
                sends.append(
                    pltpu.make_async_copy(before_ref.at[run], before_out.at[run], sems.at[9 + len(sends)])
                )
                sends[-1].start()

    for s in range(seqs):
        lead, lead_off = None, None
        total = jnp.zeros((hidden, hidden), F32)
        total_off = jnp.zeros((8, hidden), F32)
        for k in range(blocks):
            j = s * blocks + k
            lane, _, row = place(j)
            packed = right(hit_ref[j])
            reach = mul(before_ref[lane], packed)
            reach_off = mul(eight(start_ref[pl.ds(lane, 1), :]), packed) + hit_off_ref[pl.ds(j, 1), :]
            if k:
                lead_ref[j] = lead
                lead_off_ref[pl.ds(j, 1), :] = lead_off[:1]
                reach_w, whole_w = right(reach), right(running[j])
                reach, reach_off = mul(lead, reach_w), mul(lead_off, reach_w) + reach_off
                lead, lead_off = mul(lead, whole_w), mul(lead_off, whole_w) + offset[j]
            else:
                lead_ref[j] = unit
                lead_off_ref[pl.ds(j, 1), :] = jnp.zeros((1, hidden), F32)
                lead, lead_off = running[j], offset[j]
            reach_ref[j] = reach
            miss = reach_off + guess_ref[pl.ds(row, 1), :] - targets_ref[pl.ds(j, 1), :]
            reach_off_ref[pl.ds(j, 1), :] = miss[:1]
            reach_t = right_t(reach)
            total = total + mul_t(reach, reach_t)
            total_off = total_off + mul_t(miss, reach_t)
        total = total / total_seqs
        message_ref[s, pl.ds(0, hidden), :] = lead
        message_ref[s, pl.ds(hidden, hidden // 2), :] = fold(total)
        tail = hidden + hidden // 2
        for at, row in (
            (OFFSET, lead_off[:1]),
            (ADJOINT, total_off[:1] / total_seqs),
            (FIRST, guess_ref[pl.ds(s * count, 1), :]),
            (DIAGONAL, jnp.sum(unit * total, axis=0, keepdims=True)),
        ):
            message_ref[s, pl.ds(tail + at, 1), :] = row
        message_ref[s, pl.ds(tail + DIAGONAL + 1, 7 - DIAGONAL), :] = jnp.zeros((7 - DIAGONAL, hidden), F32)
    for send in [*sends, hit_copy]:
        send.wait()


def opened(ref, s, with_map=True):
    hidden = ref.shape[2]
    at = hidden if with_map else 0
    rows = [eight(ref[s, pl.ds(at + hidden // 2 + k, 1), :]) for k in range(6)]
    diagonal = ref[s, pl.ds(at + hidden // 2 + DIAGONAL, 1), :]
    half = unfold(ref[s, pl.ds(at, hidden // 2), :])
    curve = half + half.T + identity(hidden) * diagonal
    return (ref[s, pl.ds(0, hidden), :] if with_map else None, curve, rows)


def pick(flag, one, other):
    return jax.tree.map(lambda a, b: jnp.where(flag, a, b), one, other)


def crossing(last, moved, drive, first):
    activation = jnp.tanh(moved + drive)
    return euler_step * (1.0 - activation * activation), last + euler_step * activation - first


def join(one, two, drift_w, with_map=True):
    map_1, curve_1, rows_1 = one
    map_2, curve_2, rows_2 = two
    gain, resid = crossing(rows_1[LAST], rows_1[MOVED], rows_2[DRIVE], rows_2[FIRST])
    map_1 = map_1 + mul(map_1, drift_w) * gain[:1]
    off_1 = rows_1[OFFSET] + mul(rows_1[OFFSET], drift_w) * gain + resid
    curve_w, map_w, map_1_t = right(curve_2), right(map_2), right_t(map_1)
    curve = curve_1 + mul_t(mul(map_1, curve_w), map_1_t)
    adjoint = rows_1[ADJOINT] + mul_t(mul(off_1, curve_w) + rows_2[ADJOINT], map_1_t)
    rows = [mul(off_1, map_w) + rows_2[OFFSET], adjoint, rows_1[DRIVE], rows_1[FIRST], rows_2[LAST], rows_2[MOVED]]
    return (mul(map_1, map_w) if with_map else None), curve, rows


def join_kernel(level, with_map, drift_ref, mine_ref, other_ref, _, out_ref):
    seqs, hidden = mine_ref.shape[0], mine_ref.shape[2]
    upper = (lax.axis_index("seq") >> level) & 1 == 1
    drift_w = right(drift_ref[...])
    for s in range(seqs):
        mine, other = opened(mine_ref, s), opened(other_ref, s)
        whole, curve, rows = join(pick(upper, other, mine), pick(upper, mine, other), drift_w, with_map)
        at = 0
        if with_map:
            out_ref[s, pl.ds(0, hidden), :] = whole
            at = hidden
        out_ref[s, pl.ds(at, hidden // 2), :] = fold(curve)
        diagonal = jnp.sum(identity(hidden) * curve, axis=0, keepdims=True)
        out_ref[s, pl.ds(at + hidden // 2, 8), :] = vectors(*rows, diagonal)


def sides_kernel(levels, drift_ref, *refs):
    mines, others = refs[:levels], refs[levels : 2 * levels]
    entry_ref, tail_ref, back_ref, rows_ref = refs[2 * levels :]
    seqs, hidden = entry_ref.shape[0], entry_ref.shape[1]
    drift_w = right(drift_ref[...])
    unit = identity(hidden)
    for s in range(seqs):
        zero = jnp.zeros((8, hidden), F32)
        lead, lead_off = unit, zero
        after = (unit, jnp.zeros((hidden, hidden), F32), [zero] * 6)
        edge, edge_gain = zero, zero
        place = lax.axis_index("seq")
        fresh = place >= 0
        for level in range(levels):
            upper = (place >> level) & 1 == 1
            mine, other = opened(mines[level], s), opened(others[level], s)
            gain, resid = crossing(other[2][LAST], other[2][MOVED], mine[2][DRIVE], mine[2][FIRST])
            far = other[0] + mul(other[0], drift_w) * gain[:1]
            far_off = other[2][OFFSET] + mul(other[2][OFFSET], drift_w) * gain + resid
            lead_w = right(lead)
            longer = (mul(far, lead_w), mul(far_off, lead_w) + lead_off)
            known = jnp.logical_and(upper, fresh)
            edge, edge_gain = pick(known, (other[2][LAST], gain), (edge, edge_gain))
            fresh = jnp.logical_and(fresh, jnp.logical_not(upper))
            after[2][LAST], after[2][MOVED] = mine[2][LAST], mine[2][MOVED]
            extended = join(after, other, drift_w)
            lead, lead_off = pick(upper, longer, (lead, lead_off))
            after = pick(upper, after, extended)
        own_map, _, own_rows = opened(mines[0], s)
        own_w, curve_w = right(own_map), right(after[1])
        entry_ref[s] = lead
        tail_ref[s] = mul(mul(lead, own_w), curve_w)
        back_ref[s] = after[0].T
        leaving = mul(lead_off, own_w) + own_rows[OFFSET]
        tail_off = mul(leaving, curve_w) + after[2][ADJOINT]
        rows_ref[pl.ds(8 * s, 8), :] = vectors(lead_off, tail_off, edge, edge_gain)


def prepare_kernel(
    seq, blocks, steps_in, hit_in, maps_ref, _, home_ref, pull_ref, ready_ref, steps_ref, hit_ref, sems
):
    fetch_steps = pltpu.make_async_copy(steps_in, steps_ref, sems.at[0])
    fetch_hit = pltpu.make_async_copy(hit_in.at[pl.ds(seq * blocks, blocks)], hit_ref, sems.at[1])
    fetch_steps.start()
    fetch_hit.start()
    ready_ref[...] = jnp.zeros_like(ready_ref)
    chunks, hidden = home_ref.shape[:2]
    per_block = chunks // blocks
    unit = identity(hidden)
    home = unit
    pulls = [jnp.zeros((hidden, hidden), F32)] * blocks
    fetch_steps.wait()
    fetch_hit.wait()
    for chunk in reversed(range(chunks)):
        home_ref[chunk] = home
        active = [k for k in range(blocks) if chunk < (k + 1) * per_block]
        for k in active:
            pull_ref[k, chunk] = pulls[k]
        if chunk:
            stack = jnp.concatenate([home] + [pulls[k] for k in active], axis=0)
            stack = mul_t(stack, right_t(maps_ref[seq * chunks + chunk]))
            home = stack[:hidden]
            for i, k in enumerate(active):
                owner = (k * per_block * LANE + steps_ref[seq, k]) // LANE
                part = stack[(i + 1) * hidden : (i + 2) * hidden]
                pulls[k] = jnp.where(owner == chunk, hit_ref[k].T, part)


def factors_kernel(
    seqs, blocks, steps_in, x_in, guess_in, _, high_ref, low_ref, mark_ref, ready_ref,
    prev_ref, x_ref, guess_ref, steps_ref, sems,
):
    fetch_steps = pltpu.make_async_copy(steps_in, steps_ref, sems.at[2])
    fetch_steps.start()
    fetch_guess = pltpu.make_async_copy(guess_in, guess_ref, sems.at[0])
    fetch_x = pltpu.make_async_copy(x_in, x_ref, sems.at[1])
    fetch_guess.start()
    fetch_x.start()
    ready_ref[...] = jnp.zeros_like(ready_ref)
    rows, hidden = guess_ref.shape
    fetch_guess.wait()
    prev_ref[pl.ds(1, rows - 1), :] = guess_ref[pl.ds(0, rows - 1), :]
    for s in range(seqs):
        prev_ref[pl.ds(s * (rows // seqs), 1), :] = jnp.zeros((1, hidden), F32)
    high_ref[pl.ds(0, hidden), :], low_ref[pl.ds(0, hidden), :] = split(prev_ref[...].T)
    fetch_x.wait()
    rest = pl.ds(hidden, x_ref.shape[1])
    high_ref[rest, :], low_ref[rest, :] = split(x_ref[...].T)
    fetch_steps.wait()
    block = rows // (seqs * blocks)
    row = lax.broadcasted_iota(jnp.int32, (block, hidden), 0)
    for s in range(seqs):
        for k in range(blocks):
            mark_ref[pl.ds((s * blocks + k) * block, block), :] = (row == steps_ref[s, k]).astype(F32)


def ends_kernel(
    seqs, blocks, total_seqs, level, drift_ref, mine_ref, other_ref, *refs
):
    home_refs, pull_refs, refs = refs[:seqs], refs[seqs : 2 * seqs], refs[2 * seqs :]
    (
        before_ref, start_ref, lead_ref, lead_off_ref, entry_ref, tail_ref, back_ref, sides_ref,
        reach_ref, reach_off_ref, gain_ref, mark_ref,
        state_ref, carry_ref, source_ref, gain_back_ref, edge_ref,
    ) = refs
    rows, hidden = gain_ref.shape
    count = rows // seqs
    chunks = count // LANE
    block = count // blocks
    per_block = chunks // blocks
    place = lax.axis_index("seq")
    upper = (place >> level) & 1 == 1
    lowest = (place & ((1 << level) - 1)) == 0
    drift = drift_ref[...]
    drift_w = right(drift)
    drift_wt = right_t(drift)
    unit = identity(hidden)
    gain_back_ref[...] = gain_ref[...]

    entries, tails, sources = [], [], []
    for s in range(seqs):
        mine, other = opened(mine_ref, s, False), opened(other_ref, s, False)
        last, moved, middle = pick(
            upper,
            (other[2][LAST], other[2][MOVED], other[2][OFFSET]),
            (mine[2][LAST], mine[2][MOVED], mine[2][OFFSET]),
        )
        drive, first = pick(upper, (mine[2][DRIVE], mine[2][FIRST]), (other[2][DRIVE], other[2][FIRST]))
        gain, resid = crossing(last, moved, drive, first)
        middle = middle + mul(middle, drift_w) * gain + resid
        middle_col = column(middle[:1], unit)
        row = along(middle_col, jnp.where(upper, entry_ref[s], other[1]))
        lead_off, tail_off, edge, edge_gain = [sides_ref[pl.ds(8 * s + k, 1), :] for k in range(4)]
        beyond = eight(row) + other[2][ADJOINT]
        beyond = beyond + mul_t(beyond * gain, drift_wt)
        entry = column(jnp.where(upper, row, 0.0) + lead_off, unit)
        entries.append([entry])
        for k in range(1, blocks):
            j = s * blocks + k
            entries[s].append(column(along(entry, lead_ref[j]) + lead_off_ref[pl.ds(j, 1), :], unit))
        tail = jnp.where(
            upper, along(middle_col, tail_ref[s]), along(column(beyond[:1], unit), back_ref[s])
        )
        tails.append(column(tail + tail_off, unit))
        known = jnp.logical_and(upper, lowest)
        edge = jnp.where(known, last[:1], edge)
        edge_ref[pl.ds(s, 1), :] = edge
        edge_gain = jnp.where(known, gain[:1], edge_gain)
        at = pl.ds(s * count, 1)
        gain_back_ref[at, :] = gain_ref[at, :] + edge_gain
        here = []
        for k in range(blocks):
            j = s * blocks + k
            miss = (along(entries[s][0], reach_ref[j]) + reach_off_ref[pl.ds(j, 1), :]) / total_seqs
            here_rows = pl.ds(j * block, block)
            source_ref[here_rows, :] = mark_ref[here_rows, :] * miss
            here.append(column(miss, unit))
        sources.append(here)

    def starts(part, chunk, _):
        for s in range(seqs):
            lane = s * chunks + chunk
            row = along(entries[s][part], before_ref[lane])
            state_ref[pl.ds(lane, 1), :] = row + start_ref[pl.ds(lane, 1), :]
        return 0

    def homes(chunk, _):
        for s in range(seqs):
            lane = s * chunks + chunk
            carry_ref[pl.ds(lane, 1), :] = along(tails[s], home_refs[s][chunk])
        return 0

    def pulls(s, part, chunk, _):
        at = pl.ds(s * chunks + chunk, 1)
        row = sum(sources[s][k] * pull_refs[s][k, chunk] for k in range(part, blocks))
        carry_ref[at, :] = carry_ref[at, :] + jnp.sum(row, axis=0, keepdims=True)
        return 0

    for part in range(blocks):
        starting = functools.partial(starts, part)
        lax.fori_loop(part * per_block, (part + 1) * per_block, starting, 0, unroll=8)
    lax.fori_loop(0, chunks, homes, 0, unroll=8)
    for s in range(seqs):
        for part in range(blocks):
            pulling = functools.partial(pulls, s, part)
            lax.fori_loop(part * per_block, (part + 1) * per_block, pulling, 0, unroll=8)


def walk_kernel(
    drift_ref, state_ref, carry_ref, source_ref, gain_ref, gain_back_ref, resid_ref, guess_ref,
    path_ref, pre_ref,
):
    lanes, hidden = state_ref.shape
    drift = drift_ref[...]

    def walks(ahead_ref, behind_ref):
        pltpu.matmul_push_rhs(right(drift), 0, 0)
        pltpu.matmul_push_rhs(right_t(drift), 0, 1, transpose=True)

        def walk(now, both, staged=None):
            state, carry = both
            at = pl.ds(now, lanes, stride=LANE)
            back = pl.ds(LANE - 1 - now, lanes, stride=LANE)
            adjoint = source_ref[back, :] + carry
            scaled = gain_back_ref[back, :] * adjoint
            pltpu.matmul_acc_lhs(ahead_ref, left(state), staged)
            pltpu.matmul_acc_lhs(behind_ref, left(scaled), staged)
            pre_ref[back, :] = scaled
            rest = state + resid_ref[at, :]
            state = rest + gain_ref[at, :] * halves(pltpu.matmul_pop(ahead_ref))
            path_ref[at, :] = guess_ref[at, :] + state
            return state, adjoint + halves(pltpu.matmul_pop(behind_ref))

        both = walk(0, (state_ref[...], carry_ref[...]), 0)
        for now in range(1, LANE):
            both = walk(now, both)

    wide = (lanes, 2 * hidden)
    pl.run_scoped(walks, pltpu.ACC(0)(wide, F32), pltpu.ACC(1)(wide, F32))


def gradients_kernel(edge_ref, pre_ref, high_ref, low_ref, grads_ref):
    rows, hidden = pre_ref.shape
    seqs = edge_ref.shape[0]
    count = rows // seqs
    unit = identity(hidden)
    pre_high, pre_low = split(pre_ref[...])
    pre_w = jnp.concatenate([pre_high, pre_low], axis=1)
    sums = halves(jnp.dot(high_ref[...], pre_w, preferred_element_type=F32)) + jnp.dot(
        low_ref[...], pre_high, preferred_element_type=F32
    )
    recur = sums[:hidden]
    for s in range(seqs):
        recur = recur + column(edge_ref[pl.ds(s, 1), :], unit) * pre_ref[pl.ds(s * count, 1), :]
    recur = recur.T - recur
    half = hidden // 2
    grads_ref[pl.ds(0, half), :] = fold(recur)
    grads_ref[pl.ds(half, sums.shape[0] - hidden), :] = sums[hidden:]


def finish_kernel(mine_ref, other_ref, recur_ref, in_ref):
    hidden = recur_ref.shape[0]
    half = hidden // 2
    odd = lax.axis_index("batch") & 1 == 1
    mine, other = mine_ref[...], other_ref[...]
    whole = jnp.concatenate([jnp.where(odd, other, mine), jnp.where(odd, mine, other)], axis=0)
    in_ref[...] = whole[half:]
    upper = unfold(whole[:half])
    recur_ref[...] = upper - upper.T


def call(kernel, shapes, in_specs, scratch=(), flops=0, room=14):
    out_shapes = [jax.ShapeDtypeStruct(s, F32) if isinstance(s, tuple) else s for s in shapes]
    run = pl.pallas_call(
        kernel,
        out_shape=out_shapes,
        in_specs=in_specs,
        out_specs=[
            HBM if getattr(s, "memory_space", None) == pltpu.HBM else VMEM for s in out_shapes
        ],
        scratch_shapes=[pltpu.VMEM(s, F32) if isinstance(s, tuple) else s for s in scratch],
        compiler_params=pltpu.CompilerParams(vmem_limit_bytes=room * MIB),
        cost_estimate=pl.CostEstimate(flops=flops, bytes_accessed=1 << 20, transcendentals=0),
    )

    def pinned(*operands):
        placed = [
            pltpu.with_memory_space_constraint(x, pltpu.HBM) if spec is HBM else x
            for x, spec in zip(operands, in_specs, strict=True)
        ]
        return run(*placed)

    return pinned


def swapped(value, axis, distance):
    return lax.ppermute(value, axis, [(i, i ^ distance) for i in range(lax.axis_size(axis))])


def levels_of(axis):
    return lax.axis_size(axis).bit_length() - 1


def on_device(
    inputs, guess_path, recur_weight, damping, in_weight, bias_term, targets, target_steps
):
    seqs, count, hidden = guess_path.shape
    blocks = targets.shape[1]
    features = inputs.shape[2]
    rows = seqs * count
    lanes = rows // LANE
    chunks = lanes // seqs
    hits = seqs * blocks
    total_seqs = seqs * lax.axis_size("batch")
    x = inputs.reshape(rows, features)
    guess = guess_path.reshape(rows, hidden)
    keep = rows * hidden * hidden * 4 <= KEEP
    depth = LANE if keep else 1

    message, maps, before, start, lead, lead_off, hit, reach, reach_off, gain, resid, drift = call(
        functools.partial(compose_kernel, seqs, blocks, total_seqs, keep),
        [
            near((seqs, hidden + hidden // 2 + 8, hidden)),
            near((lanes, hidden, hidden)),
            far((lanes, hidden, hidden)),
            near((lanes, hidden)),
            near((hits, hidden, hidden)),
            near((hits, hidden)),
            far((hits, hidden, hidden)),
            near((hits, hidden, hidden)),
            (hits, hidden),
            far((rows, hidden)),
            far((rows, hidden)),
            (hidden, hidden),
        ],
        [HBM] * 8,
        [
            (rows, hidden),
            (rows, hidden),
            (depth, lanes if keep else 1, hidden, hidden),
            (depth, lanes if keep else 1, hidden),
            (lanes, hidden, hidden),
            (lanes, hidden),
            (hits, hidden, hidden),
            (hits, hidden),
            (rows, hidden),
            pltpu.SMEM((seqs, blocks), jnp.int32),
            (rows, features),
            (rows, hidden),
            (hidden, hidden),
            (1, hidden),
            (features, hidden),
            (1, hidden),
            (hits, hidden),
            pltpu.SemaphoreType.DMA((11 + lanes // RUN,)),
        ],
        room=ROOM,
    )(target_steps, x, guess, recur_weight, damping.reshape(1, hidden), in_weight,
      bias_term.reshape(1, hidden), targets.reshape(hits, hidden))

    def prepare(seq, gate):
        return call(
            functools.partial(prepare_kernel, seq, blocks),
            [
                near((chunks, hidden, hidden)),
                near((blocks, chunks, hidden, hidden)),
                (8, hidden),
            ],
            [HBM, HBM, VMEM, VMEM],
            [
                pltpu.SMEM((seqs, blocks), jnp.int32),
                (blocks, hidden, hidden),
                pltpu.SemaphoreType.DMA((2,)),
            ],
            flops=1 << 32,
        )(target_steps, hit, maps, gate)

    prepared = [prepare(0, drift)]
    ready = prepared[0][2]
    levels = levels_of("seq")
    groups, received = [message], []
    for level in range(levels - 1):
        received.append(swapped(groups[-1], "seq", 1 << level))
        if level == 1:
            prepared += [prepare(s, groups[1]) for s in range(1, seqs)]
            high, low, mark, ready = call(
                functools.partial(factors_kernel, seqs, blocks),
                [
                    jax.ShapeDtypeStruct((hidden + features, rows), BF16),
                    jax.ShapeDtypeStruct((hidden + features, rows), BF16),
                    near((rows, hidden)),
                    (8, hidden),
                ],
                [HBM, HBM, HBM, VMEM],
                [
                    (rows, hidden),
                    (rows, features),
                    (rows, hidden),
                    pltpu.SMEM((seqs, blocks), jnp.int32),
                    pltpu.SemaphoreType.DMA((3,)),
                ],
                flops=1 << 31,
            )(target_steps, x, guess, prepared[-1][2])
        with_map = level < levels - 2
        height = (hidden if with_map else 0) + hidden // 2 + 8
        groups += call(
            functools.partial(join_kernel, level, with_map),
            [(seqs, height, hidden)],
            [VMEM, VMEM, VMEM, VMEM],
        )(drift, groups[-1], received[-1], ready)
    other = swapped(groups[-1], "seq", 1 << (levels - 1))
    square = (seqs, hidden, hidden)
    entry, tail, back, sides = call(
        functools.partial(sides_kernel, levels - 1),
        [square, square, square, (8 * seqs, hidden)],
        [VMEM] * (2 * levels - 1),
        flops=1 << 30,
    )(drift, *groups[:-1], *received)

    state, carry, source, gain_back, edge = call(
        functools.partial(ends_kernel, seqs, blocks, total_seqs, levels - 1),
        [
            near((lanes, hidden)),
            near((lanes, hidden)),
            near((rows, hidden)),
            near((rows, hidden)),
            near((seqs, hidden)),
        ],
        [VMEM] * (15 + 2 * seqs),
    )(drift, groups[-1], other, *[p[0] for p in prepared], *[p[1] for p in prepared], before, start, lead, lead_off, entry, tail, back, sides, reach, reach_off, gain, mark)
    path, pre = call(
        walk_kernel,
        [near((rows, hidden)), near((rows, hidden))],
        [VMEM] * 8,
    )(drift, state, carry, source, gain, gain_back, resid, guess)
    (grads,) = call(
        gradients_kernel, [near((hidden // 2 + features, hidden))], [VMEM] * 4
    )(edge, pre, high, low)

    middle = grads.shape[0] // 2
    odd = lax.axis_index("batch") & 1 == 1
    kept = jnp.where(odd, grads[middle:], grads[:middle])
    given = jnp.where(odd, grads[:middle], grads[middle:])
    kept = kept + swapped(given, "batch", 1)
    width = lax.axis_size("batch")
    hops = [(0, 1 << k) for k in range(1, levels_of("batch"))] + [(1 << k, 0) for k in range(levels)]
    for stage in range(len(hops)):
        route = []
        for i in range(lax.axis_size("seq")):
            for j in range(width):
                along_seq, along_batch = hops[(stage + (j & 1) * (len(hops) // 2)) % len(hops)]
                route.append((i * width + j, (i ^ along_seq) * width + (j ^ along_batch)))
        kept = kept + lax.ppermute(kept, ("seq", "batch"), route)
    grad_recur, grad_in = call(
        finish_kernel,
        [(hidden, hidden), (features, hidden)],
        [VMEM, VMEM],
    )(kept, swapped(kept, "batch", 1))
    return (path.reshape(seqs, count, hidden), grad_recur, grad_in)


def solution(mesh):
    placed = (
        P("batch", "seq", None),
        P("batch", "seq", None),
        P(),
        P(),
        P(),
        P(),
        P("batch", "seq", None),
        P("batch", "seq"),
    )
    return jax.shard_map(
        on_device,
        mesh=mesh,
        in_specs=placed,
        out_specs=(P("batch", "seq", None), P(), P()),
        check_vma=False,
    )
```

```python
import functools

import jax
import jax.numpy as jnp
from jax import lax
from jax.experimental import pallas as pl
from jax.experimental.pallas import tpu as pltpu
from jax.sharding import PartitionSpec as P

LANE = 16
MIB = 1 << 20
UNROLL = 14
RUN = 4
ROOM = 40
KEEP = 36 * MIB
F32 = jnp.float32
BF16 = jnp.bfloat16
VMEM = pl.BlockSpec(memory_space=pltpu.VMEM)
HBM = pl.BlockSpec(memory_space=pltpu.HBM)


def far(shape):
    return pltpu.HBM(shape, F32)


def near(shape):
    return pltpu.VMEM(shape, F32)


euler_step = 0.02


def split(value):
    high = value.astype(BF16)
    return high, (value - high.astype(F32)).astype(BF16)


def left(value):
    return jnp.concatenate(split(value), axis=1)


def right(weight):
    row = jnp.concatenate(split(weight), axis=1)
    return jnp.concatenate([row, row], axis=0)


def right_t(weight):
    high, low = split(weight)
    return jnp.concatenate(
        [jnp.concatenate([high, high], axis=1), jnp.concatenate([low, low], axis=1)], axis=0
    )


def halves(wide):
    hidden = wide.shape[1] // 2
    return wide[:, :hidden] + wide[:, hidden:]


def mul(x, packed):
    return halves(jnp.dot(left(x), packed, preferred_element_type=F32))


def mul_t(x, packed):
    return halves(
        lax.dot_general(left(x), packed, (((1,), (1,)), ((), ())), preferred_element_type=F32)
    )


def mm(x, weight):
    return mul(x, right(weight))


def mm_t(x, weight):
    return mul_t(x, right_t(weight))


def eight(row):
    return jnp.broadcast_to(row, (8, row.shape[1]))


def identity(hidden):
    rows = lax.broadcasted_iota(jnp.int32, (hidden, hidden), 0)
    return (rows == lax.broadcasted_iota(jnp.int32, (hidden, hidden), 1)).astype(F32)


def drift_t(recur_ref, damping_ref):
    weight = recur_ref[...]
    return weight.T - weight - identity(weight.shape[0]) * damping_ref[...]


def column(row, unit):
    return jnp.broadcast_to(jnp.sum(unit * row, axis=1, keepdims=True), unit.shape)


def along(col, weight):
    return jnp.sum(col * weight, axis=0, keepdims=True)


OFFSET, ADJOINT, DRIVE, FIRST, LAST, MOVED, DIAGONAL = range(7)


def triangles(half):
    row = lax.broadcasted_iota(jnp.int32, (half, half), 0)
    col = lax.broadcasted_iota(jnp.int32, (half, half), 1)
    return col > row, col < row


def fold(whole):
    half = whole.shape[0] // 2
    above, _ = triangles(half)
    return jnp.concatenate(
        [jnp.where(above, whole[:half, :half], whole[half:, half:]), whole[:half, half:]], axis=1
    )


def unfold(folded):
    half = folded.shape[0]
    above, below = triangles(half)
    both = folded[:, :half]
    upper = jnp.concatenate([jnp.where(above, both, 0.0), folded[:, half:]], axis=1)
    lower = jnp.concatenate([jnp.zeros((half, half), F32), jnp.where(below, both, 0.0)], axis=1)
    return jnp.concatenate([upper, lower], axis=0)


def vectors(*rows):
    hidden = rows[0].shape[1]
    blank = jnp.zeros((8 - len(rows), hidden), F32)
    return jnp.concatenate([row[:1] for row in rows] + [blank], axis=0)


def compose_kernel(
    seqs, blocks, total_seqs, keep, steps_in, x_in, guess_in, recur_in, damping_in, in_in, bias_in,
    targets_in,
    message_ref, maps_ref, before_out, start_ref, lead_ref, lead_off_ref, hit_out, reach_ref,
    reach_off_ref, gain_out, resid_out, drift_ref,
    gain_ref, resid_ref, record_ref, record_off_ref, before_ref, off_ref, hit_ref, hit_off_ref, prev_ref,
    steps_ref, x_ref, guess_ref, recur_ref, damping_ref, in_ref, bias_ref, targets_ref, sems,
):
    fetches = [
        pltpu.make_async_copy(source, to, sems.at[i])
        for i, (source, to) in enumerate([
            (recur_in, recur_ref), (damping_in, damping_ref), (guess_in, guess_ref), (x_in, x_ref),
            (in_in, in_ref), (bias_in, bias_ref), (targets_in, targets_ref), (steps_in, steps_ref),
        ])
    ]
    for fetch in fetches:
        fetch.start()
    for fetch in fetches[:3]:
        fetch.wait()
    rows, hidden = guess_ref.shape
    count = rows // seqs
    chunks = count // LANE
    lanes = seqs * chunks
    block = count // blocks
    per_block = chunks // blocks
    drift = drift_t(recur_ref, damping_ref)
    drift_ref[...] = drift
    drift_w = right(drift)
    for s in range(seqs):
        last = guess_ref[pl.ds((s + 1) * count - 1, 1), :]
        message_ref[s, pl.ds(hidden + hidden // 2 + LAST, 1), :] = last
        message_ref[s, pl.ds(hidden + hidden // 2 + MOVED, 1), :] = mul(eight(last), drift_w)[:1]
    prev_ref[pl.ds(1, rows - 1), :] = guess_ref[pl.ds(0, rows - 1), :]
    for s in range(seqs):
        prev_ref[pl.ds(s * count, 1), :] = jnp.zeros((1, hidden), F32)
    for fetch in fetches[3:]:
        fetch.wait()
    in_w = jnp.concatenate(split(in_ref[...]), axis=1)

    for top in range(0, rows, block):
        part = pl.ds(top, block)
        x_high, x_low = split(x_ref[part, :])
        drive = bias_ref[...] + halves(
            jnp.dot(x_high, in_w, preferred_element_type=F32)
            + jnp.dot(x_low, in_w, preferred_element_type=F32)
        )
        prev = prev_ref[part, :]
        activation = jnp.tanh(mul(prev, drift_w) + drive)
        gain_ref[part, :] = euler_step * (1.0 - activation * activation)
        resid_ref[part, :] = prev + euler_step * activation - guess_ref[part, :]
        if top % count == 0:
            own = (lax.axis_index("seq") == 0).astype(F32)
            edge = pl.ds(top, 1)
            gain_ref[edge, :] = gain_ref[edge, :] * own
            resid_ref[edge, :] = resid_ref[edge, :] * own
            message_ref[top // count, pl.ds(hidden + hidden // 2 + DRIVE, 1), :] = drive[:1]

    sends = [
        pltpu.make_async_copy(gain_ref, gain_out, sems.at[9]),
        pltpu.make_async_copy(resid_ref, resid_out, sems.at[10]),
    ]
    for send in sends:
        send.start()
    unit = identity(hidden)

    def place(j):
        step = (j % blocks) * block + steps_ref[j // blocks, j % blocks]
        return (j // blocks) * chunks + step // LANE, step % LANE, (j // blocks) * count + step

    def opening(lane):
        return unit + drift * gain_ref[pl.ds(lane * LANE, 1), :]

    def capture(now):
        for j in range(seqs * blocks):
            lane, at, _ = place(j)

            @pl.when(at == now)
            def _():
                hit_ref[j] = maps_ref[lane]
                hit_off_ref[pl.ds(j, 1), :] = off_ref[pl.ds(lane, 1), :]

    def advance(now, _, opened_here=False):
        off = off_ref[...]
        off = (
            off
            + gain_ref[pl.ds(now, lanes, stride=LANE), :] * mul(off, drift_w)
            + resid_ref[pl.ds(now, lanes, stride=LANE), :]
        )
        off_ref[...] = off
        if keep:
            record_off_ref[now] = off
        for lane in range(0, lanes, 2):
            if opened_here:
                pair = jnp.concatenate([opening(lane), opening(lane + 1)], axis=0)
            else:
                pair = maps_ref[lane : lane + 2].reshape(2 * hidden, hidden)
            moved = mul(pair, drift_w)
            for k in range(2):
                gain_now = gain_ref[pl.ds((lane + k) * LANE + now, 1), :]
                part = slice(k * hidden, (k + 1) * hidden)
                longer = pair[part] + gain_now * moved[part]
                maps_ref[lane + k] = longer
                if keep:
                    record_ref[now, lane + k] = longer
        if not keep:
            capture(now)
        return 0

    off_ref[...] = resid_ref[pl.ds(0, lanes, stride=LANE), :]
    if keep:
        record_off_ref[0] = off_ref[...]
        advance(1, 0, True)
        lax.fori_loop(2, LANE, advance, 0, unroll=UNROLL)
        for j in range(seqs * blocks):
            lane, at, _ = place(j)
            hit_ref[j] = jnp.where(at == 0, opening(lane), record_ref[jnp.maximum(at, 1), lane])
            hit_off_ref[pl.ds(j, 1), :] = record_off_ref[at, pl.ds(lane, 1), :]
    else:
        for lane in range(lanes):
            maps_ref[lane] = opening(lane)
        capture(0)
        lax.fori_loop(1, LANE, advance, 0)
    hit_copy = pltpu.make_async_copy(hit_ref, hit_out, sems.at[8])
    hit_copy.start()

    hits = seqs * blocks
    running = [None] * hits
    offset = [None] * hits
    for chunk in range(per_block):
        for j in range(hits):
            lane = j * per_block + chunk
            this, this_off = maps_ref[lane], off_ref[pl.ds(lane, 1), :]
            if chunk == 0:
                before_ref[lane] = unit
                start_ref[pl.ds(lane, 1), :] = jnp.zeros((1, hidden), F32)
                running[j], offset[j] = this, eight(this_off)
            else:
                before_ref[lane] = running[j]
                start_ref[pl.ds(lane, 1), :] = offset[j][:1]
                packed = right(this)
                running[j] = mul(running[j], packed)
                offset[j] = mul(offset[j], packed) + this_off
            if (chunk + 1) % RUN == 0:
                run = pl.ds(lane + 1 - RUN, RUN)
                sends.append(
                    pltpu.make_async_copy(before_ref.at[run], before_out.at[run], sems.at[9 + len(sends)])
                )
                sends[-1].start()

    for s in range(seqs):
        lead, lead_off = None, None
        total = jnp.zeros((hidden, hidden), F32)
        total_off = jnp.zeros((8, hidden), F32)
        for k in range(blocks):
            j = s * blocks + k
            lane, _, row = place(j)
            packed = right(hit_ref[j])
            reach = mul(before_ref[lane], packed)
            reach_off = mul(eight(start_ref[pl.ds(lane, 1), :]), packed) + hit_off_ref[pl.ds(j, 1), :]
            if k:
                lead_ref[j] = lead
                lead_off_ref[pl.ds(j, 1), :] = lead_off[:1]
                reach_w, whole_w = right(reach), right(running[j])
                reach, reach_off = mul(lead, reach_w), mul(lead_off, reach_w) + reach_off
                lead, lead_off = mul(lead, whole_w), mul(lead_off, whole_w) + offset[j]
            else:
                lead_ref[j] = unit
                lead_off_ref[pl.ds(j, 1), :] = jnp.zeros((1, hidden), F32)
                lead, lead_off = running[j], offset[j]
            reach_ref[j] = reach
            miss = reach_off + guess_ref[pl.ds(row, 1), :] - targets_ref[pl.ds(j, 1), :]
            reach_off_ref[pl.ds(j, 1), :] = miss[:1]
            reach_t = right_t(reach)
            total = total + mul_t(reach, reach_t)
            total_off = total_off + mul_t(miss, reach_t)
        total = total / total_seqs
        message_ref[s, pl.ds(0, hidden), :] = lead
        message_ref[s, pl.ds(hidden, hidden // 2), :] = fold(total)
        tail = hidden + hidden // 2
        for at, row in (
            (OFFSET, lead_off[:1]),
            (ADJOINT, total_off[:1] / total_seqs),
            (FIRST, guess_ref[pl.ds(s * count, 1), :]),
            (DIAGONAL, jnp.sum(unit * total, axis=0, keepdims=True)),
        ):
            message_ref[s, pl.ds(tail + at, 1), :] = row
        message_ref[s, pl.ds(tail + DIAGONAL + 1, 7 - DIAGONAL), :] = jnp.zeros((7 - DIAGONAL, hidden), F32)
    for send in [*sends, hit_copy]:
        send.wait()


def opened(ref, s, with_map=True):
    hidden = ref.shape[2]
    at = hidden if with_map else 0
    rows = [eight(ref[s, pl.ds(at + hidden // 2 + k, 1), :]) for k in range(6)]
    diagonal = ref[s, pl.ds(at + hidden // 2 + DIAGONAL, 1), :]
    half = unfold(ref[s, pl.ds(at, hidden // 2), :])
    curve = half + half.T + identity(hidden) * diagonal
    return (ref[s, pl.ds(0, hidden), :] if with_map else None, curve, rows)


def pick(flag, one, other):
    return jax.tree.map(lambda a, b: jnp.where(flag, a, b), one, other)


def crossing(last, moved, drive, first):
    activation = jnp.tanh(moved + drive)
    return euler_step * (1.0 - activation * activation), last + euler_step * activation - first


def join(one, two, drift_w, with_map=True):
    map_1, curve_1, rows_1 = one
    map_2, curve_2, rows_2 = two
    gain, resid = crossing(rows_1[LAST], rows_1[MOVED], rows_2[DRIVE], rows_2[FIRST])
    map_1 = map_1 + mul(map_1, drift_w) * gain[:1]
    off_1 = rows_1[OFFSET] + mul(rows_1[OFFSET], drift_w) * gain + resid
    curve_w, map_w, map_1_t = right(curve_2), right(map_2), right_t(map_1)
    curve = curve_1 + mul_t(mul(map_1, curve_w), map_1_t)
    adjoint = rows_1[ADJOINT] + mul_t(mul(off_1, curve_w) + rows_2[ADJOINT], map_1_t)
    rows = [mul(off_1, map_w) + rows_2[OFFSET], adjoint, rows_1[DRIVE], rows_1[FIRST], rows_2[LAST], rows_2[MOVED]]
    return (mul(map_1, map_w) if with_map else None), curve, rows


def join_kernel(level, with_map, drift_ref, mine_ref, other_ref, _, out_ref):
    seqs, hidden = mine_ref.shape[0], mine_ref.shape[2]
    upper = (lax.axis_index("seq") >> level) & 1 == 1
    drift_w = right(drift_ref[...])
    for s in range(seqs):
        mine, other = opened(mine_ref, s), opened(other_ref, s)
        whole, curve, rows = join(pick(upper, other, mine), pick(upper, mine, other), drift_w, with_map)
        at = 0
        if with_map:
            out_ref[s, pl.ds(0, hidden), :] = whole
            at = hidden
        out_ref[s, pl.ds(at, hidden // 2), :] = fold(curve)
        diagonal = jnp.sum(identity(hidden) * curve, axis=0, keepdims=True)
        out_ref[s, pl.ds(at + hidden // 2, 8), :] = vectors(*rows, diagonal)


def sides_kernel(levels, drift_ref, *refs):
    mines, others = refs[:levels], refs[levels : 2 * levels]
    entry_ref, tail_ref, back_ref, rows_ref = refs[2 * levels :]
    seqs, hidden = entry_ref.shape[0], entry_ref.shape[1]
    drift_w = right(drift_ref[...])
    unit = identity(hidden)
    for s in range(seqs):
        zero = jnp.zeros((8, hidden), F32)
        lead, lead_off = unit, zero
        after = (unit, jnp.zeros((hidden, hidden), F32), [zero] * 6)
        edge, edge_gain = zero, zero
        place = lax.axis_index("seq")
        fresh = place >= 0
        for level in range(levels):
            upper = (place >> level) & 1 == 1
            mine, other = opened(mines[level], s), opened(others[level], s)
            gain, resid = crossing(other[2][LAST], other[2][MOVED], mine[2][DRIVE], mine[2][FIRST])
            far = other[0] + mul(other[0], drift_w) * gain[:1]
            far_off = other[2][OFFSET] + mul(other[2][OFFSET], drift_w) * gain + resid
            lead_w = right(lead)
            longer = (mul(far, lead_w), mul(far_off, lead_w) + lead_off)
            known = jnp.logical_and(upper, fresh)
            edge, edge_gain = pick(known, (other[2][LAST], gain), (edge, edge_gain))
            fresh = jnp.logical_and(fresh, jnp.logical_not(upper))
            after[2][LAST], after[2][MOVED] = mine[2][LAST], mine[2][MOVED]
            extended = join(after, other, drift_w)
            lead, lead_off = pick(upper, longer, (lead, lead_off))
            after = pick(upper, after, extended)
        own_map, _, own_rows = opened(mines[0], s)
        own_w, curve_w = right(own_map), right(after[1])
        entry_ref[s] = lead
        tail_ref[s] = mul(mul(lead, own_w), curve_w)
        back_ref[s] = after[0].T
        leaving = mul(lead_off, own_w) + own_rows[OFFSET]
        tail_off = mul(leaving, curve_w) + after[2][ADJOINT]
        rows_ref[pl.ds(8 * s, 8), :] = vectors(lead_off, tail_off, edge, edge_gain)


def prepare_kernel(
    seq, blocks, steps_in, hit_in, maps_ref, _, home_ref, pull_ref, ready_ref, steps_ref, hit_ref, sems
):
    fetch_steps = pltpu.make_async_copy(steps_in, steps_ref, sems.at[0])
    fetch_hit = pltpu.make_async_copy(hit_in.at[pl.ds(seq * blocks, blocks)], hit_ref, sems.at[1])
    fetch_steps.start()
    fetch_hit.start()
    ready_ref[...] = jnp.zeros_like(ready_ref)
    chunks, hidden = home_ref.shape[:2]
    per_block = chunks // blocks
    unit = identity(hidden)
    home = unit
    pulls = [jnp.zeros((hidden, hidden), F32)] * blocks
    fetch_steps.wait()
    fetch_hit.wait()
    for chunk in reversed(range(chunks)):
        home_ref[chunk] = home
        active = [k for k in range(blocks) if chunk < (k + 1) * per_block]
        for k in active:
            pull_ref[k, chunk] = pulls[k]
        if chunk:
            stack = jnp.concatenate([home] + [pulls[k] for k in active], axis=0)
            stack = mul_t(stack, right_t(maps_ref[seq * chunks + chunk]))
            home = stack[:hidden]
            for i, k in enumerate(active):
                owner = (k * per_block * LANE + steps_ref[seq, k]) // LANE
                part = stack[(i + 1) * hidden : (i + 2) * hidden]
                pulls[k] = jnp.where(owner == chunk, hit_ref[k].T, part)


def factors_kernel(
    seqs, blocks, steps_in, x_in, guess_in, _, high_ref, low_ref, mark_ref, ready_ref,
    prev_ref, x_ref, guess_ref, steps_ref, sems,
):
    fetch_steps = pltpu.make_async_copy(steps_in, steps_ref, sems.at[2])
    fetch_steps.start()
    fetch_guess = pltpu.make_async_copy(guess_in, guess_ref, sems.at[0])
    fetch_x = pltpu.make_async_copy(x_in, x_ref, sems.at[1])
    fetch_guess.start()
    fetch_x.start()
    ready_ref[...] = jnp.zeros_like(ready_ref)
    rows, hidden = guess_ref.shape
    fetch_guess.wait()
    prev_ref[pl.ds(1, rows - 1), :] = guess_ref[pl.ds(0, rows - 1), :]
    for s in range(seqs):
        prev_ref[pl.ds(s * (rows // seqs), 1), :] = jnp.zeros((1, hidden), F32)
    high_ref[pl.ds(0, hidden), :], low_ref[pl.ds(0, hidden), :] = split(prev_ref[...].T)
    fetch_x.wait()
    rest = pl.ds(hidden, x_ref.shape[1])
    high_ref[rest, :], low_ref[rest, :] = split(x_ref[...].T)
    fetch_steps.wait()
    block = rows // (seqs * blocks)
    row = lax.broadcasted_iota(jnp.int32, (block, hidden), 0)
    for s in range(seqs):
        for k in range(blocks):
            mark_ref[pl.ds((s * blocks + k) * block, block), :] = (row == steps_ref[s, k]).astype(F32)


def ends_kernel(
    seqs, blocks, total_seqs, level, drift_ref, mine_ref, other_ref, *refs
):
    home_refs, pull_refs, refs = refs[:seqs], refs[seqs : 2 * seqs], refs[2 * seqs :]
    (
        before_ref, start_ref, lead_ref, lead_off_ref, entry_ref, tail_ref, back_ref, sides_ref,
        reach_ref, reach_off_ref, gain_ref, mark_ref,
        state_ref, carry_ref, source_ref, gain_back_ref, edge_ref,
    ) = refs
    rows, hidden = gain_ref.shape
    count = rows // seqs
    chunks = count // LANE
    block = count // blocks
    per_block = chunks // blocks
    place = lax.axis_index("seq")
    upper = (place >> level) & 1 == 1
    lowest = (place & ((1 << level) - 1)) == 0
    drift = drift_ref[...]
    drift_w = right(drift)
    drift_wt = right_t(drift)
    unit = identity(hidden)
    gain_back_ref[...] = gain_ref[...]

    entries, tails, sources = [], [], []
    for s in range(seqs):
        mine, other = opened(mine_ref, s, False), opened(other_ref, s, False)
        last, moved, middle = pick(
            upper,
            (other[2][LAST], other[2][MOVED], other[2][OFFSET]),
            (mine[2][LAST], mine[2][MOVED], mine[2][OFFSET]),
        )
        drive, first = pick(upper, (mine[2][DRIVE], mine[2][FIRST]), (other[2][DRIVE], other[2][FIRST]))
        gain, resid = crossing(last, moved, drive, first)
        middle = middle + mul(middle, drift_w) * gain + resid
        middle_col = column(middle[:1], unit)
        row = along(middle_col, jnp.where(upper, entry_ref[s], other[1]))
        lead_off, tail_off, edge, edge_gain = [sides_ref[pl.ds(8 * s + k, 1), :] for k in range(4)]
        beyond = eight(row) + other[2][ADJOINT]
        beyond = beyond + mul_t(beyond * gain, drift_wt)
        entry = column(jnp.where(upper, row, 0.0) + lead_off, unit)
        entries.append([entry])
        for k in range(1, blocks):
            j = s * blocks + k
            entries[s].append(column(along(entry, lead_ref[j]) + lead_off_ref[pl.ds(j, 1), :], unit))
        tail = jnp.where(
            upper, along(middle_col, tail_ref[s]), along(column(beyond[:1], unit), back_ref[s])
        )
        tails.append(column(tail + tail_off, unit))
        known = jnp.logical_and(upper, lowest)
        edge = jnp.where(known, last[:1], edge)
        edge_ref[pl.ds(s, 1), :] = edge
        edge_gain = jnp.where(known, gain[:1], edge_gain)
        at = pl.ds(s * count, 1)
        gain_back_ref[at, :] = gain_ref[at, :] + edge_gain
        here = []
        for k in range(blocks):
            j = s * blocks + k
            miss = (along(entries[s][0], reach_ref[j]) + reach_off_ref[pl.ds(j, 1), :]) / total_seqs
            here_rows = pl.ds(j * block, block)
            source_ref[here_rows, :] = mark_ref[here_rows, :] * miss
            here.append(column(miss, unit))
        sources.append(here)

    def starts(part, chunk, _):
        for s in range(seqs):
            lane = s * chunks + chunk
            row = along(entries[s][part], before_ref[lane])
            state_ref[pl.ds(lane, 1), :] = row + start_ref[pl.ds(lane, 1), :]
        return 0

    def homes(chunk, _):
        for s in range(seqs):
            lane = s * chunks + chunk
            carry_ref[pl.ds(lane, 1), :] = along(tails[s], home_refs[s][chunk])
        return 0

    def pulls(s, part, chunk, _):
        at = pl.ds(s * chunks + chunk, 1)
        row = sum(sources[s][k] * pull_refs[s][k, chunk] for k in range(part, blocks))
        carry_ref[at, :] = carry_ref[at, :] + jnp.sum(row, axis=0, keepdims=True)
        return 0

    for part in range(blocks):
        starting = functools.partial(starts, part)
        lax.fori_loop(part * per_block, (part + 1) * per_block, starting, 0, unroll=8)
    lax.fori_loop(0, chunks, homes, 0, unroll=8)
    for s in range(seqs):
        for part in range(blocks):
            pulling = functools.partial(pulls, s, part)
            lax.fori_loop(part * per_block, (part + 1) * per_block, pulling, 0, unroll=8)


def walk_kernel(
    drift_ref, state_ref, carry_ref, source_ref, gain_ref, gain_back_ref, resid_ref, guess_ref,
    path_ref, pre_ref,
):
    lanes, hidden = state_ref.shape
    drift = drift_ref[...]

    def walks(ahead_ref, behind_ref):
        pltpu.matmul_push_rhs(right(drift), 0, 0)
        pltpu.matmul_push_rhs(right_t(drift), 0, 1, transpose=True)

        def walk(now, both, staged=None):
            state, carry = both
            at = pl.ds(now, lanes, stride=LANE)
            back = pl.ds(LANE - 1 - now, lanes, stride=LANE)
            adjoint = source_ref[back, :] + carry
            scaled = gain_back_ref[back, :] * adjoint
            pltpu.matmul_acc_lhs(ahead_ref, left(state), staged)
            pltpu.matmul_acc_lhs(behind_ref, left(scaled), staged)
            pre_ref[back, :] = scaled
            rest = state + resid_ref[at, :]
            state = rest + gain_ref[at, :] * halves(pltpu.matmul_pop(ahead_ref))
            path_ref[at, :] = guess_ref[at, :] + state
            return state, adjoint + halves(pltpu.matmul_pop(behind_ref))

        both = walk(0, (state_ref[...], carry_ref[...]), 0)
        for now in range(1, LANE):
            both = walk(now, both)

    wide = (lanes, 2 * hidden)
    pl.run_scoped(walks, pltpu.ACC(0)(wide, F32), pltpu.ACC(1)(wide, F32))


def gradients_kernel(edge_ref, pre_ref, high_ref, low_ref, grads_ref):
    rows, hidden = pre_ref.shape
    seqs = edge_ref.shape[0]
    count = rows // seqs
    unit = identity(hidden)
    pre_high, pre_low = split(pre_ref[...])
    pre_w = jnp.concatenate([pre_high, pre_low], axis=1)
    sums = halves(jnp.dot(high_ref[...], pre_w, preferred_element_type=F32)) + jnp.dot(
        low_ref[...], pre_high, preferred_element_type=F32
    )
    recur = sums[:hidden]
    for s in range(seqs):
        recur = recur + column(edge_ref[pl.ds(s, 1), :], unit) * pre_ref[pl.ds(s * count, 1), :]
    recur = recur.T - recur
    half = hidden // 2
    grads_ref[pl.ds(0, half), :] = fold(recur)
    grads_ref[pl.ds(half, sums.shape[0] - hidden), :] = sums[hidden:]


def finish_kernel(mine_ref, other_ref, recur_ref, in_ref):
    hidden = recur_ref.shape[0]
    half = hidden // 2
    odd = lax.axis_index("batch") & 1 == 1
    mine, other = mine_ref[...], other_ref[...]
    whole = jnp.concatenate([jnp.where(odd, other, mine), jnp.where(odd, mine, other)], axis=0)
    in_ref[...] = whole[half:]
    upper = unfold(whole[:half])
    recur_ref[...] = upper - upper.T


def call(kernel, shapes, in_specs, scratch=(), flops=0, room=14):
    out_shapes = [jax.ShapeDtypeStruct(s, F32) if isinstance(s, tuple) else s for s in shapes]
    run = pl.pallas_call(
        kernel,
        out_shape=out_shapes,
        in_specs=in_specs,
        out_specs=[
            HBM if getattr(s, "memory_space", None) == pltpu.HBM else VMEM for s in out_shapes
        ],
        scratch_shapes=[pltpu.VMEM(s, F32) if isinstance(s, tuple) else s for s in scratch],
        compiler_params=pltpu.CompilerParams(vmem_limit_bytes=room * MIB),
        cost_estimate=pl.CostEstimate(flops=flops, bytes_accessed=1 << 20, transcendentals=0),
    )

    def pinned(*operands):
        placed = [
            pltpu.with_memory_space_constraint(x, pltpu.HBM) if spec is HBM else x
            for x, spec in zip(operands, in_specs, strict=True)
        ]
        return run(*placed)

    return pinned


def swapped(value, axis, distance):
    return lax.ppermute(value, axis, [(i, i ^ distance) for i in range(lax.axis_size(axis))])


def levels_of(axis):
    return lax.axis_size(axis).bit_length() - 1


def on_device(
    inputs, guess_path, recur_weight, damping, in_weight, bias_term, targets, target_steps
):
    seqs, count, hidden = guess_path.shape
    blocks = targets.shape[1]
    features = inputs.shape[2]
    rows = seqs * count
    lanes = rows // LANE
    chunks = lanes // seqs
    hits = seqs * blocks
    total_seqs = seqs * lax.axis_size("batch")
    x = inputs.reshape(rows, features)
    guess = guess_path.reshape(rows, hidden)
    keep = rows * hidden * hidden * 4 <= KEEP
    depth = LANE if keep else 1

    message, maps, before, start, lead, lead_off, hit, reach, reach_off, gain, resid, drift = call(
        functools.partial(compose_kernel, seqs, blocks, total_seqs, keep),
        [
            near((seqs, hidden + hidden // 2 + 8, hidden)),
            near((lanes, hidden, hidden)),
            far((lanes, hidden, hidden)),
            near((lanes, hidden)),
            near((hits, hidden, hidden)),
            near((hits, hidden)),
            far((hits, hidden, hidden)),
            near((hits, hidden, hidden)),
            (hits, hidden),
            far((rows, hidden)),
            far((rows, hidden)),
            (hidden, hidden),
        ],
        [HBM] * 8,
        [
            (rows, hidden),
            (rows, hidden),
            (depth, lanes if keep else 1, hidden, hidden),
            (depth, lanes if keep else 1, hidden),
            (lanes, hidden, hidden),
            (lanes, hidden),
            (hits, hidden, hidden),
            (hits, hidden),
            (rows, hidden),
            pltpu.SMEM((seqs, blocks), jnp.int32),
            (rows, features),
            (rows, hidden),
            (hidden, hidden),
            (1, hidden),
            (features, hidden),
            (1, hidden),
            (hits, hidden),
            pltpu.SemaphoreType.DMA((11 + lanes // RUN,)),
        ],
        room=ROOM,
    )(target_steps, x, guess, recur_weight, damping.reshape(1, hidden), in_weight,
      bias_term.reshape(1, hidden), targets.reshape(hits, hidden))

    def prepare(seq, gate):
        return call(
            functools.partial(prepare_kernel, seq, blocks),
            [
                near((chunks, hidden, hidden)),
                near((blocks, chunks, hidden, hidden)),
                (8, hidden),
            ],
            [HBM, HBM, VMEM, VMEM],
            [
                pltpu.SMEM((seqs, blocks), jnp.int32),
                (blocks, hidden, hidden),
                pltpu.SemaphoreType.DMA((2,)),
            ],
            flops=1 << 32,
        )(target_steps, hit, maps, gate)

    prepared = [prepare(0, drift)]
    ready = prepared[0][2]
    levels = levels_of("seq")
    groups, received = [message], []
    for level in range(levels - 1):
        received.append(swapped(groups[-1], "seq", 1 << level))
        if level == 1:
            prepared += [prepare(s, groups[1]) for s in range(1, seqs)]
            high, low, mark, ready = call(
                functools.partial(factors_kernel, seqs, blocks),
                [
                    jax.ShapeDtypeStruct((hidden + features, rows), BF16),
                    jax.ShapeDtypeStruct((hidden + features, rows), BF16),
                    near((rows, hidden)),
                    (8, hidden),
                ],
                [HBM, HBM, HBM, VMEM],
                [
                    (rows, hidden),
                    (rows, features),
                    (rows, hidden),
                    pltpu.SMEM((seqs, blocks), jnp.int32),
                    pltpu.SemaphoreType.DMA((3,)),
                ],
                flops=1 << 31,
            )(target_steps, x, guess, prepared[-1][2])
        with_map = level < levels - 2
        height = (hidden if with_map else 0) + hidden // 2 + 8
        groups += call(
            functools.partial(join_kernel, level, with_map),
            [(seqs, height, hidden)],
            [VMEM, VMEM, VMEM, VMEM],
        )(drift, groups[-1], received[-1], ready)
    other = swapped(groups[-1], "seq", 1 << (levels - 1))
    square = (seqs, hidden, hidden)
    entry, tail, back, sides = call(
        functools.partial(sides_kernel, levels - 1),
        [square, square, square, (8 * seqs, hidden)],
        [VMEM] * (2 * levels - 1),
        flops=1 << 30,
    )(drift, *groups[:-1], *received)

    state, carry, source, gain_back, edge = call(
        functools.partial(ends_kernel, seqs, blocks, total_seqs, levels - 1),
        [
            near((lanes, hidden)),
            near((lanes, hidden)),
            near((rows, hidden)),
            near((rows, hidden)),
            near((seqs, hidden)),
        ],
        [VMEM] * (15 + 2 * seqs),
    )(drift, groups[-1], other, *[p[0] for p in prepared], *[p[1] for p in prepared], before, start, lead, lead_off, entry, tail, back, sides, reach, reach_off, gain, mark)
    path, pre = call(
        walk_kernel,
        [near((rows, hidden)), near((rows, hidden))],
        [VMEM] * 8,
    )(drift, state, carry, source, gain, gain_back, resid, guess)
    (grads,) = call(
        gradients_kernel, [near((hidden // 2 + features, hidden))], [VMEM] * 4
    )(edge, pre, high, low)

    middle = grads.shape[0] // 2
    odd = lax.axis_index("batch") & 1 == 1
    kept = jnp.where(odd, grads[middle:], grads[:middle])
    given = jnp.where(odd, grads[:middle], grads[middle:])
    kept = kept + swapped(given, "batch", 1)
    width = lax.axis_size("batch")
    hops = [(0, 1 << k) for k in range(1, levels_of("batch"))] + [(1 << k, 0) for k in range(levels)]

    def moved(value, hop_of):
        route = []
        for i in range(lax.axis_size("seq")):
            for j in range(width):
                along_seq, along_batch = hop_of(j & 1)
                route.append((i * width + j, (i ^ along_seq) * width + (j ^ along_batch)))
        return lax.ppermute(value, ("seq", "batch"), route)

    fours = []
    for one, two in zip(hops[::2], hops[1::2]):
        fours.append([one, two, (one[0] ^ two[0], one[1] ^ two[1])])
    for stage in range(len(fours)):
        parts = []
        for which in range(3):
            turn = lambda odd: fours[(stage + odd * (len(fours) // 2)) % len(fours)][which]
            parts.append(moved(kept, turn))
        kept = (kept + parts[0]) + (parts[1] + parts[2])
    if len(hops) % 2:
        kept = kept + moved(kept, lambda odd: hops[-1])
    grad_recur, grad_in = call(
        finish_kernel,
        [(hidden, hidden), (features, hidden)],
        [VMEM, VMEM],
    )(kept, swapped(kept, "batch", 1))
    return (path.reshape(seqs, count, hidden), grad_recur, grad_in)


def solution(mesh):
    placed = (
        P("batch", "seq", None),
        P("batch", "seq", None),
        P(),
        P(),
        P(),
        P(),
        P("batch", "seq", None),
        P("batch", "seq"),
    )
    return jax.shard_map(
        on_device,
        mesh=mesh,
        in_specs=placed,
        out_specs=(P("batch", "seq", None), P(), P()),
        check_vma=False,
    )
```

```python
import functools

import jax
import jax.numpy as jnp
from jax import lax
from jax.experimental import pallas as pl
from jax.experimental.pallas import tpu as pltpu
from jax.sharding import PartitionSpec as P

LANE = 16
MIB = 1 << 20
UNROLL = 14
RUN = 4
ROOM = 40
KEEP = 36 * MIB
F32 = jnp.float32
BF16 = jnp.bfloat16
VMEM = pl.BlockSpec(memory_space=pltpu.VMEM)
HBM = pl.BlockSpec(memory_space=pltpu.HBM)


def far(shape):
    return pltpu.HBM(shape, F32)


def near(shape):
    return pltpu.VMEM(shape, F32)


euler_step = 0.02


def split(value):
    high = value.astype(BF16)
    return high, (value - high.astype(F32)).astype(BF16)


def left(value):
    return jnp.concatenate(split(value), axis=1)


def right(weight):
    row = jnp.concatenate(split(weight), axis=1)
    return jnp.concatenate([row, row], axis=0)


def right_t(weight):
    high, low = split(weight)
    return jnp.concatenate(
        [jnp.concatenate([high, high], axis=1), jnp.concatenate([low, low], axis=1)], axis=0
    )


def halves(wide):
    hidden = wide.shape[1] // 2
    return wide[:, :hidden] + wide[:, hidden:]


def mul(x, packed):
    return halves(jnp.dot(left(x), packed, preferred_element_type=F32))


def mul_t(x, packed):
    return halves(
        lax.dot_general(left(x), packed, (((1,), (1,)), ((), ())), preferred_element_type=F32)
    )


def mm(x, weight):
    return mul(x, right(weight))


def mm_t(x, weight):
    return mul_t(x, right_t(weight))


def eight(row):
    return jnp.broadcast_to(row, (8, row.shape[1]))


def identity(hidden):
    rows = lax.broadcasted_iota(jnp.int32, (hidden, hidden), 0)
    return (rows == lax.broadcasted_iota(jnp.int32, (hidden, hidden), 1)).astype(F32)


def drift_t(recur_ref, damping_ref):
    weight = recur_ref[...]
    return weight.T - weight - identity(weight.shape[0]) * damping_ref[...]


def column(row, unit):
    return jnp.broadcast_to(jnp.sum(unit * row, axis=1, keepdims=True), unit.shape)


def along(col, weight):
    return jnp.sum(col * weight, axis=0, keepdims=True)


OFFSET, ADJOINT, DRIVE, FIRST, LAST, MOVED, DIAGONAL = range(7)


def triangles(half):
    row = lax.broadcasted_iota(jnp.int32, (half, half), 0)
    col = lax.broadcasted_iota(jnp.int32, (half, half), 1)
    return col > row, col < row


def fold(whole):
    half = whole.shape[0] // 2
    above, _ = triangles(half)
    return jnp.concatenate(
        [jnp.where(above, whole[:half, :half], whole[half:, half:]), whole[:half, half:]], axis=1
    )


def unfold(folded):
    half = folded.shape[0]
    above, below = triangles(half)
    both = folded[:, :half]
    upper = jnp.concatenate([jnp.where(above, both, 0.0), folded[:, half:]], axis=1)
    lower = jnp.concatenate([jnp.zeros((half, half), F32), jnp.where(below, both, 0.0)], axis=1)
    return jnp.concatenate([upper, lower], axis=0)


def vectors(*rows):
    hidden = rows[0].shape[1]
    blank = jnp.zeros((8 - len(rows), hidden), F32)
    return jnp.concatenate([row[:1] for row in rows] + [blank], axis=0)


def compose_kernel(
    seqs, blocks, total_seqs, keep, steps_in, x_in, guess_in, recur_in, damping_in, in_in, bias_in,
    targets_in,
    message_ref, maps_ref, before_out, start_ref, lead_ref, lead_off_ref, hit_out, reach_ref,
    reach_off_ref, gain_out, resid_out, drift_ref,
    gain_ref, resid_ref, record_ref, record_off_ref, before_ref, off_ref, hit_ref, hit_off_ref, prev_ref,
    steps_ref, x_ref, guess_ref, recur_ref, damping_ref, in_ref, bias_ref, targets_ref, sems,
):
    fetches = [
        pltpu.make_async_copy(source, to, sems.at[i])
        for i, (source, to) in enumerate([
            (recur_in, recur_ref), (damping_in, damping_ref), (guess_in, guess_ref), (x_in, x_ref),
            (in_in, in_ref), (bias_in, bias_ref), (targets_in, targets_ref), (steps_in, steps_ref),
        ])
    ]
    for fetch in fetches:
        fetch.start()
    for fetch in fetches[:3]:
        fetch.wait()
    rows, hidden = guess_ref.shape
    count = rows // seqs
    chunks = count // LANE
    lanes = seqs * chunks
    block = count // blocks
    per_block = chunks // blocks
    drift = drift_t(recur_ref, damping_ref)
    drift_ref[...] = drift
    drift_w = right(drift)
    for s in range(seqs):
        last = guess_ref[pl.ds((s + 1) * count - 1, 1), :]
        message_ref[s, pl.ds(hidden + hidden // 2 + LAST, 1), :] = last
        message_ref[s, pl.ds(hidden + hidden // 2 + MOVED, 1), :] = mul(eight(last), drift_w)[:1]
    prev_ref[pl.ds(1, rows - 1), :] = guess_ref[pl.ds(0, rows - 1), :]
    for s in range(seqs):
        prev_ref[pl.ds(s * count, 1), :] = jnp.zeros((1, hidden), F32)
    for fetch in fetches[3:]:
        fetch.wait()
    in_w = jnp.concatenate(split(in_ref[...]), axis=1)

    for top in range(0, rows, block):
        part = pl.ds(top, block)
        x_high, x_low = split(x_ref[part, :])
        drive = bias_ref[...] + halves(
            jnp.dot(x_high, in_w, preferred_element_type=F32)
            + jnp.dot(x_low, in_w, preferred_element_type=F32)
        )
        prev = prev_ref[part, :]
        activation = jnp.tanh(mul(prev, drift_w) + drive)
        gain_ref[part, :] = euler_step * (1.0 - activation * activation)
        resid_ref[part, :] = prev + euler_step * activation - guess_ref[part, :]
        if top % count == 0:
            own = (lax.axis_index("seq") == 0).astype(F32)
            edge = pl.ds(top, 1)
            gain_ref[edge, :] = gain_ref[edge, :] * own
            resid_ref[edge, :] = resid_ref[edge, :] * own
            message_ref[top // count, pl.ds(hidden + hidden // 2 + DRIVE, 1), :] = drive[:1]

    sends = [
        pltpu.make_async_copy(gain_ref, gain_out, sems.at[9]),
        pltpu.make_async_copy(resid_ref, resid_out, sems.at[10]),
    ]
    for send in sends:
        send.start()
    unit = identity(hidden)

    def place(j):
        step = (j % blocks) * block + steps_ref[j // blocks, j % blocks]
        return (j // blocks) * chunks + step // LANE, step % LANE, (j // blocks) * count + step

    def opening(lane):
        return unit + drift * gain_ref[pl.ds(lane * LANE, 1), :]

    def capture(now):
        for j in range(seqs * blocks):
            lane, at, _ = place(j)

            @pl.when(at == now)
            def _():
                hit_ref[j] = maps_ref[lane]
                hit_off_ref[pl.ds(j, 1), :] = off_ref[pl.ds(lane, 1), :]

    def advance(now, _, opened_here=False):
        off = off_ref[...]
        off = (
            off
            + gain_ref[pl.ds(now, lanes, stride=LANE), :] * mul(off, drift_w)
            + resid_ref[pl.ds(now, lanes, stride=LANE), :]
        )
        off_ref[...] = off
        if keep:
            record_off_ref[now] = off
        for lane in range(0, lanes, 2):
            if opened_here:
                pair = jnp.concatenate([opening(lane), opening(lane + 1)], axis=0)
            else:
                pair = maps_ref[lane : lane + 2].reshape(2 * hidden, hidden)
            moved = mul(pair, drift_w)
            for k in range(2):
                gain_now = gain_ref[pl.ds((lane + k) * LANE + now, 1), :]
                part = slice(k * hidden, (k + 1) * hidden)
                longer = pair[part] + gain_now * moved[part]
                maps_ref[lane + k] = longer
                if keep:
                    record_ref[now, lane + k] = longer
        if not keep:
            capture(now)
        return 0

    off_ref[...] = resid_ref[pl.ds(0, lanes, stride=LANE), :]
    if keep:
        record_off_ref[0] = off_ref[...]
        advance(1, 0, True)
        lax.fori_loop(2, LANE, advance, 0, unroll=UNROLL)
        for j in range(seqs * blocks):
            lane, at, _ = place(j)
            hit_ref[j] = jnp.where(at == 0, opening(lane), record_ref[jnp.maximum(at, 1), lane])
            hit_off_ref[pl.ds(j, 1), :] = record_off_ref[at, pl.ds(lane, 1), :]
    else:
        for lane in range(lanes):
            maps_ref[lane] = opening(lane)
        capture(0)
        lax.fori_loop(1, LANE, advance, 0)
    hit_copy = pltpu.make_async_copy(hit_ref, hit_out, sems.at[8])
    hit_copy.start()

    hits = seqs * blocks
    running = [None] * hits
    offset = [None] * hits
    for chunk in range(per_block):
        for j in range(hits):
            lane = j * per_block + chunk
            this, this_off = maps_ref[lane], off_ref[pl.ds(lane, 1), :]
            if chunk == 0:
                before_ref[lane] = unit
                start_ref[pl.ds(lane, 1), :] = jnp.zeros((1, hidden), F32)
                running[j], offset[j] = this, eight(this_off)
            else:
                before_ref[lane] = running[j]
                start_ref[pl.ds(lane, 1), :] = offset[j][:1]
                packed = right(this)
                running[j] = mul(running[j], packed)
                offset[j] = mul(offset[j], packed) + this_off
            if (chunk + 1) % RUN == 0:
                run = pl.ds(lane + 1 - RUN, RUN)
                sends.append(
                    pltpu.make_async_copy(before_ref.at[run], before_out.at[run], sems.at[9 + len(sends)])
                )
                sends[-1].start()

    for s in range(seqs):
        lead, lead_off = None, None
        total = jnp.zeros((hidden, hidden), F32)
        total_off = jnp.zeros((8, hidden), F32)
        for k in range(blocks):
            j = s * blocks + k
            lane, _, row = place(j)
            packed = right(hit_ref[j])
            reach = mul(before_ref[lane], packed)
            reach_off = mul(eight(start_ref[pl.ds(lane, 1), :]), packed) + hit_off_ref[pl.ds(j, 1), :]
            if k:
                lead_ref[j] = lead
                lead_off_ref[pl.ds(j, 1), :] = lead_off[:1]
                reach_w, whole_w = right(reach), right(running[j])
                reach, reach_off = mul(lead, reach_w), mul(lead_off, reach_w) + reach_off
                lead, lead_off = mul(lead, whole_w), mul(lead_off, whole_w) + offset[j]
            else:
                lead_ref[j] = unit
                lead_off_ref[pl.ds(j, 1), :] = jnp.zeros((1, hidden), F32)
                lead, lead_off = running[j], offset[j]
            reach_ref[j] = reach
            miss = reach_off + guess_ref[pl.ds(row, 1), :] - targets_ref[pl.ds(j, 1), :]
            reach_off_ref[pl.ds(j, 1), :] = miss[:1]
            reach_t = right_t(reach)
            total = total + mul_t(reach, reach_t)
            total_off = total_off + mul_t(miss, reach_t)
        total = total / total_seqs
        message_ref[s, pl.ds(0, hidden), :] = lead
        message_ref[s, pl.ds(hidden, hidden // 2), :] = fold(total)
        tail = hidden + hidden // 2
        for at, row in (
            (OFFSET, lead_off[:1]),
            (ADJOINT, total_off[:1] / total_seqs),
            (FIRST, guess_ref[pl.ds(s * count, 1), :]),
            (DIAGONAL, jnp.sum(unit * total, axis=0, keepdims=True)),
        ):
            message_ref[s, pl.ds(tail + at, 1), :] = row
        message_ref[s, pl.ds(tail + DIAGONAL + 1, 7 - DIAGONAL), :] = jnp.zeros((7 - DIAGONAL, hidden), F32)
    for send in [*sends, hit_copy]:
        send.wait()


def opened(ref, s, with_map=True):
    hidden = ref.shape[2]
    at = hidden if with_map else 0
    rows = [eight(ref[s, pl.ds(at + hidden // 2 + k, 1), :]) for k in range(6)]
    diagonal = ref[s, pl.ds(at + hidden // 2 + DIAGONAL, 1), :]
    half = unfold(ref[s, pl.ds(at, hidden // 2), :])
    curve = half + half.T + identity(hidden) * diagonal
    return (ref[s, pl.ds(0, hidden), :] if with_map else None, curve, rows)


def pick(flag, one, other):
    return jax.tree.map(lambda a, b: jnp.where(flag, a, b), one, other)


def crossing(last, moved, drive, first):
    activation = jnp.tanh(moved + drive)
    return euler_step * (1.0 - activation * activation), last + euler_step * activation - first


def join(one, two, drift_w, with_map=True):
    map_1, curve_1, rows_1 = one
    map_2, curve_2, rows_2 = two
    gain, resid = crossing(rows_1[LAST], rows_1[MOVED], rows_2[DRIVE], rows_2[FIRST])
    map_1 = map_1 + mul(map_1, drift_w) * gain[:1]
    off_1 = rows_1[OFFSET] + mul(rows_1[OFFSET], drift_w) * gain + resid
    curve_w, map_w, map_1_t = right(curve_2), right(map_2), right_t(map_1)
    curve = curve_1 + mul_t(mul(map_1, curve_w), map_1_t)
    adjoint = rows_1[ADJOINT] + mul_t(mul(off_1, curve_w) + rows_2[ADJOINT], map_1_t)
    rows = [mul(off_1, map_w) + rows_2[OFFSET], adjoint, rows_1[DRIVE], rows_1[FIRST], rows_2[LAST], rows_2[MOVED]]
    return (mul(map_1, map_w) if with_map else None), curve, rows


def join_kernel(level, with_map, drift_ref, mine_ref, other_ref, _, out_ref):
    seqs, hidden = mine_ref.shape[0], mine_ref.shape[2]
    upper = (lax.axis_index("seq") >> level) & 1 == 1
    drift_w = right(drift_ref[...])
    for s in range(seqs):
        mine, other = opened(mine_ref, s), opened(other_ref, s)
        whole, curve, rows = join(pick(upper, other, mine), pick(upper, mine, other), drift_w, with_map)
        at = 0
        if with_map:
            out_ref[s, pl.ds(0, hidden), :] = whole
            at = hidden
        out_ref[s, pl.ds(at, hidden // 2), :] = fold(curve)
        diagonal = jnp.sum(identity(hidden) * curve, axis=0, keepdims=True)
        out_ref[s, pl.ds(at + hidden // 2, 8), :] = vectors(*rows, diagonal)


def sides_kernel(levels, drift_ref, *refs):
    mines, others = refs[:levels], refs[levels : 2 * levels]
    entry_ref, tail_ref, back_ref, rows_ref = refs[2 * levels :]
    seqs, hidden = entry_ref.shape[0], entry_ref.shape[1]
    drift_w = right(drift_ref[...])
    unit = identity(hidden)
    for s in range(seqs):
        zero = jnp.zeros((8, hidden), F32)
        lead, lead_off = unit, zero
        after = (unit, jnp.zeros((hidden, hidden), F32), [zero] * 6)
        edge, edge_gain = zero, zero
        place = lax.axis_index("seq")
        fresh = place >= 0
        for level in range(levels):
            upper = (place >> level) & 1 == 1
            mine, other = opened(mines[level], s), opened(others[level], s)
            gain, resid = crossing(other[2][LAST], other[2][MOVED], mine[2][DRIVE], mine[2][FIRST])
            far = other[0] + mul(other[0], drift_w) * gain[:1]
            far_off = other[2][OFFSET] + mul(other[2][OFFSET], drift_w) * gain + resid
            lead_w = right(lead)
            longer = (mul(far, lead_w), mul(far_off, lead_w) + lead_off)
            known = jnp.logical_and(upper, fresh)
            edge, edge_gain = pick(known, (other[2][LAST], gain), (edge, edge_gain))
            fresh = jnp.logical_and(fresh, jnp.logical_not(upper))
            after[2][LAST], after[2][MOVED] = mine[2][LAST], mine[2][MOVED]
            extended = join(after, other, drift_w)
            lead, lead_off = pick(upper, longer, (lead, lead_off))
            after = pick(upper, after, extended)
        own_map, _, own_rows = opened(mines[0], s)
        own_w, curve_w = right(own_map), right(after[1])
        entry_ref[s] = lead
        tail_ref[s] = mul(mul(lead, own_w), curve_w)
        back_ref[s] = after[0].T
        leaving = mul(lead_off, own_w) + own_rows[OFFSET]
        tail_off = mul(leaving, curve_w) + after[2][ADJOINT]
        rows_ref[pl.ds(8 * s, 8), :] = vectors(lead_off, tail_off, edge, edge_gain)


def prepare_kernel(
    seq, blocks, steps_in, hit_in, maps_ref, _, home_ref, pull_ref, ready_ref, steps_ref, hit_ref, sems
):
    fetch_steps = pltpu.make_async_copy(steps_in, steps_ref, sems.at[0])
    fetch_hit = pltpu.make_async_copy(hit_in.at[pl.ds(seq * blocks, blocks)], hit_ref, sems.at[1])
    fetch_steps.start()
    fetch_hit.start()
    ready_ref[...] = jnp.zeros_like(ready_ref)
    chunks, hidden = home_ref.shape[:2]
    per_block = chunks // blocks
    unit = identity(hidden)
    home = unit
    pulls = [jnp.zeros((hidden, hidden), F32)] * blocks
    fetch_steps.wait()
    fetch_hit.wait()
    for chunk in reversed(range(chunks)):
        home_ref[chunk] = home
        active = [k for k in range(blocks) if chunk < (k + 1) * per_block]
        for k in active:
            pull_ref[k, chunk] = pulls[k]
        if chunk:
            stack = jnp.concatenate([home] + [pulls[k] for k in active], axis=0)
            stack = mul_t(stack, right_t(maps_ref[seq * chunks + chunk]))
            home = stack[:hidden]
            for i, k in enumerate(active):
                owner = (k * per_block * LANE + steps_ref[seq, k]) // LANE
                part = stack[(i + 1) * hidden : (i + 2) * hidden]
                pulls[k] = jnp.where(owner == chunk, hit_ref[k].T, part)


def factors_kernel(
    seqs, blocks, steps_in, x_in, guess_in, _, high_ref, low_ref, mark_ref, ready_ref,
    prev_ref, x_ref, guess_ref, steps_ref, sems,
):
    fetch_steps = pltpu.make_async_copy(steps_in, steps_ref, sems.at[2])
    fetch_steps.start()
    fetch_guess = pltpu.make_async_copy(guess_in, guess_ref, sems.at[0])
    fetch_x = pltpu.make_async_copy(x_in, x_ref, sems.at[1])
    fetch_guess.start()
    fetch_x.start()
    ready_ref[...] = jnp.zeros_like(ready_ref)
    rows, hidden = guess_ref.shape
    fetch_guess.wait()
    prev_ref[pl.ds(1, rows - 1), :] = guess_ref[pl.ds(0, rows - 1), :]
    for s in range(seqs):
        prev_ref[pl.ds(s * (rows // seqs), 1), :] = jnp.zeros((1, hidden), F32)
    high_ref[pl.ds(0, hidden), :], low_ref[pl.ds(0, hidden), :] = split(prev_ref[...].T)
    fetch_x.wait()
    rest = pl.ds(hidden, x_ref.shape[1])
    high_ref[rest, :], low_ref[rest, :] = split(x_ref[...].T)
    fetch_steps.wait()
    block = rows // (seqs * blocks)
    row = lax.broadcasted_iota(jnp.int32, (block, hidden), 0)
    for s in range(seqs):
        for k in range(blocks):
            mark_ref[pl.ds((s * blocks + k) * block, block), :] = (row == steps_ref[s, k]).astype(F32)


def ends_kernel(
    seqs, blocks, total_seqs, level, drift_ref, mine_ref, other_ref, *refs
):
    home_refs, pull_refs, refs = refs[:seqs], refs[seqs : 2 * seqs], refs[2 * seqs :]
    (
        before_ref, start_ref, lead_ref, lead_off_ref, entry_ref, tail_ref, back_ref, sides_ref,
        reach_ref, reach_off_ref, gain_ref, mark_ref,
        state_ref, carry_ref, source_ref, gain_back_ref, edge_ref,
    ) = refs
    rows, hidden = gain_ref.shape
    count = rows // seqs
    chunks = count // LANE
    block = count // blocks
    per_block = chunks // blocks
    place = lax.axis_index("seq")
    upper = (place >> level) & 1 == 1
    lowest = (place & ((1 << level) - 1)) == 0
    drift = drift_ref[...]
    drift_w = right(drift)
    drift_wt = right_t(drift)
    unit = identity(hidden)
    gain_back_ref[...] = gain_ref[...]

    entries, tails, sources = [], [], []
    for s in range(seqs):
        mine, other = opened(mine_ref, s, False), opened(other_ref, s, False)
        last, moved, middle = pick(
            upper,
            (other[2][LAST], other[2][MOVED], other[2][OFFSET]),
            (mine[2][LAST], mine[2][MOVED], mine[2][OFFSET]),
        )
        drive, first = pick(upper, (mine[2][DRIVE], mine[2][FIRST]), (other[2][DRIVE], other[2][FIRST]))
        gain, resid = crossing(last, moved, drive, first)
        middle = middle + mul(middle, drift_w) * gain + resid
        middle_col = column(middle[:1], unit)
        row = along(middle_col, jnp.where(upper, entry_ref[s], other[1]))
        lead_off, tail_off, edge, edge_gain = [sides_ref[pl.ds(8 * s + k, 1), :] for k in range(4)]
        beyond = eight(row) + other[2][ADJOINT]
        beyond = beyond + mul_t(beyond * gain, drift_wt)
        entry = column(jnp.where(upper, row, 0.0) + lead_off, unit)
        entries.append([entry])
        for k in range(1, blocks):
            j = s * blocks + k
            entries[s].append(column(along(entry, lead_ref[j]) + lead_off_ref[pl.ds(j, 1), :], unit))
        tail = jnp.where(
            upper, along(middle_col, tail_ref[s]), along(column(beyond[:1], unit), back_ref[s])
        )
        tails.append(column(tail + tail_off, unit))
        known = jnp.logical_and(upper, lowest)
        edge = jnp.where(known, last[:1], edge)
        edge_ref[pl.ds(s, 1), :] = edge
        edge_gain = jnp.where(known, gain[:1], edge_gain)
        at = pl.ds(s * count, 1)
        gain_back_ref[at, :] = gain_ref[at, :] + edge_gain
        here = []
        for k in range(blocks):
            j = s * blocks + k
            miss = (along(entries[s][0], reach_ref[j]) + reach_off_ref[pl.ds(j, 1), :]) / total_seqs
            here_rows = pl.ds(j * block, block)
            source_ref[here_rows, :] = mark_ref[here_rows, :] * miss
            here.append(column(miss, unit))
        sources.append(here)

    def starts(part, chunk, _):
        for s in range(seqs):
            lane = s * chunks + chunk
            row = along(entries[s][part], before_ref[lane])
            state_ref[pl.ds(lane, 1), :] = row + start_ref[pl.ds(lane, 1), :]
        return 0

    def homes(chunk, _):
        for s in range(seqs):
            lane = s * chunks + chunk
            carry_ref[pl.ds(lane, 1), :] = along(tails[s], home_refs[s][chunk])
        return 0

    def pulls(s, part, chunk, _):
        at = pl.ds(s * chunks + chunk, 1)
        row = sum(sources[s][k] * pull_refs[s][k, chunk] for k in range(part, blocks))
        carry_ref[at, :] = carry_ref[at, :] + jnp.sum(row, axis=0, keepdims=True)
        return 0

    for part in range(blocks):
        starting = functools.partial(starts, part)
        lax.fori_loop(part * per_block, (part + 1) * per_block, starting, 0, unroll=8)
    lax.fori_loop(0, chunks, homes, 0, unroll=8)
    for s in range(seqs):
        for part in range(blocks):
            pulling = functools.partial(pulls, s, part)
            lax.fori_loop(part * per_block, (part + 1) * per_block, pulling, 0, unroll=8)


def walk_kernel(
    drift_ref, state_ref, carry_ref, source_ref, gain_ref, gain_back_ref, resid_ref, guess_ref,
    path_ref, pre_ref,
):
    lanes, hidden = state_ref.shape
    drift = drift_ref[...]

    def walks(ahead_ref, behind_ref):
        pltpu.matmul_push_rhs(right(drift), 0, 0)
        pltpu.matmul_push_rhs(right_t(drift), 0, 1, transpose=True)

        def walk(now, both, staged=None):
            state, carry = both
            at = pl.ds(now, lanes, stride=LANE)
            back = pl.ds(LANE - 1 - now, lanes, stride=LANE)
            adjoint = source_ref[back, :] + carry
            scaled = gain_back_ref[back, :] * adjoint
            pltpu.matmul_acc_lhs(ahead_ref, left(state), staged)
            pltpu.matmul_acc_lhs(behind_ref, left(scaled), staged)
            pre_ref[back, :] = scaled
            rest = state + resid_ref[at, :]
            state = rest + gain_ref[at, :] * halves(pltpu.matmul_pop(ahead_ref))
            path_ref[at, :] = guess_ref[at, :] + state
            return state, adjoint + halves(pltpu.matmul_pop(behind_ref))

        both = walk(0, (state_ref[...], carry_ref[...]), 0)
        for now in range(1, LANE):
            both = walk(now, both)

    wide = (lanes, 2 * hidden)
    pl.run_scoped(walks, pltpu.ACC(0)(wide, F32), pltpu.ACC(1)(wide, F32))


def gradients_kernel(edge_ref, pre_ref, high_ref, low_ref, grads_ref):
    rows, hidden = pre_ref.shape
    seqs = edge_ref.shape[0]
    count = rows // seqs
    unit = identity(hidden)
    pre_high, pre_low = split(pre_ref[...])
    pre_w = jnp.concatenate([pre_high, pre_low], axis=1)
    sums = halves(jnp.dot(high_ref[...], pre_w, preferred_element_type=F32)) + jnp.dot(
        low_ref[...], pre_high, preferred_element_type=F32
    )
    recur = sums[:hidden]
    for s in range(seqs):
        recur = recur + column(edge_ref[pl.ds(s, 1), :], unit) * pre_ref[pl.ds(s * count, 1), :]
    recur = recur.T - recur
    half = hidden // 2
    grads_ref[pl.ds(0, half), :] = fold(recur)
    grads_ref[pl.ds(half, sums.shape[0] - hidden), :] = sums[hidden:]


def finish_kernel(mine_ref, other_ref, recur_ref, in_ref):
    hidden = recur_ref.shape[0]
    half = hidden // 2
    odd = lax.axis_index("batch") & 1 == 1
    mine, other = mine_ref[...], other_ref[...]
    whole = jnp.concatenate([jnp.where(odd, other, mine), jnp.where(odd, mine, other)], axis=0)
    in_ref[...] = whole[half:]
    upper = unfold(whole[:half])
    recur_ref[...] = upper - upper.T


def call(kernel, shapes, in_specs, scratch=(), flops=0, room=14):
    out_shapes = [jax.ShapeDtypeStruct(s, F32) if isinstance(s, tuple) else s for s in shapes]
    run = pl.pallas_call(
        kernel,
        out_shape=out_shapes,
        in_specs=in_specs,
        out_specs=[
            HBM if getattr(s, "memory_space", None) == pltpu.HBM else VMEM for s in out_shapes
        ],
        scratch_shapes=[pltpu.VMEM(s, F32) if isinstance(s, tuple) else s for s in scratch],
        compiler_params=pltpu.CompilerParams(vmem_limit_bytes=room * MIB),
        cost_estimate=pl.CostEstimate(flops=flops, bytes_accessed=1 << 20, transcendentals=0),
    )

    def pinned(*operands):
        placed = [
            pltpu.with_memory_space_constraint(x, pltpu.HBM) if spec is HBM else x
            for x, spec in zip(operands, in_specs, strict=True)
        ]
        return run(*placed)

    return pinned


def swapped(value, axis, distance):
    return lax.ppermute(value, axis, [(i, i ^ distance) for i in range(lax.axis_size(axis))])


def levels_of(axis):
    return lax.axis_size(axis).bit_length() - 1


def on_device(
    inputs, guess_path, recur_weight, damping, in_weight, bias_term, targets, target_steps
):
    seqs, count, hidden = guess_path.shape
    blocks = targets.shape[1]
    features = inputs.shape[2]
    rows = seqs * count
    lanes = rows // LANE
    chunks = lanes // seqs
    hits = seqs * blocks
    total_seqs = seqs * lax.axis_size("batch")
    x = inputs.reshape(rows, features)
    guess = guess_path.reshape(rows, hidden)
    keep = rows * hidden * hidden * 4 <= KEEP
    depth = LANE if keep else 1

    message, maps, before, start, lead, lead_off, hit, reach, reach_off, gain, resid, drift = call(
        functools.partial(compose_kernel, seqs, blocks, total_seqs, keep),
        [
            near((seqs, hidden + hidden // 2 + 8, hidden)),
            near((lanes, hidden, hidden)),
            far((lanes, hidden, hidden)),
            near((lanes, hidden)),
            near((hits, hidden, hidden)),
            near((hits, hidden)),
            far((hits, hidden, hidden)),
            near((hits, hidden, hidden)),
            (hits, hidden),
            far((rows, hidden)),
            far((rows, hidden)),
            (hidden, hidden),
        ],
        [HBM] * 8,
        [
            (rows, hidden),
            (rows, hidden),
            (depth, lanes if keep else 1, hidden, hidden),
            (depth, lanes if keep else 1, hidden),
            (lanes, hidden, hidden),
            (lanes, hidden),
            (hits, hidden, hidden),
            (hits, hidden),
            (rows, hidden),
            pltpu.SMEM((seqs, blocks), jnp.int32),
            (rows, features),
            (rows, hidden),
            (hidden, hidden),
            (1, hidden),
            (features, hidden),
            (1, hidden),
            (hits, hidden),
            pltpu.SemaphoreType.DMA((11 + lanes // RUN,)),
        ],
        room=ROOM,
    )(target_steps, x, guess, recur_weight, damping.reshape(1, hidden), in_weight,
      bias_term.reshape(1, hidden), targets.reshape(hits, hidden))

    def prepare(seq, gate):
        return call(
            functools.partial(prepare_kernel, seq, blocks),
            [
                near((chunks, hidden, hidden)),
                near((blocks, chunks, hidden, hidden)),
                (8, hidden),
            ],
            [HBM, HBM, VMEM, VMEM],
            [
                pltpu.SMEM((seqs, blocks), jnp.int32),
                (blocks, hidden, hidden),
                pltpu.SemaphoreType.DMA((2,)),
            ],
            flops=1 << 32,
        )(target_steps, hit, maps, gate)

    prepared = [prepare(0, drift)]
    ready = prepared[0][2]
    levels = levels_of("seq")
    groups, received = [message], []
    for level in range(levels - 1):
        received.append(swapped(groups[-1], "seq", 1 << level))
        if level == 1:
            prepared += [prepare(s, groups[1]) for s in range(1, seqs)]
            high, low, mark, ready = call(
                functools.partial(factors_kernel, seqs, blocks),
                [
                    jax.ShapeDtypeStruct((hidden + features, rows), BF16),
                    jax.ShapeDtypeStruct((hidden + features, rows), BF16),
                    near((rows, hidden)),
                    (8, hidden),
                ],
                [HBM, HBM, HBM, VMEM],
                [
                    (rows, hidden),
                    (rows, features),
                    (rows, hidden),
                    pltpu.SMEM((seqs, blocks), jnp.int32),
                    pltpu.SemaphoreType.DMA((3,)),
                ],
                flops=1 << 31,
            )(target_steps, x, guess, prepared[-1][2])
        with_map = level < levels - 2
        height = (hidden if with_map else 0) + hidden // 2 + 8
        groups += call(
            functools.partial(join_kernel, level, with_map),
            [(seqs, height, hidden)],
            [VMEM, VMEM, VMEM, VMEM],
        )(drift, groups[-1], received[-1], ready)
    other = swapped(groups[-1], "seq", 1 << (levels - 1))
    square = (seqs, hidden, hidden)
    entry, tail, back, sides = call(
        functools.partial(sides_kernel, levels - 1),
        [square, square, square, (8 * seqs, hidden)],
        [VMEM] * (2 * levels - 1),
        flops=1 << 30,
    )(drift, *groups[:-1], *received)

    state, carry, source, gain_back, edge = call(
        functools.partial(ends_kernel, seqs, blocks, total_seqs, levels - 1),
        [
            near((lanes, hidden)),
            near((lanes, hidden)),
            near((rows, hidden)),
            near((rows, hidden)),
            near((seqs, hidden)),
        ],
        [VMEM] * (15 + 2 * seqs),
    )(drift, groups[-1], other, *[p[0] for p in prepared], *[p[1] for p in prepared], before, start, lead, lead_off, entry, tail, back, sides, reach, reach_off, gain, mark)
    path, pre = call(
        walk_kernel,
        [near((rows, hidden)), near((rows, hidden))],
        [VMEM] * 8,
    )(drift, state, carry, source, gain, gain_back, resid, guess)
    (grads,) = call(
        gradients_kernel, [near((hidden // 2 + features, hidden))], [VMEM] * 4
    )(edge, pre, high, low)

    middle = grads.shape[0] // 2
    odd = lax.axis_index("batch") & 1 == 1
    kept = jnp.where(odd, grads[middle:], grads[:middle])
    given = jnp.where(odd, grads[:middle], grads[middle:])
    kept = kept + swapped(given, "batch", 1)
    width = lax.axis_size("batch")
    hops = [(0, 1 << k) for k in range(1, levels_of("batch"))] + [(1 << k, 0) for k in range(levels)]

    def moved(value, hop_of):
        route = []
        for i in range(lax.axis_size("seq")):
            for j in range(width):
                along_seq, along_batch = hop_of(j & 1)
                route.append((i * width + j, (i ^ along_seq) * width + (j ^ along_batch)))
        return lax.ppermute(value, ("seq", "batch"), route)

    one, two = hops[:2]
    near_by = [one, two, (one[0] ^ two[0], one[1] ^ two[1])]
    parts = [moved(kept, lambda odd: hop) for hop in near_by]
    kept = (kept + parts[0]) + (parts[1] + parts[2])
    rest = hops[2:]
    for stage in range(len(rest)):
        turn = lambda odd: rest[(stage + odd * (len(rest) // 2)) % len(rest)]
        kept = kept + moved(kept, turn)
    grad_recur, grad_in = call(
        finish_kernel,
        [(hidden, hidden), (features, hidden)],
        [VMEM, VMEM],
    )(kept, swapped(kept, "batch", 1))
    return (path.reshape(seqs, count, hidden), grad_recur, grad_in)


def solution(mesh):
    placed = (
        P("batch", "seq", None),
        P("batch", "seq", None),
        P(),
        P(),
        P(),
        P(),
        P("batch", "seq", None),
        P("batch", "seq"),
    )
    return jax.shard_map(
        on_device,
        mesh=mesh,
        in_specs=placed,
        out_specs=(P("batch", "seq", None), P(), P()),
        check_vma=False,
    )
```

```python
import functools

import jax
import jax.numpy as jnp
from jax import lax
from jax.experimental import pallas as pl
from jax.experimental.pallas import tpu as pltpu
from jax.sharding import PartitionSpec as P

LANE = 16
MIB = 1 << 20
UNROLL = 14
RUN = 4
ROOM = 40
KEEP = 36 * MIB
F32 = jnp.float32
BF16 = jnp.bfloat16
VMEM = pl.BlockSpec(memory_space=pltpu.VMEM)
HBM = pl.BlockSpec(memory_space=pltpu.HBM)


def far(shape):
    return pltpu.HBM(shape, F32)


def near(shape):
    return pltpu.VMEM(shape, F32)


euler_step = 0.02


def split(value):
    high = value.astype(BF16)
    return high, (value - high.astype(F32)).astype(BF16)


def left(value):
    return jnp.concatenate(split(value), axis=1)


def right(weight):
    row = jnp.concatenate(split(weight), axis=1)
    return jnp.concatenate([row, row], axis=0)


def right_t(weight):
    high, low = split(weight)
    return jnp.concatenate(
        [jnp.concatenate([high, high], axis=1), jnp.concatenate([low, low], axis=1)], axis=0
    )


def halves(wide):
    hidden = wide.shape[1] // 2
    return wide[:, :hidden] + wide[:, hidden:]


def mul(x, packed):
    return halves(jnp.dot(left(x), packed, preferred_element_type=F32))


def mul_t(x, packed):
    return halves(
        lax.dot_general(left(x), packed, (((1,), (1,)), ((), ())), preferred_element_type=F32)
    )


def mm(x, weight):
    return mul(x, right(weight))


def mm_t(x, weight):
    return mul_t(x, right_t(weight))


def eight(row):
    return jnp.broadcast_to(row, (8, row.shape[1]))


def identity(hidden):
    rows = lax.broadcasted_iota(jnp.int32, (hidden, hidden), 0)
    return (rows == lax.broadcasted_iota(jnp.int32, (hidden, hidden), 1)).astype(F32)


def drift_t(recur_ref, damping_ref):
    weight = recur_ref[...]
    return weight.T - weight - identity(weight.shape[0]) * damping_ref[...]


def column(row, unit):
    return jnp.broadcast_to(jnp.sum(unit * row, axis=1, keepdims=True), unit.shape)


def along(col, weight):
    return jnp.sum(col * weight, axis=0, keepdims=True)


OFFSET, ADJOINT, DRIVE, FIRST, LAST, MOVED, DIAGONAL = range(7)


def triangles(half):
    row = lax.broadcasted_iota(jnp.int32, (half, half), 0)
    col = lax.broadcasted_iota(jnp.int32, (half, half), 1)
    return col > row, col < row


def fold(whole):
    half = whole.shape[0] // 2
    above, _ = triangles(half)
    return jnp.concatenate(
        [jnp.where(above, whole[:half, :half], whole[half:, half:]), whole[:half, half:]], axis=1
    )


def unfold(folded):
    half = folded.shape[0]
    above, below = triangles(half)
    both = folded[:, :half]
    upper = jnp.concatenate([jnp.where(above, both, 0.0), folded[:, half:]], axis=1)
    lower = jnp.concatenate([jnp.zeros((half, half), F32), jnp.where(below, both, 0.0)], axis=1)
    return jnp.concatenate([upper, lower], axis=0)


def vectors(*rows):
    hidden = rows[0].shape[1]
    blank = jnp.zeros((8 - len(rows), hidden), F32)
    return jnp.concatenate([row[:1] for row in rows] + [blank], axis=0)


def compose_kernel(
    seqs, blocks, total_seqs, keep, steps_in, x_in, guess_in, recur_in, damping_in, in_in, bias_in,
    targets_in,
    message_ref, maps_ref, before_out, start_ref, lead_ref, lead_off_ref, hit_out, reach_ref,
    reach_off_ref, gain_out, resid_out, drift_ref,
    gain_ref, resid_ref, record_ref, record_off_ref, before_ref, off_ref, hit_ref, hit_off_ref, prev_ref,
    steps_ref, x_ref, guess_ref, recur_ref, damping_ref, in_ref, bias_ref, targets_ref, sems,
):
    fetches = [
        pltpu.make_async_copy(source, to, sems.at[i])
        for i, (source, to) in enumerate([
            (recur_in, recur_ref), (damping_in, damping_ref), (guess_in, guess_ref), (x_in, x_ref),
            (in_in, in_ref), (bias_in, bias_ref), (targets_in, targets_ref), (steps_in, steps_ref),
        ])
    ]
    for fetch in fetches:
        fetch.start()
    for fetch in fetches[:3]:
        fetch.wait()
    rows, hidden = guess_ref.shape
    count = rows // seqs
    chunks = count // LANE
    lanes = seqs * chunks
    block = count // blocks
    per_block = chunks // blocks
    drift = drift_t(recur_ref, damping_ref)
    drift_ref[...] = drift
    drift_w = right(drift)
    for s in range(seqs):
        last = guess_ref[pl.ds((s + 1) * count - 1, 1), :]
        message_ref[s, pl.ds(hidden + hidden // 2 + LAST, 1), :] = last
        message_ref[s, pl.ds(hidden + hidden // 2 + MOVED, 1), :] = mul(eight(last), drift_w)[:1]
    prev_ref[pl.ds(1, rows - 1), :] = guess_ref[pl.ds(0, rows - 1), :]
    for s in range(seqs):
        prev_ref[pl.ds(s * count, 1), :] = jnp.zeros((1, hidden), F32)
    for fetch in fetches[3:]:
        fetch.wait()
    in_w = jnp.concatenate(split(in_ref[...]), axis=1)

    for top in range(0, rows, block):
        part = pl.ds(top, block)
        x_high, x_low = split(x_ref[part, :])
        drive = bias_ref[...] + halves(
            jnp.dot(x_high, in_w, preferred_element_type=F32)
            + jnp.dot(x_low, in_w, preferred_element_type=F32)
        )
        prev = prev_ref[part, :]
        activation = jnp.tanh(mul(prev, drift_w) + drive)
        gain_ref[part, :] = euler_step * (1.0 - activation * activation)
        resid_ref[part, :] = prev + euler_step * activation - guess_ref[part, :]
        if top % count == 0:
            own = (lax.axis_index("seq") == 0).astype(F32)
            edge = pl.ds(top, 1)
            gain_ref[edge, :] = gain_ref[edge, :] * own
            resid_ref[edge, :] = resid_ref[edge, :] * own
            message_ref[top // count, pl.ds(hidden + hidden // 2 + DRIVE, 1), :] = drive[:1]

    sends = [
        pltpu.make_async_copy(gain_ref, gain_out, sems.at[9]),
        pltpu.make_async_copy(resid_ref, resid_out, sems.at[10]),
    ]
    for send in sends:
        send.start()
    unit = identity(hidden)

    def place(j):
        step = (j % blocks) * block + steps_ref[j // blocks, j % blocks]
        return (j // blocks) * chunks + step // LANE, step % LANE, (j // blocks) * count + step

    def opening(lane):
        return unit + drift * gain_ref[pl.ds(lane * LANE, 1), :]

    def capture(now):
        for j in range(seqs * blocks):
            lane, at, _ = place(j)

            @pl.when(at == now)
            def _():
                hit_ref[j] = maps_ref[lane]
                hit_off_ref[pl.ds(j, 1), :] = off_ref[pl.ds(lane, 1), :]

    def advance(now, _, opened_here=False):
        off = off_ref[...]
        off = (
            off
            + gain_ref[pl.ds(now, lanes, stride=LANE), :] * mul(off, drift_w)
            + resid_ref[pl.ds(now, lanes, stride=LANE), :]
        )
        off_ref[...] = off
        if keep:
            record_off_ref[now] = off
        for lane in range(0, lanes, 2):
            if opened_here:
                pair = jnp.concatenate([opening(lane), opening(lane + 1)], axis=0)
            else:
                pair = maps_ref[lane : lane + 2].reshape(2 * hidden, hidden)
            moved = mul(pair, drift_w)
            for k in range(2):
                gain_now = gain_ref[pl.ds((lane + k) * LANE + now, 1), :]
                part = slice(k * hidden, (k + 1) * hidden)
                longer = pair[part] + gain_now * moved[part]
                maps_ref[lane + k] = longer
                if keep:
                    record_ref[now, lane + k] = longer
        if not keep:
            capture(now)
        return 0

    off_ref[...] = resid_ref[pl.ds(0, lanes, stride=LANE), :]
    if keep:
        record_off_ref[0] = off_ref[...]
        advance(1, 0, True)
        lax.fori_loop(2, LANE, advance, 0, unroll=UNROLL)
        for j in range(seqs * blocks):
            lane, at, _ = place(j)
            hit_ref[j] = jnp.where(at == 0, opening(lane), record_ref[jnp.maximum(at, 1), lane])
            hit_off_ref[pl.ds(j, 1), :] = record_off_ref[at, pl.ds(lane, 1), :]
    else:
        for lane in range(lanes):
            maps_ref[lane] = opening(lane)
        capture(0)
        lax.fori_loop(1, LANE, advance, 0)
    hit_copy = pltpu.make_async_copy(hit_ref, hit_out, sems.at[8])
    hit_copy.start()

    hits = seqs * blocks
    running = [None] * hits
    offset = [None] * hits
    for chunk in range(per_block):
        for j in range(hits):
            lane = j * per_block + chunk
            this, this_off = maps_ref[lane], off_ref[pl.ds(lane, 1), :]
            if chunk == 0:
                before_ref[lane] = unit
                start_ref[pl.ds(lane, 1), :] = jnp.zeros((1, hidden), F32)
                running[j], offset[j] = this, eight(this_off)
            else:
                before_ref[lane] = running[j]
                start_ref[pl.ds(lane, 1), :] = offset[j][:1]
                packed = right(this)
                running[j] = mul(running[j], packed)
                offset[j] = mul(offset[j], packed) + this_off
            if (chunk + 1) % RUN == 0:
                run = pl.ds(lane + 1 - RUN, RUN)
                sends.append(
                    pltpu.make_async_copy(before_ref.at[run], before_out.at[run], sems.at[9 + len(sends)])
                )
                sends[-1].start()

    for s in range(seqs):
        lead, lead_off = None, None
        total = jnp.zeros((hidden, hidden), F32)
        total_off = jnp.zeros((8, hidden), F32)
        for k in range(blocks):
            j = s * blocks + k
            lane, _, row = place(j)
            packed = right(hit_ref[j])
            reach = mul(before_ref[lane], packed)
            reach_off = mul(eight(start_ref[pl.ds(lane, 1), :]), packed) + hit_off_ref[pl.ds(j, 1), :]
            if k:
                lead_ref[j] = lead
                lead_off_ref[pl.ds(j, 1), :] = lead_off[:1]
                reach_w, whole_w = right(reach), right(running[j])
                reach, reach_off = mul(lead, reach_w), mul(lead_off, reach_w) + reach_off
                lead, lead_off = mul(lead, whole_w), mul(lead_off, whole_w) + offset[j]
            else:
                lead_ref[j] = unit
                lead_off_ref[pl.ds(j, 1), :] = jnp.zeros((1, hidden), F32)
                lead, lead_off = running[j], offset[j]
            reach_ref[j] = reach
            miss = reach_off + guess_ref[pl.ds(row, 1), :] - targets_ref[pl.ds(j, 1), :]
            reach_off_ref[pl.ds(j, 1), :] = miss[:1]
            reach_t = right_t(reach)
            total = total + mul_t(reach, reach_t)
            total_off = total_off + mul_t(miss, reach_t)
        total = total / total_seqs
        message_ref[s, pl.ds(0, hidden), :] = lead
        message_ref[s, pl.ds(hidden, hidden // 2), :] = fold(total)
        tail = hidden + hidden // 2
        for at, row in (
            (OFFSET, lead_off[:1]),
            (ADJOINT, total_off[:1] / total_seqs),
            (FIRST, guess_ref[pl.ds(s * count, 1), :]),
            (DIAGONAL, jnp.sum(unit * total, axis=0, keepdims=True)),
        ):
            message_ref[s, pl.ds(tail + at, 1), :] = row
        message_ref[s, pl.ds(tail + DIAGONAL + 1, 7 - DIAGONAL), :] = jnp.zeros((7 - DIAGONAL, hidden), F32)
    for send in [*sends, hit_copy]:
        send.wait()


def opened(ref, s, with_map=True):
    hidden = ref.shape[2]
    at = hidden if with_map else 0
    rows = [eight(ref[s, pl.ds(at + hidden // 2 + k, 1), :]) for k in range(6)]
    diagonal = ref[s, pl.ds(at + hidden // 2 + DIAGONAL, 1), :]
    curve = (unfold(ref[s, pl.ds(at, hidden // 2), :]), diagonal)
    return (ref[s, pl.ds(0, hidden), :] if with_map else None, curve, rows)


def entire(curve):
    half, diagonal = curve
    return half + half.T + identity(half.shape[0]) * diagonal


def pick(flag, one, other):
    return jax.tree.map(lambda a, b: jnp.where(flag, a, b), one, other)


def crossing(last, moved, drive, first):
    activation = jnp.tanh(moved + drive)
    return euler_step * (1.0 - activation * activation), last + euler_step * activation - first


def join(one, two, drift_w, with_map=True):
    map_1, curve_1, rows_1 = one
    map_2, curve_2, rows_2 = two
    gain, resid = crossing(rows_1[LAST], rows_1[MOVED], rows_2[DRIVE], rows_2[FIRST])
    map_1 = map_1 + mul(map_1, drift_w) * gain[:1]
    off_1 = rows_1[OFFSET] + mul(rows_1[OFFSET], drift_w) * gain + resid
    half_2, diagonal_2 = curve_2
    half_w, half_wt, map_w, map_1_t = right(half_2), right_t(half_2), right(map_2), right_t(map_1)

    def bent(value):
        return mul(value, half_w) + mul_t(value, half_wt) + value * diagonal_2

    square = mul_t(bent(map_1), map_1_t)
    unit = identity(square.shape[0])
    curve = (
        curve_1[0] + unfold(fold(square)),
        curve_1[1] + jnp.sum(unit * square, axis=0, keepdims=True),
    )
    adjoint = rows_1[ADJOINT] + mul_t(bent(off_1) + rows_2[ADJOINT], map_1_t)
    rows = [mul(off_1, map_w) + rows_2[OFFSET], adjoint, rows_1[DRIVE], rows_1[FIRST], rows_2[LAST], rows_2[MOVED]]
    return (mul(map_1, map_w) if with_map else None), curve, rows


def join_kernel(level, with_map, drift_ref, mine_ref, other_ref, _, out_ref):
    seqs, hidden = mine_ref.shape[0], mine_ref.shape[2]
    upper = (lax.axis_index("seq") >> level) & 1 == 1
    drift_w = right(drift_ref[...])
    for s in range(seqs):
        mine, other = opened(mine_ref, s), opened(other_ref, s)
        whole, curve, rows = join(pick(upper, other, mine), pick(upper, mine, other), drift_w, with_map)
        at = 0
        if with_map:
            out_ref[s, pl.ds(0, hidden), :] = whole
            at = hidden
        out_ref[s, pl.ds(at, hidden // 2), :] = fold(curve[0])
        diagonal = curve[1]
        out_ref[s, pl.ds(at + hidden // 2, 8), :] = vectors(*rows, diagonal)


def sides_kernel(levels, drift_ref, *refs):
    mines, others = refs[:levels], refs[levels : 2 * levels]
    entry_ref, tail_ref, back_ref, rows_ref = refs[2 * levels :]
    seqs, hidden = entry_ref.shape[0], entry_ref.shape[1]
    drift_w = right(drift_ref[...])
    unit = identity(hidden)
    for s in range(seqs):
        zero = jnp.zeros((8, hidden), F32)
        lead, lead_off = unit, zero
        after = (unit, (jnp.zeros((hidden, hidden), F32), zero[:1]), [zero] * 6)
        edge, edge_gain = zero, zero
        place = lax.axis_index("seq")
        fresh = place >= 0
        for level in range(levels):
            upper = (place >> level) & 1 == 1
            mine, other = opened(mines[level], s), opened(others[level], s)
            gain, resid = crossing(other[2][LAST], other[2][MOVED], mine[2][DRIVE], mine[2][FIRST])
            far = other[0] + mul(other[0], drift_w) * gain[:1]
            far_off = other[2][OFFSET] + mul(other[2][OFFSET], drift_w) * gain + resid
            lead_w = right(lead)
            longer = (mul(far, lead_w), mul(far_off, lead_w) + lead_off)
            known = jnp.logical_and(upper, fresh)
            edge, edge_gain = pick(known, (other[2][LAST], gain), (edge, edge_gain))
            fresh = jnp.logical_and(fresh, jnp.logical_not(upper))
            after[2][LAST], after[2][MOVED] = mine[2][LAST], mine[2][MOVED]
            extended = join(after, other, drift_w)
            lead, lead_off = pick(upper, longer, (lead, lead_off))
            after = pick(upper, after, extended)
        own_map, _, own_rows = opened(mines[0], s)
        own_w, curve_w = right(own_map), right(entire(after[1]))
        entry_ref[s] = lead
        tail_ref[s] = mul(mul(lead, own_w), curve_w)
        back_ref[s] = after[0].T
        leaving = mul(lead_off, own_w) + own_rows[OFFSET]
        tail_off = mul(leaving, curve_w) + after[2][ADJOINT]
        rows_ref[pl.ds(8 * s, 8), :] = vectors(lead_off, tail_off, edge, edge_gain)


def prepare_kernel(
    seq, blocks, steps_in, hit_in, maps_ref, _, home_ref, pull_ref, ready_ref, steps_ref, hit_ref, sems
):
    fetch_steps = pltpu.make_async_copy(steps_in, steps_ref, sems.at[0])
    fetch_hit = pltpu.make_async_copy(hit_in.at[pl.ds(seq * blocks, blocks)], hit_ref, sems.at[1])
    fetch_steps.start()
    fetch_hit.start()
    ready_ref[...] = jnp.zeros_like(ready_ref)
    chunks, hidden = home_ref.shape[:2]
    per_block = chunks // blocks
    unit = identity(hidden)
    home = unit
    pulls = [jnp.zeros((hidden, hidden), F32)] * blocks
    fetch_steps.wait()
    fetch_hit.wait()
    for chunk in reversed(range(chunks)):
        home_ref[chunk] = home
        active = [k for k in range(blocks) if chunk < (k + 1) * per_block]
        for k in active:
            pull_ref[k, chunk] = pulls[k]
        if chunk:
            stack = jnp.concatenate([home] + [pulls[k] for k in active], axis=0)
            stack = mul_t(stack, right_t(maps_ref[seq * chunks + chunk]))
            home = stack[:hidden]
            for i, k in enumerate(active):
                owner = (k * per_block * LANE + steps_ref[seq, k]) // LANE
                part = stack[(i + 1) * hidden : (i + 2) * hidden]
                pulls[k] = jnp.where(owner == chunk, hit_ref[k].T, part)


def factors_kernel(
    seqs, blocks, steps_in, x_in, guess_in, _, high_ref, low_ref, mark_ref, ready_ref,
    prev_ref, x_ref, guess_ref, steps_ref, sems,
):
    fetch_steps = pltpu.make_async_copy(steps_in, steps_ref, sems.at[2])
    fetch_steps.start()
    fetch_guess = pltpu.make_async_copy(guess_in, guess_ref, sems.at[0])
    fetch_x = pltpu.make_async_copy(x_in, x_ref, sems.at[1])
    fetch_guess.start()
    fetch_x.start()
    ready_ref[...] = jnp.zeros_like(ready_ref)
    rows, hidden = guess_ref.shape
    fetch_guess.wait()
    prev_ref[pl.ds(1, rows - 1), :] = guess_ref[pl.ds(0, rows - 1), :]
    for s in range(seqs):
        prev_ref[pl.ds(s * (rows // seqs), 1), :] = jnp.zeros((1, hidden), F32)
    high_ref[pl.ds(0, hidden), :], low_ref[pl.ds(0, hidden), :] = split(prev_ref[...].T)
    fetch_x.wait()
    rest = pl.ds(hidden, x_ref.shape[1])
    high_ref[rest, :], low_ref[rest, :] = split(x_ref[...].T)
    fetch_steps.wait()
    block = rows // (seqs * blocks)
    row = lax.broadcasted_iota(jnp.int32, (block, hidden), 0)
    for s in range(seqs):
        for k in range(blocks):
            mark_ref[pl.ds((s * blocks + k) * block, block), :] = (row == steps_ref[s, k]).astype(F32)


def ends_kernel(
    seqs, blocks, total_seqs, level, drift_ref, mine_ref, other_ref, *refs
):
    home_refs, pull_refs, refs = refs[:seqs], refs[seqs : 2 * seqs], refs[2 * seqs :]
    (
        before_ref, start_ref, lead_ref, lead_off_ref, entry_ref, tail_ref, back_ref, sides_ref,
        reach_ref, reach_off_ref, gain_ref, mark_ref,
        state_ref, carry_ref, source_ref, gain_back_ref, edge_ref,
    ) = refs
    rows, hidden = gain_ref.shape
    count = rows // seqs
    chunks = count // LANE
    block = count // blocks
    per_block = chunks // blocks
    place = lax.axis_index("seq")
    upper = (place >> level) & 1 == 1
    lowest = (place & ((1 << level) - 1)) == 0
    drift = drift_ref[...]
    drift_w = right(drift)
    drift_wt = right_t(drift)
    unit = identity(hidden)
    gain_back_ref[...] = gain_ref[...]

    entries, tails, sources = [], [], []
    for s in range(seqs):
        mine, other = opened(mine_ref, s, False), opened(other_ref, s, False)
        last, moved, middle = pick(
            upper,
            (other[2][LAST], other[2][MOVED], other[2][OFFSET]),
            (mine[2][LAST], mine[2][MOVED], mine[2][OFFSET]),
        )
        drive, first = pick(upper, (mine[2][DRIVE], mine[2][FIRST]), (other[2][DRIVE], other[2][FIRST]))
        gain, resid = crossing(last, moved, drive, first)
        middle = middle + mul(middle, drift_w) * gain + resid
        middle_col = column(middle[:1], unit)
        row = along(middle_col, jnp.where(upper, entry_ref[s], entire(other[1])))
        lead_off, tail_off, edge, edge_gain = [sides_ref[pl.ds(8 * s + k, 1), :] for k in range(4)]
        beyond = eight(row) + other[2][ADJOINT]
        beyond = beyond + mul_t(beyond * gain, drift_wt)
        entry = column(jnp.where(upper, row, 0.0) + lead_off, unit)
        entries.append([entry])
        for k in range(1, blocks):
            j = s * blocks + k
            entries[s].append(column(along(entry, lead_ref[j]) + lead_off_ref[pl.ds(j, 1), :], unit))
        tail = jnp.where(
            upper, along(middle_col, tail_ref[s]), along(column(beyond[:1], unit), back_ref[s])
        )
        tails.append(column(tail + tail_off, unit))
        known = jnp.logical_and(upper, lowest)
        edge = jnp.where(known, last[:1], edge)
        edge_ref[pl.ds(s, 1), :] = edge
        edge_gain = jnp.where(known, gain[:1], edge_gain)
        at = pl.ds(s * count, 1)
        gain_back_ref[at, :] = gain_ref[at, :] + edge_gain
        here = []
        for k in range(blocks):
            j = s * blocks + k
            miss = (along(entries[s][0], reach_ref[j]) + reach_off_ref[pl.ds(j, 1), :]) / total_seqs
            here_rows = pl.ds(j * block, block)
            source_ref[here_rows, :] = mark_ref[here_rows, :] * miss
            here.append(column(miss, unit))
        sources.append(here)

    def starts(part, chunk, _):
        for s in range(seqs):
            lane = s * chunks + chunk
            row = along(entries[s][part], before_ref[lane])
            state_ref[pl.ds(lane, 1), :] = row + start_ref[pl.ds(lane, 1), :]
        return 0

    def homes(chunk, _):
        for s in range(seqs):
            lane = s * chunks + chunk
            carry_ref[pl.ds(lane, 1), :] = along(tails[s], home_refs[s][chunk])
        return 0

    def pulls(s, part, chunk, _):
        at = pl.ds(s * chunks + chunk, 1)
        row = sum(sources[s][k] * pull_refs[s][k, chunk] for k in range(part, blocks))
        carry_ref[at, :] = carry_ref[at, :] + jnp.sum(row, axis=0, keepdims=True)
        return 0

    for part in range(blocks):
        starting = functools.partial(starts, part)
        lax.fori_loop(part * per_block, (part + 1) * per_block, starting, 0, unroll=8)
    lax.fori_loop(0, chunks, homes, 0, unroll=8)
    for s in range(seqs):
        for part in range(blocks):
            pulling = functools.partial(pulls, s, part)
            lax.fori_loop(part * per_block, (part + 1) * per_block, pulling, 0, unroll=8)


def walk_kernel(
    drift_ref, state_ref, carry_ref, source_ref, gain_ref, gain_back_ref, resid_ref, guess_ref,
    path_ref, pre_ref,
):
    lanes, hidden = state_ref.shape
    drift = drift_ref[...]

    def walks(ahead_ref, behind_ref):
        pltpu.matmul_push_rhs(right(drift), 0, 0)
        pltpu.matmul_push_rhs(right_t(drift), 0, 1, transpose=True)

        def walk(now, both, staged=None):
            state, carry = both
            at = pl.ds(now, lanes, stride=LANE)
            back = pl.ds(LANE - 1 - now, lanes, stride=LANE)
            adjoint = source_ref[back, :] + carry
            scaled = gain_back_ref[back, :] * adjoint
            pltpu.matmul_acc_lhs(ahead_ref, left(state), staged)
            pltpu.matmul_acc_lhs(behind_ref, left(scaled), staged)
            pre_ref[back, :] = scaled
            rest = state + resid_ref[at, :]
            state = rest + gain_ref[at, :] * halves(pltpu.matmul_pop(ahead_ref))
            path_ref[at, :] = guess_ref[at, :] + state
            return state, adjoint + halves(pltpu.matmul_pop(behind_ref))

        both = walk(0, (state_ref[...], carry_ref[...]), 0)
        for now in range(1, LANE):
            both = walk(now, both)

    wide = (lanes, 2 * hidden)
    pl.run_scoped(walks, pltpu.ACC(0)(wide, F32), pltpu.ACC(1)(wide, F32))


def gradients_kernel(edge_ref, pre_ref, high_ref, low_ref, grads_ref):
    rows, hidden = pre_ref.shape
    seqs = edge_ref.shape[0]
    count = rows // seqs
    unit = identity(hidden)
    pre_high, pre_low = split(pre_ref[...])
    pre_w = jnp.concatenate([pre_high, pre_low], axis=1)
    sums = halves(jnp.dot(high_ref[...], pre_w, preferred_element_type=F32)) + jnp.dot(
        low_ref[...], pre_high, preferred_element_type=F32
    )
    recur = sums[:hidden]
    for s in range(seqs):
        recur = recur + column(edge_ref[pl.ds(s, 1), :], unit) * pre_ref[pl.ds(s * count, 1), :]
    recur = recur.T - recur
    half = hidden // 2
    grads_ref[pl.ds(0, half), :] = fold(recur)
    grads_ref[pl.ds(half, sums.shape[0] - hidden), :] = sums[hidden:]


def finish_kernel(mine_ref, other_ref, recur_ref, in_ref):
    hidden = recur_ref.shape[0]
    half = hidden // 2
    odd = lax.axis_index("batch") & 1 == 1
    mine, other = mine_ref[...], other_ref[...]
    whole = jnp.concatenate([jnp.where(odd, other, mine), jnp.where(odd, mine, other)], axis=0)
    in_ref[...] = whole[half:]
    upper = unfold(whole[:half])
    recur_ref[...] = upper - upper.T


def call(kernel, shapes, in_specs, scratch=(), flops=0, room=14):
    out_shapes = [jax.ShapeDtypeStruct(s, F32) if isinstance(s, tuple) else s for s in shapes]
    run = pl.pallas_call(
        kernel,
        out_shape=out_shapes,
        in_specs=in_specs,
        out_specs=[
            HBM if getattr(s, "memory_space", None) == pltpu.HBM else VMEM for s in out_shapes
        ],
        scratch_shapes=[pltpu.VMEM(s, F32) if isinstance(s, tuple) else s for s in scratch],
        compiler_params=pltpu.CompilerParams(vmem_limit_bytes=room * MIB),
        cost_estimate=pl.CostEstimate(flops=flops, bytes_accessed=1 << 20, transcendentals=0),
    )

    def pinned(*operands):
        placed = [
            pltpu.with_memory_space_constraint(x, pltpu.HBM) if spec is HBM else x
            for x, spec in zip(operands, in_specs, strict=True)
        ]
        return run(*placed)

    return pinned


def swapped(value, axis, distance):
    return lax.ppermute(value, axis, [(i, i ^ distance) for i in range(lax.axis_size(axis))])


def levels_of(axis):
    return lax.axis_size(axis).bit_length() - 1


def on_device(
    inputs, guess_path, recur_weight, damping, in_weight, bias_term, targets, target_steps
):
    seqs, count, hidden = guess_path.shape
    blocks = targets.shape[1]
    features = inputs.shape[2]
    rows = seqs * count
    lanes = rows // LANE
    chunks = lanes // seqs
    hits = seqs * blocks
    total_seqs = seqs * lax.axis_size("batch")
    x = inputs.reshape(rows, features)
    guess = guess_path.reshape(rows, hidden)
    keep = rows * hidden * hidden * 4 <= KEEP
    depth = LANE if keep else 1

    message, maps, before, start, lead, lead_off, hit, reach, reach_off, gain, resid, drift = call(
        functools.partial(compose_kernel, seqs, blocks, total_seqs, keep),
        [
            near((seqs, hidden + hidden // 2 + 8, hidden)),
            near((lanes, hidden, hidden)),
            far((lanes, hidden, hidden)),
            near((lanes, hidden)),
            near((hits, hidden, hidden)),
            near((hits, hidden)),
            far((hits, hidden, hidden)),
            near((hits, hidden, hidden)),
            (hits, hidden),
            far((rows, hidden)),
            far((rows, hidden)),
            (hidden, hidden),
        ],
        [HBM] * 8,
        [
            (rows, hidden),
            (rows, hidden),
            (depth, lanes if keep else 1, hidden, hidden),
            (depth, lanes if keep else 1, hidden),
            (lanes, hidden, hidden),
            (lanes, hidden),
            (hits, hidden, hidden),
            (hits, hidden),
            (rows, hidden),
            pltpu.SMEM((seqs, blocks), jnp.int32),
            (rows, features),
            (rows, hidden),
            (hidden, hidden),
            (1, hidden),
            (features, hidden),
            (1, hidden),
            (hits, hidden),
            pltpu.SemaphoreType.DMA((11 + lanes // RUN,)),
        ],
        room=ROOM,
    )(target_steps, x, guess, recur_weight, damping.reshape(1, hidden), in_weight,
      bias_term.reshape(1, hidden), targets.reshape(hits, hidden))

    def prepare(seq, gate):
        return call(
            functools.partial(prepare_kernel, seq, blocks),
            [
                near((chunks, hidden, hidden)),
                near((blocks, chunks, hidden, hidden)),
                (8, hidden),
            ],
            [HBM, HBM, VMEM, VMEM],
            [
                pltpu.SMEM((seqs, blocks), jnp.int32),
                (blocks, hidden, hidden),
                pltpu.SemaphoreType.DMA((2,)),
            ],
            flops=1 << 32,
        )(target_steps, hit, maps, gate)

    prepared = [prepare(0, drift)]
    ready = prepared[0][2]
    levels = levels_of("seq")
    groups, received = [message], []
    for level in range(levels - 1):
        received.append(swapped(groups[-1], "seq", 1 << level))
        if level == 1:
            prepared += [prepare(s, groups[1]) for s in range(1, seqs)]
            high, low, mark, ready = call(
                functools.partial(factors_kernel, seqs, blocks),
                [
                    jax.ShapeDtypeStruct((hidden + features, rows), BF16),
                    jax.ShapeDtypeStruct((hidden + features, rows), BF16),
                    near((rows, hidden)),
                    (8, hidden),
                ],
                [HBM, HBM, HBM, VMEM],
                [
                    (rows, hidden),
                    (rows, features),
                    (rows, hidden),
                    pltpu.SMEM((seqs, blocks), jnp.int32),
                    pltpu.SemaphoreType.DMA((3,)),
                ],
                flops=1 << 31,
            )(target_steps, x, guess, prepared[-1][2])
        with_map = level < levels - 2
        height = (hidden if with_map else 0) + hidden // 2 + 8
        groups += call(
            functools.partial(join_kernel, level, with_map),
            [(seqs, height, hidden)],
            [VMEM, VMEM, VMEM, VMEM],
        )(drift, groups[-1], received[-1], ready)
    other = swapped(groups[-1], "seq", 1 << (levels - 1))
    square = (seqs, hidden, hidden)
    entry, tail, back, sides = call(
        functools.partial(sides_kernel, levels - 1),
        [square, square, square, (8 * seqs, hidden)],
        [VMEM] * (2 * levels - 1),
        flops=1 << 30,
    )(drift, *groups[:-1], *received)

    state, carry, source, gain_back, edge = call(
        functools.partial(ends_kernel, seqs, blocks, total_seqs, levels - 1),
        [
            near((lanes, hidden)),
            near((lanes, hidden)),
            near((rows, hidden)),
            near((rows, hidden)),
            near((seqs, hidden)),
        ],
        [VMEM] * (15 + 2 * seqs),
    )(drift, groups[-1], other, *[p[0] for p in prepared], *[p[1] for p in prepared], before, start, lead, lead_off, entry, tail, back, sides, reach, reach_off, gain, mark)
    path, pre = call(
        walk_kernel,
        [near((rows, hidden)), near((rows, hidden))],
        [VMEM] * 8,
    )(drift, state, carry, source, gain, gain_back, resid, guess)
    (grads,) = call(
        gradients_kernel, [near((hidden // 2 + features, hidden))], [VMEM] * 4
    )(edge, pre, high, low)

    middle = grads.shape[0] // 2
    odd = lax.axis_index("batch") & 1 == 1
    kept = jnp.where(odd, grads[middle:], grads[:middle])
    given = jnp.where(odd, grads[:middle], grads[middle:])
    kept = kept + swapped(given, "batch", 1)
    width = lax.axis_size("batch")
    hops = [(0, 1 << k) for k in range(1, levels_of("batch"))] + [(1 << k, 0) for k in range(levels)]

    def moved(value, hop_of):
        route = []
        for i in range(lax.axis_size("seq")):
            for j in range(width):
                along_seq, along_batch = hop_of(j & 1)
                route.append((i * width + j, (i ^ along_seq) * width + (j ^ along_batch)))
        return lax.ppermute(value, ("seq", "batch"), route)

    one, two = hops[:2]
    near_by = [one, two, (one[0] ^ two[0], one[1] ^ two[1])]
    parts = [moved(kept, lambda odd: hop) for hop in near_by]
    kept = (kept + parts[0]) + (parts[1] + parts[2])
    rest = hops[2:]
    for stage in range(len(rest)):
        turn = lambda odd: rest[(stage + odd * (len(rest) // 2)) % len(rest)]
        kept = kept + moved(kept, turn)
    grad_recur, grad_in = call(
        finish_kernel,
        [(hidden, hidden), (features, hidden)],
        [VMEM, VMEM],
    )(kept, swapped(kept, "batch", 1))
    return (path.reshape(seqs, count, hidden), grad_recur, grad_in)


def solution(mesh):
    placed = (
        P("batch", "seq", None),
        P("batch", "seq", None),
        P(),
        P(),
        P(),
        P(),
        P("batch", "seq", None),
        P("batch", "seq"),
    )
    return jax.shard_map(
        on_device,
        mesh=mesh,
        in_specs=placed,
        out_specs=(P("batch", "seq", None), P(), P()),
        check_vma=False,
    )
```
